32 devices in a mesh: seq: 8 (over z, x), batch: 4 (over y, core).
Axes of the slice: x: 2, y: 2, z: 4, core: 2. Of those that a mesh axis runs over, the one named last changes fastest.
Arguments:
- tokens: bfloat16 [1024, 4, 768], P('seq', 'batch'), may hold values from -6 to 6
- segments: int32 [1024, 4], P(None, 'batch'), may hold values from 0 to 2, as said below
- buckets: int32 [2047], replicated, may hold values from 0 to 31
- gain_attn: bfloat16 [768], P(('seq', 'batch')), may hold values from 0.5 to 1.5
- w_query: bfloat16 [768, 768], P(('seq', 'batch')), may hold values from -0.0546875 to 0.0546875
- w_key: bfloat16 [768, 768], P(('seq', 'batch')), may hold values from -0.21875 to 0.21875
- w_value: bfloat16 [768, 768], P(('seq', 'batch')), may hold values from -0.21875 to 0.21875
- w_output: bfloat16 [768, 768], P(('seq', 'batch')), may hold values from -0.625 to 0.625
- gain_ffn: bfloat16 [768], P(('seq', 'batch')), may hold values from 0.5 to 1.5
- w_gate: bfloat16 [768, 2048], P(('seq', 'batch')), may hold values from -0.21875 to 0.21875
- w_up: bfloat16 [768, 2048], P(('seq', 'batch')), may hold values from -0.21875 to 0.21875
- w_down: bfloat16 [2048, 768], P(('seq', 'batch')), may hold values from -0.125 to 0.125
- bucket_bias_matrix: bfloat16 [32, 12], replicated, may hold values from -4 to 4
- cotangent: bfloat16 [1024, 4, 768], P('seq', 'batch'), may hold values from -6 to 6
Outputs:
- mixed: bfloat16 [1024, 4, 768], P('seq', 'batch')
- tokens_grad: bfloat16 [1024, 4, 768], P('seq', 'batch')
- gain_attn_grad: float32 [768], P(('seq', 'batch'))
- w_query_grad: float32 [768, 768], P(('seq', 'batch'))
- w_key_grad: float32 [768, 768], P(('seq', 'batch'))
- w_value_grad: float32 [768, 768], P(('seq', 'batch'))
- w_output_grad: float32 [768, 768], P(('seq', 'batch'))
- gain_ffn_grad: float32 [768], P(('seq', 'batch'))
- w_gate_grad: float32 [768, 2048], P(('seq', 'batch'))
- w_up_grad: float32 [768, 2048], P(('seq', 'batch'))
- w_down_grad: float32 [2048, 768], P(('seq', 'batch'))
- bias_table_grad: float32 [32, 12], replicated
The draws below stay inside these ranges and needn't reach their ends.
Inputs may be any that keep to these rules, and one draw needn't show every extreme that they name: `segments`: each column holds exactly three documents, numbered 0, 1 and 2 in order, each a run of positions; in each group of 1 column of one index of batch, one column has a document that holds both position 127 and position 896.
All inputs are finite; a program needn't handle non-finite values.
Results may differ from the reference program's by a relative error of at most 0.023.
Values may be sent and summed in bfloat16 or wider, within the bound.
A program may use at most 256 MiB of HBM per device.

```python
import math
import jax
import jax.numpy as jnp
from jax import lax

D = 768
HEADS = 12
FF = 2048
BUCKETS = 32
TOK_DEV = 128
SEQ_DEV = 1
INNER = 768
L = 1024
SEQS = 4
OFFSETS = 2047


def draw_segments(key, part):
    key = jax.random.fold_in(key, 11)
    first_key, second_key, pick_key, begin_key, finish_key = jax.random.split(key, 5)
    places = jnp.arange(L, dtype=jnp.int32)[:, None]
    half_way = L // 2
    first_cut = jax.random.randint(first_key, (1, SEQS), 1, half_way)
    second_cut = jax.random.randint(second_key, (1, SEQS), half_way, L)
    group_count = SEQS // SEQ_DEV
    chosen = jax.random.randint(pick_key, (group_count,), 0, SEQ_DEV)
    columns = jnp.arange(SEQS, dtype=jnp.int32)
    selected_bias = (columns % SEQ_DEV == jnp.repeat(chosen, SEQ_DEV))[None, :]
    begins = jax.random.randint(begin_key, (1, SEQS), 1, TOK_DEV)
    finishes = L - jax.random.randint(finish_key, (1, SEQS), 1, TOK_DEV)
    lower_cut = jnp.where(selected_bias, begins, first_cut)
    upper_cut = jnp.where(selected_bias, finishes, second_cut)
    return ((places >= lower_cut).astype(jnp.int32) + (places >= upper_cut).astype(jnp.int32)).astype(jnp.int32)


def touch_ends(values, key, low, high):
    longest = values.shape.index(max(values.shape))
    spots = []
    for shift in (0, 1):
        where = [jax.random.randint(jax.random.fold_in(key, axis), (), 0, length) for axis, length in enumerate(values.shape)]
        where[longest] = (where[longest] + shift) % values.shape[longest]
        spots.append(tuple(where))
    return values.at[spots[0]].set(low).at[spots[1]].set(high)


def levels(own_key, shape, cuts, least, largest):
    def one(position, shards_of):
        heights = jax.random.uniform(jax.random.fold_in(jax.random.fold_in(own_key, 6), position), (shards_of,), jnp.float32, least / len(cuts), largest / len(cuts))
        return jnp.repeat(jnp.exp(heights), shape[position] // shards_of).reshape((-1,) + (1,) * (len(shape) - position - 1))

    level = one(*cuts[0])
    for cut in cuts[1:]:
        level = level * one(*cut)
    return level


def scatter_about(own_key, extent, spread, reach, cuts=(), kind=jnp.bfloat16):
    gain = levels(own_key, extent, cuts, -0.22, 0.18) if cuts else 1.0
    drawn = jax.random.normal(own_key, extent, jnp.float32) * spread * gain
    return jnp.minimum(jnp.maximum(drawn, -reach), reach).astype(kind)


def setup_inputs(seed: int = 0) -> dict:
    key_of = jax.random.split(jax.random.key(seed), 15)
    tokens = scatter_about(key_of[0], (L, SEQS, D), 1.0, 6.0, ((0, 8), (1, 4)))
    segments = draw_segments(jax.random.fold_in(key_of[14], 71), 0)
    buckets = touch_ends(jax.random.randint(key_of[2], (OFFSETS,), 0, BUCKETS), jax.random.fold_in(key_of[2], 1), 0, BUCKETS - 1).astype(jnp.int32)
    gain_attn = jnp.clip(1.0 + 0.1 * jax.random.normal(key_of[3], (D,), jnp.float32), 0.5, 1.5).astype(jnp.bfloat16)
    w_query = scatter_about(key_of[4], (D, INNER), (16 * D) ** -0.5, 0.0546875, ((0, 32),))
    w_key = scatter_about(key_of[5], (D, INNER), D ** -0.5, 0.21875, ((0, 32),))
    w_value = scatter_about(key_of[6], (D, INNER), D ** -0.5, 0.21875, ((0, 32),))
    w_output = scatter_about(key_of[7], (INNER, D), (INNER // 8) ** -0.5, 0.625, ((0, 32),))
    gain_ffn = jnp.clip(1.0 + 0.1 * jax.random.normal(key_of[8], (D,), jnp.float32), 0.5, 1.5).astype(jnp.bfloat16)
    w_gate = scatter_about(key_of[9], (D, FF), D ** -0.5, 0.21875, ((0, 32),))
    w_up = scatter_about(key_of[10], (D, FF), D ** -0.5, 0.21875, ((0, 32),))
    w_down = scatter_about(key_of[11], (FF, D), FF ** -0.5, 0.125, ((0, 32),))
    bucket_bias_matrix = scatter_about(key_of[12], (BUCKETS, HEADS), 1.0, 4.0)
    cotangent = scatter_about(key_of[13], (L, SEQS, D), 1.0, 6.0, ((0, 8), (1, 4)))
    return {"tokens": tokens, "segments": segments, "buckets": buckets, "gain_attn": gain_attn, "w_query": w_query, "w_key": w_key, "w_value": w_value, "w_output": w_output, "gain_ffn": gain_ffn, "w_gate": w_gate, "w_up": w_up, "w_down": w_down, "bucket_bias_matrix": bucket_bias_matrix, "cotangent": cotangent}


EPSILON = 1e-06
NEGATIVE = -1e+30
HIGHEST = lax.Precision.HIGHEST

@jax.custom_vjp
def low(v):
    return lax.optimization_barrier(v.astype(jnp.bfloat16)).astype(jnp.float32)

@jax.custom_vjp
def low_back(v):
    return v

def low_keep(v):
    return (low(v), None)

def low_pass(kept, grad):
    return (grad,)

def back_keep(v):
    return (v, None)

def back_low(kept, grad):
    return (low(grad),)
low.defvjp(low_keep, low_pass)
low_back.defvjp(back_keep, back_low)

def normalize(hidden_state, scale_vec):
    return hidden_state * lax.rsqrt(lax.optimization_barrier(jnp.mean(hidden_state * hidden_state, axis=-1, keepdims=True)) + EPSILON) * scale_vec

def layer(hidden_in, seg_col, buckets, params):
    gain_attn, w_query, w_key, w_value, w_output, gain_ffn, w_gate, w_up, w_down, bucket_bias_matrix = params
    seq_length = hidden_in.shape[0]
    head_count = bucket_bias_matrix.shape[1]
    head_width = w_query.shape[1] // head_count
    head_shape = (seq_length, head_count, head_width)
    normed1 = low(normalize(hidden_in, gain_attn))
    query_heads = low_back(low(jnp.dot(normed1, w_query, precision=HIGHEST))).reshape(head_shape)
    key_heads = low_back(low(jnp.dot(normed1, w_key, precision=HIGHEST))).reshape(head_shape)
    value_heads = low_back(low(jnp.dot(normed1, w_value, precision=HIGHEST))).reshape(head_shape)
    block_rows = math.gcd(seq_length, 512)
    positions = jnp.arange(seq_length, dtype=jnp.int32)

    def one_block(block_start):
        query_block = lax.dynamic_slice_in_dim(query_heads, block_start, block_rows, 0)
        seg_block = lax.dynamic_slice_in_dim(seg_col, block_start, block_rows, 0)
        offsets = positions[None, :] - (block_start + jnp.arange(block_rows, dtype=jnp.int32))[:, None] + seq_length - 1
        bias_contributions = jnp.transpose(bucket_bias_matrix[buckets[offsets]], (2, 0, 1))
        scores = jnp.einsum('qhd,khd->hqk', query_block, key_heads, precision=HIGHEST) + bias_contributions
        scores = low_back(scores)
        allowed = (seg_block[:, None] == seg_col[None, :])[None]
        scores = jnp.where(allowed, scores, NEGATIVE)
        weights_now = jax.nn.softmax(scores, axis=-1)
        return jnp.einsum('hqk,khd->qhd', low(weights_now), value_heads, precision=HIGHEST)
    block_starts = jnp.arange(0, seq_length, block_rows, dtype=jnp.int32)
    attended = lax.map(jax.checkpoint(one_block), block_starts).reshape(seq_length, head_count * head_width)
    attended = low_back(low(attended))
    hidden1 = hidden_in + low_back(jnp.dot(attended, w_output, precision=HIGHEST))
    normed2 = low(normalize(hidden1, gain_ffn))
    gate = low_back(jnp.dot(normed2, w_gate, precision=HIGHEST))
    up_val = low_back(jnp.dot(normed2, w_up, precision=HIGHEST))
    activated = low(jax.nn.gelu(gate, approximate=True) * up_val)
    return hidden1 + jnp.dot(activated, w_down, precision=HIGHEST)

def reference(tokens, segments, buckets, gain_attn, w_query, w_key, w_value, w_output, gain_ffn, w_gate, w_up, w_down, bucket_bias_matrix, cotangent):
    params = tuple((weight.astype(jnp.float32) for weight in (gain_attn, w_query, w_key, w_value, w_output, gain_ffn, w_gate, w_up, w_down, bucket_bias_matrix)))

    def per_sequence(totals, scan_item):
        hidden_in, seg_col, grad_in = scan_item
        result, pull = jax.vjp(lambda hidden_now, params_now: layer(hidden_now, seg_col, buckets, params_now), hidden_in.astype(jnp.float32), params)
        grad_hidden, grad_params = pull(grad_in.astype(jnp.float32))
        totals = tuple((total_now + grad_now for total_now, grad_now in zip(totals, grad_params)))
        return (totals, (result.astype(jnp.bfloat16), grad_hidden.astype(jnp.bfloat16)))
    zero_grads = tuple((jnp.zeros(weight.shape, jnp.float32) for weight in params))
    totals, (outputs, input_grads) = lax.scan(per_sequence, zero_grads, (jnp.transpose(tokens, (1, 0, 2)), jnp.transpose(segments), jnp.transpose(cotangent, (1, 0, 2))))
    return (jnp.transpose(outputs, (1, 0, 2)), jnp.transpose(input_grads, (1, 0, 2)), totals[0], totals[1], totals[2], totals[3], totals[4], totals[5], totals[6], totals[7], totals[8], totals[9])
```

```python
from functools import partial
import math
from types import SimpleNamespace

import jax
import jax.numpy as jnp
from jax import lax
from jax.experimental import pallas as pl
from jax.experimental.pallas import tpu as pltpu
from jax.sharding import PartitionSpec as P

EPSILON = 1e-06
NEGATIVE = -1e30
HIGHEST = lax.Precision.HIGHEST


def normalize(hidden_state, scale_vec):
    return (
        hidden_state
        * lax.rsqrt(jnp.mean(hidden_state * hidden_state, axis=-1, keepdims=True) + EPSILON)
        * scale_vec
    )


def gelu_tanh(gate_vals):
    return jax.nn.gelu(gate_vals, approximate=True)


def project(left_side, weight):
    return jnp.einsum("tsk,kn->tsn", left_side, weight, preferred_element_type=jnp.float32)


def project_back(grad_rows, weight):
    return jnp.einsum("tsn,kn->tsk", grad_rows, weight, preferred_element_type=jnp.float32)


def weight_grad(left_side, grad_rows):
    return jnp.einsum("tsk,tsn->kn", left_side, grad_rows, preferred_element_type=jnp.float32)


def position_bias(
    buckets, bucket_bias_matrix, query_start, key_start, query_rows, key_rows, seq_length
):
    span = query_rows + key_rows - 1
    head_count = bucket_bias_matrix.shape[1]
    first = key_start - query_start + seq_length - query_rows
    chosen = lax.dynamic_slice_in_dim(buckets, first, span, 0)
    onehot = (
        chosen[:, None] == jnp.arange(bucket_bias_matrix.shape[0], dtype=jnp.int32)[None, :]
    ).astype(jnp.float32)
    per_offset = jnp.dot(onehot, bucket_bias_matrix.astype(jnp.float32), precision=HIGHEST)
    padded = jnp.concatenate((per_offset.T, jnp.zeros((head_count, 1), jnp.float32)), axis=1)
    tiled = jnp.broadcast_to(padded[:, None, :], (head_count, query_rows, span + 1)).reshape(
        head_count, query_rows * (span + 1)
    )
    skewed = tiled[:, : query_rows * span].reshape(head_count, query_rows, span)
    return (onehot, skewed[:, :, query_rows - 1 : query_rows - 1 + key_rows])


def table_term(onehot, score_gradient):
    summed = jnp.sum(score_gradient.astype(jnp.float32), axis=0)
    head_count, query_rows, key_rows = summed.shape
    span = query_rows + key_rows - 1
    placed = jnp.pad(summed, ((0, 0), (0, 0), (query_rows - 1, 0))).reshape(
        head_count, query_rows * span
    )
    placed = jnp.pad(placed, ((0, 0), (0, query_rows)))
    diagonal_sums = jnp.sum(placed.reshape(head_count, query_rows, span + 1), axis=1)[:, :span]
    return jnp.dot(onehot.T, diagonal_sums.T, precision=HIGHEST)


def pair_scores(table_set, query_block, query_segs, query_start, key_block, key_segs, key_start):
    buckets, bucket_bias_matrix, seq_length = table_set
    onehot, bias_contributions = position_bias(
        buckets,
        bucket_bias_matrix,
        query_start,
        key_start,
        query_block.shape[0],
        key_block.shape[0],
        seq_length,
    )
    scores = (
        jnp.einsum("qshd,kshd->shqk", query_block, key_block, preferred_element_type=jnp.float32)
        + bias_contributions[None]
    )
    allowed = (query_segs.T[:, :, None] == key_segs.T[:, None, :])[:, None]
    return (onehot, scores, allowed)


def pair_grads(
    table_set,
    query_block,
    query_segs,
    query_start,
    dout_block,
    log_sums,
    deltas,
    key_block,
    value_block,
    key_segs,
    key_start,
):
    onehot, scores, allowed = pair_scores(
        table_set, query_block, query_segs, query_start, key_block, key_segs, key_start
    )
    probabilities = jnp.where(allowed, jnp.exp(scores - log_sums[..., None]), 0.0)
    dprobs = jnp.einsum(
        "qshd,kshd->shqk", dout_block, value_block, preferred_element_type=jnp.float32
    )
    score_gradient = (probabilities * (dprobs - deltas[..., None])).astype(jnp.bfloat16)
    return (onehot, probabilities, score_gradient)


def attend_block(setting, carried, blocks, key_start):
    table_set, segments, query_heads, query_segs, query_start = setting
    running_max, running_sum, accum = carried
    key_block, value_block = blocks
    key_segs = lax.dynamic_slice_in_dim(segments, key_start, key_block.shape[0], 0)
    _, scores, allowed = pair_scores(
        table_set, query_heads, query_segs, query_start, key_block, key_segs, key_start
    )
    new_max = jnp.maximum(running_max, jnp.max(jnp.where(allowed, scores, NEGATIVE), axis=-1))
    weights_raw = jnp.where(allowed, jnp.exp(scores - new_max[..., None]), 0.0)
    factor = jnp.exp(running_max - new_max)
    running_sum = running_sum * factor + jnp.sum(weights_raw, axis=-1)
    accum = accum * jnp.transpose(factor, (2, 0, 1))[..., None] + jnp.einsum(
        "shqk,kshd->qshd",
        weights_raw.astype(jnp.bfloat16),
        value_block,
        preferred_element_type=jnp.float32,
    )
    return (new_max, running_sum, accum)


def merged_block(setting, extras, carried, scan_item):
    table_set, segments, query_heads, query_segs, query_start = setting
    dout_heads, log_sums, deltas = extras
    dquery, dtable = carried
    key_start, key_block, value_block = scan_item
    key_rows = key_block.shape[0]
    seq_count = key_block.shape[1]
    key_segs = lax.dynamic_slice_in_dim(segments, key_start, key_rows, 0)
    onehot, probabilities, score_gradient = pair_grads(
        table_set,
        query_heads,
        query_segs,
        query_start,
        dout_heads,
        log_sums,
        deltas,
        key_block,
        value_block,
        key_segs,
        key_start,
    )
    dquery = dquery + jnp.einsum(
        "shqk,kshd->qshd", score_gradient, key_block, preferred_element_type=jnp.float32
    )
    dtable = dtable + table_term(onehot, score_gradient)
    key_gradient = jnp.einsum(
        "shqk,qshd->kshd", score_gradient, query_heads, preferred_element_type=jnp.float32
    )
    dvalue = jnp.einsum(
        "shqk,qshd->kshd",
        probabilities.astype(jnp.bfloat16),
        dout_heads,
        preferred_element_type=jnp.float32,
    )
    joined = jnp.concatenate(
        (key_gradient.reshape(key_rows, seq_count, -1), dvalue.reshape(key_rows, seq_count, -1)),
        axis=2,
    )
    return ((dquery, dtable), joined)


def fold_blocks(step_fn, carried, pieces):
    piece_rows = pieces[0].shape[0]
    block_rows = math.gcd(piece_rows, 512)
    block_count = piece_rows // block_rows
    stacked = tuple(
        (piece.reshape((block_count, block_rows) + piece.shape[1:]) for piece in pieces)
    )

    def advance(state_now, scan_item):
        block_index, blocks = scan_item
        return (step_fn(state_now, blocks, block_index * block_rows), None)

    result, _ = lax.scan(advance, carried, (jnp.arange(block_count, dtype=jnp.int32), stacked))
    return result


def on_device(
    tokens,
    segments,
    buckets,
    gain_attn,
    w_query,
    w_key,
    w_value,
    w_output,
    gain_ffn,
    w_gate,
    w_up,
    w_down,
    bucket_bias_matrix,
    cotangent,
):
    tok_rows, seq_count, _ = tokens.shape
    head_count = bucket_bias_matrix.shape[1]
    inner_width = w_query.shape[1]
    head_width = inner_width // head_count
    head_shape = (tok_rows, seq_count, head_count, head_width)
    seq_length = (buckets.shape[0] + 1) // 2
    query_start = lax.axis_index("seq") * tok_rows
    (
        full_gain_attn,
        full_query,
        full_key,
        full_value,
        full_output,
        full_gain_ffn,
        full_gate,
        full_up,
        full_down,
    ) = (
        lax.all_gather(gain_attn, ("seq", "batch"), axis=0, tiled=True),
        lax.all_gather(w_query, ("seq", "batch"), axis=0, tiled=True),
        lax.all_gather(w_key, ("seq", "batch"), axis=0, tiled=True),
        lax.all_gather(w_value, ("seq", "batch"), axis=0, tiled=True),
        lax.all_gather(w_output, ("seq", "batch"), axis=0, tiled=True),
        lax.all_gather(gain_ffn, ("seq", "batch"), axis=0, tiled=True),
        lax.all_gather(w_gate, ("seq", "batch"), axis=0, tiled=True),
        lax.all_gather(w_up, ("seq", "batch"), axis=0, tiled=True),
        lax.all_gather(w_down, ("seq", "batch"), axis=0, tiled=True),
    )
    tokens_full = tokens.astype(jnp.float32)
    normed1 = normalize(tokens_full, full_gain_attn.astype(jnp.float32)).astype(jnp.bfloat16)
    query_heads = project(normed1, full_query).astype(jnp.bfloat16).reshape(head_shape)
    key_heads = project(normed1, full_key).astype(jnp.bfloat16).reshape(head_shape)
    value_heads = project(normed1, full_value).astype(jnp.bfloat16).reshape(head_shape)
    query_segs = lax.dynamic_slice_in_dim(segments, query_start, tok_rows, 0)
    table_set = (buckets, bucket_bias_matrix, seq_length)
    setting = (table_set, segments, query_heads, query_segs, query_start)
    start_state = (
        jnp.full((seq_count, head_count, tok_rows), NEGATIVE, jnp.float32),
        jnp.zeros((seq_count, head_count, tok_rows), jnp.float32),
        jnp.zeros(head_shape, jnp.float32),
    )
    step_forward = partial(attend_block, setting)
    running_max, running_sum, accum = fold_blocks(
        step_forward,
        start_state,
        (
            lax.all_gather(key_heads, "seq", axis=0, tiled=True),
            lax.all_gather(value_heads, "seq", axis=0, tiled=True),
        ),
    )
    attended_full = accum / jnp.transpose(running_sum, (2, 0, 1))[..., None]
    log_sums = running_max + jnp.log(running_sum)
    attended = attended_full.astype(jnp.bfloat16).reshape(tok_rows, seq_count, inner_width)
    hidden1 = tokens_full + project(attended, full_output)
    normed2 = normalize(hidden1, full_gain_ffn.astype(jnp.float32)).astype(jnp.bfloat16)
    gate = project(normed2, full_gate)
    up_val = project(normed2, full_up)
    gelu_out, gelu_pull = jax.vjp(gelu_tanh, gate)
    activated = (gelu_out * up_val).astype(jnp.bfloat16)
    mixed = (hidden1 + project(activated, full_down)).astype(jnp.bfloat16)
    (
        full_gain_attn,
        full_query,
        full_key,
        full_value,
        full_output,
        full_gain_ffn,
        full_gate,
        full_up,
        full_down,
    ) = (
        lax.all_gather(gain_attn, ("seq", "batch"), axis=0, tiled=True),
        lax.all_gather(w_query, ("seq", "batch"), axis=0, tiled=True),
        lax.all_gather(w_key, ("seq", "batch"), axis=0, tiled=True),
        lax.all_gather(w_value, ("seq", "batch"), axis=0, tiled=True),
        lax.all_gather(w_output, ("seq", "batch"), axis=0, tiled=True),
        lax.all_gather(gain_ffn, ("seq", "batch"), axis=0, tiled=True),
        lax.all_gather(w_gate, ("seq", "batch"), axis=0, tiled=True),
        lax.all_gather(w_up, ("seq", "batch"), axis=0, tiled=True),
        lax.all_gather(w_down, ("seq", "batch"), axis=0, tiled=True),
    )
    grad_down = weight_grad(activated, cotangent)
    d_activated = project_back(cotangent, full_down)
    d_gate = gelu_pull(d_activated * up_val)[0].astype(jnp.bfloat16)
    d_up = (gelu_out * d_activated).astype(jnp.bfloat16)
    grad_gate = weight_grad(normed2, d_gate)
    grad_up = weight_grad(normed2, d_up)
    d_normed2 = project_back(d_gate, full_gate) + project_back(d_up, full_up)
    _, norm_pull2 = jax.vjp(normalize, hidden1, full_gain_ffn.astype(jnp.float32))
    d_hidden_part, grad_gain_ffn = norm_pull2(d_normed2)
    d_hidden1 = cotangent.astype(jnp.float32) + d_hidden_part
    d_branch = d_hidden1.astype(jnp.bfloat16)
    grad_output = weight_grad(attended, d_branch)
    dout_heads = project_back(d_branch, full_output).astype(jnp.bfloat16).reshape(head_shape)
    deltas = jnp.transpose(
        jnp.sum(dout_heads.astype(jnp.float32) * attended_full, axis=-1), (1, 2, 0)
    )
    extras = (dout_heads, log_sums, deltas)
    keys_all, values_all = (
        lax.all_gather(key_heads, "seq", axis=0, tiled=True),
        lax.all_gather(value_heads, "seq", axis=0, tiled=True),
    )
    block_rows = math.gcd(seq_length, 512)
    block_count = seq_length // block_rows
    stacked_keys = keys_all.reshape((block_count, block_rows) + keys_all.shape[1:])
    stacked_values = values_all.reshape((block_count, block_rows) + values_all.shape[1:])
    block_starts = jnp.arange(block_count, dtype=jnp.int32) * block_rows
    query_init = (
        jnp.zeros(head_shape, jnp.float32),
        jnp.zeros(bucket_bias_matrix.shape, jnp.float32),
    )
    (dquery, dtable), joined_all = lax.scan(
        partial(merged_block, setting, extras),
        query_init,
        (block_starts, stacked_keys, stacked_values),
    )
    every_key_contribution = joined_all.reshape(seq_length, seq_count, 2 * inner_width)
    key_sums = lax.psum_scatter(every_key_contribution, "seq", scatter_dimension=0, tiled=True)
    dkey_rows = key_sums[:, :, :inner_width].astype(jnp.bfloat16)
    dvalue_rows = key_sums[:, :, inner_width:].astype(jnp.bfloat16)
    dquery_rows = dquery.reshape(tok_rows, seq_count, inner_width).astype(jnp.bfloat16)
    grad_query = weight_grad(normed1, dquery_rows)
    grad_key = weight_grad(normed1, dkey_rows)
    grad_value = weight_grad(normed1, dvalue_rows)
    d_normed1 = (
        project_back(dquery_rows, full_query)
        + project_back(dkey_rows, full_key)
        + project_back(dvalue_rows, full_value)
    )
    _, norm_pull1 = jax.vjp(normalize, tokens_full, full_gain_attn.astype(jnp.float32))
    d_input_part, grad_gain_attn = norm_pull1(d_normed1)
    tokens_grad = (d_hidden1 + d_input_part).astype(jnp.bfloat16)
    owned = (
        lax.psum_scatter(grad_gain_attn, ("seq", "batch"), scatter_dimension=0, tiled=True),
        lax.psum_scatter(grad_query, ("seq", "batch"), scatter_dimension=0, tiled=True),
        lax.psum_scatter(grad_key, ("seq", "batch"), scatter_dimension=0, tiled=True),
        lax.psum_scatter(grad_value, ("seq", "batch"), scatter_dimension=0, tiled=True),
        lax.psum_scatter(grad_output, ("seq", "batch"), scatter_dimension=0, tiled=True),
        lax.psum_scatter(grad_gain_ffn, ("seq", "batch"), scatter_dimension=0, tiled=True),
        lax.psum_scatter(grad_gate, ("seq", "batch"), scatter_dimension=0, tiled=True),
        lax.psum_scatter(grad_up, ("seq", "batch"), scatter_dimension=0, tiled=True),
        lax.psum_scatter(grad_down, ("seq", "batch"), scatter_dimension=0, tiled=True),
    )
    table_total = lax.psum(dtable, ("seq", "batch"))
    return (
        mixed,
        tokens_grad,
        owned[0],
        owned[1],
        owned[2],
        owned[3],
        owned[4],
        owned[5],
        owned[6],
        owned[7],
        owned[8],
        table_total,
    )


BF16 = jnp.bfloat16
F32 = jnp.float32
MESH_IDS = pl.DeviceIdType.MESH

ZS, XS, YS, CS = 4, 2, 2, 2
SEQ_DEVICES = ZS * XS
BATCH_DEVICES = YS * CS
TOK = 128
LENGTH = SEQ_DEVICES * TOK
DIM = 768
HALF = DIM // CS
PAIRS = HALF // 128
SHARD = DIM // (SEQ_DEVICES * BATCH_DEVICES)
CHIP_ROWS = SHARD * CS
GROUP_ROWS = SHARD * BATCH_DEVICES
FF_ALL = 2048
QUARTER = FF_ALL // BATCH_DEVICES
DOWN_ROWS = FF_ALL // (SEQ_DEVICES * BATCH_DEVICES)
CHUNKS = PAIRS + 1
SPAN = LENGTH + TOK
HEADS_HERE = 2 * PAIRS


def dot(a, b):
    return lax.dot_general(a, b, (((1,), (0,)), ((), ())), preferred_element_type=F32)


def dot_tb(a, b):
    return lax.dot_general(a, b, (((1,), (1,)), ((), ())), preferred_element_type=F32)


def dot_ta(a, b):
    return lax.dot_general(a, b, (((0,), (0,)), ((), ())), preferred_element_type=F32)


def to_column(row):
    n = row.shape[1]
    eye = lax.broadcasted_iota(jnp.int32, (n, n), 0) == lax.broadcasted_iota(jnp.int32, (n, n), 1)
    return jnp.sum(jnp.where(eye, jnp.broadcast_to(row, (n, n)), 0.0), axis=1, keepdims=True)


def to_row(col):
    n = col.shape[0]
    eye = lax.broadcasted_iota(jnp.int32, (n, n), 0) == lax.broadcasted_iota(jnp.int32, (n, n), 1)
    return jnp.sum(jnp.where(eye, jnp.broadcast_to(col, (n, n)), 0.0), axis=0, keepdims=True)


def unit_rows(x):
    r = lax.rsqrt(jnp.mean(x * x, axis=1, keepdims=True) + EPSILON)
    return x * r, r


def stack_heads(pair):
    low = lax.broadcasted_iota(jnp.int32, pair.shape, 1) < 64
    return jnp.concatenate((jnp.where(low, pair, 0.0), jnp.where(low, 0.0, pair)), axis=0).astype(BF16)


def unstack_heads(stacked):
    rows = stacked.shape[0] // 2
    low = lax.broadcasted_iota(jnp.int32, (rows, 128), 1) < 64
    return jnp.where(low, stacked[:rows], stacked[rows:])


def split_quarters(whole):
    low = lax.broadcasted_iota(jnp.int32, (whole.shape[0], 128), 1) < 64
    parts = []
    for q in range(BATCH_DEVICES):
        cols = []
        for m in range(QUARTER // 128):
            first = 4 * m + q // 2
            a = whole[:, 128 * first : 128 * first + 128]
            b = whole[:, 128 * (first + 2) : 128 * (first + 2) + 128]
            if q % 2 == 0:
                cols.append(jnp.where(low, a, pltpu.roll(b, 64, 1)))
            else:
                cols.append(jnp.where(low, pltpu.roll(a, 64, 1), b))
        parts.append(jnp.concatenate(cols, axis=1))
    return parts


def join_quarters(parts):
    low = lax.broadcasted_iota(jnp.int32, (parts[0].shape[0], 128), 1) < 64
    cols = []
    for block in range(FF_ALL // 128):
        q0 = (2 * block) % 4
        m = block // 2
        lanes = slice(128 * (m // 2), 128 * (m // 2) + 128)
        a, b = parts[q0][:, lanes], parts[q0 + 1][:, lanes]
        if m % 2 == 0:
            cols.append(jnp.where(low, a, pltpu.roll(b, 64, 1)))
        else:
            cols.append(jnp.where(low, pltpu.roll(a, 64, 1), b))
    return jnp.concatenate(cols, axis=1)


SCRATCH = dict(
    W_MINE=((CS, SHARD, 4 * HALF), F32),
    W_CORE=((CS, SHARD, 4 * HALF), F32),
    U_MINE=((BATCH_DEVICES, SHARD, 2 * QUARTER), F32),
    U_ALL=((BATCH_DEVICES, SHARD, 2 * QUARTER), F32),
    WA=((PAIRS, ZS, XS, YS, CHIP_ROWS, HALF), BF16),
    WO=((CS, ZS, XS, YS, CHIP_ROWS, HALF), BF16),
    WG=((ZS, XS, GROUP_ROWS, 2 * QUARTER), BF16),
    WD=((ZS, XS, DOWN_ROWS, DIM), BF16),
    X=((CS, ZS, XS, TOK, DIM), BF16),
    N1=((CS, ZS, XS, TOK, DIM), BF16),
    N1O=((CS, TOK, DIM), BF16),
    COT=((YS, CS, TOK, DIM), BF16),
    SEG=((CS, 8, LENGTH), F32),
    BK=((1, 2 * LENGTH), jnp.int32),
    PH=((2 * CS * PAIRS, SPAN), F32),
    BIAS=((PAIRS, 2 * TOK, LENGTH), F32),
    MASK=((CS, TOK, LENGTH), F32),
    KV=((PAIRS, CS, LENGTH, 256), BF16),
    QS=((PAIRS, CS, 2 * TOK, 128), BF16),
    PS=((PAIRS, CS, 2 * TOK, LENGTH), BF16),
    ATT=((CS, CS, TOK, HALF), BF16),
    H=((TOK, DIM), F32),
    N2=((YS, CS, TOK, DIM), BF16),
    ACT=((YS, 2 * TOK, QUARTER), BF16),
    DGU=((YS, 2 * TOK, 2 * QUARTER), BF16),
    MX=((YS, CS, TOK, DIM), BF16),
    MXC=((YS, TOK, DIM), BF16),
    MXS=((TOK, DIM), BF16),
    MXY=((TOK, DIM), BF16),
    E2=((YS, CS, TOK, DIM), BF16),
    E2C=((YS, TOK, DIM), BF16),
    E2S=((TOK, DIM), BF16),
    E2Y=((TOK, DIM), BF16),
    GG=((ZS, XS, GROUP_ROWS, 2 * QUARTER), BF16),
    GGX=((ZS, GROUP_ROWS, 2 * QUARTER), BF16),
    GGZ=((ZS, GROUP_ROWS, 2 * QUARTER), BF16),
    GD=((ZS, XS, DOWN_ROWS, DIM), BF16),
    GDX=((ZS, DOWN_ROWS, DIM), BF16),
    GDZ=((ZS, DOWN_ROWS, DIM), BF16),
    F4S=((BATCH_DEVICES, SHARD, 2 * QUARTER), F32),
    F4=((BATCH_DEVICES, SHARD, 2 * QUARTER), F32),
    DH=((TOK, DIM), F32),
    DB=((CS, TOK, DIM), BF16),
    DO=((CS, TOK, HALF), BF16),
    DS=((CS, 2 * TOK, LENGTH), BF16),
    DQ=((PAIRS, CS, TOK, 128), BF16),
    DKV=((PAIRS, CS, 256, LENGTH), BF16),
    DG=((8, SPAN), F32),
    GA=((CHUNKS, ZS, XS, YS, CHIP_ROWS, HALF), BF16),
    GAY=((CHUNKS, ZS, XS, CHIP_ROWS, HALF), BF16),
    GAX=((CHUNKS, ZS, CHIP_ROWS, HALF), BF16),
    GAZ=((CHUNKS, ZS, CHIP_ROWS, HALF), BF16),
    FA=((CS, SHARD, 4 * HALF), F32),
    F2=((CS, SHARD, 4 * HALF), F32),
    DN=((CS, ZS, XS, DIM, TOK), BF16),
    DNC=((ZS, XS, DIM, TOK), BF16),
    DNX=((ZS, DIM, TOK), BF16),
    DNZ=((ZS, DIM, TOK), BF16),
    T1=((8, 128), F32),
    TY=((8, 128), F32),
    T2=((8, 128), F32),
    TX=((8, 128), F32),
    T3=((8, 128), F32),
    TZ=((ZS, 8, 128), F32),
    TO=((CS, 8, 128), F32),
)
SEND_COUNT = 224
SLOTS = dict(
    segc=1, wc=1, u=4, xz=4, xx=4, xc=8, wz=4 * CHUNKS, wx=CHUNKS, wy=2 * CHUNKS, woc=1,
    gz=4, gx=4, dz=4, dx=1, coty=1, cotc=2, att=1, n2y=1, n2c=2, mxc=2, mxy=1, e2c=2, e2y=1,
    rdx=4, rdz=4, rgx=4, rgz=4, f4=4, db=1, ray=CHUNKS, rax=CHUNKS, raz=4 * CHUNKS, f2=1,
    dnc=4, dnx=4, dnz=4, ty=1, tx=1, tz=4, tc=1,
)
RECV_COUNT = sum(SLOTS.values())


def slot_bases():
    bases, used = {}, 0
    for name, count in SLOTS.items():
        bases[name] = used
        used += count
    return SimpleNamespace(**bases)


INPUTS = dict(
    tok=0, cot=0, seg=0, buckets=0, table=0, ga=0, gf=0, wq=0, wk=0, wv=0, wo=0, wg=0, wu=0, wd=0
)
OUTPUTS = dict(
    mixed=((TOK, DIM), BF16), tg=((TOK, DIM), BF16), gga=((1, SHARD), F32),
    gwq=((SHARD, DIM), F32), gwk=((SHARD, DIM), F32), gwv=((SHARD, DIM), F32), gwo=((SHARD, DIM), F32),
    ggf=((1, SHARD), F32), gwg=((SHARD, FF_ALL), F32), gwu=((SHARD, FF_ALL), F32),
    gwd=((DOWN_ROWS, DIM), F32), gtab=((2 * CS * PAIRS, 32), F32),
)


def layer_kernel(*refs):
    names = (*INPUTS, *OUTPUTS, *SCRATCH)
    r = SimpleNamespace(**dict(zip(names, refs[:-2], strict=True)))
    ssem, rsem = refs[-2:]
    k = slot_bases()
    s, b = lax.axis_index("seq"), lax.axis_index("batch")
    z, x = s // XS, s % XS
    y, c = b // CS, b % CS
    xo, yo, co = 1 - x, 1 - y, 1 - c
    zo = [(z + j) % ZS for j in range(1, ZS)]

    def at(zz, xx, yy, cc):
        return (XS * zz + xx, CS * yy + cc)

    to_core, to_y, to_diag, to_x = at(z, x, y, co), at(z, x, yo, c), at(z, x, yo, co), at(z, xo, y, c)
    to_z = [at(zz, x, y, c) for zz in zo]

    barrier = pltpu.get_barrier_semaphore()
    friends = [to_core, to_y, to_diag, to_x] + to_z
    for who in friends:
        pl.semaphore_signal(barrier, inc=1, device_id=who, device_id_type=MESH_IDS)

    sent = []

    def put(src, dst, who, slot):
        copy = pltpu.make_async_remote_copy(
            src_ref=src, dst_ref=dst, send_sem=ssem.at[len(sent)], recv_sem=rsem.at[slot],
            device_id=who, device_id_type=MESH_IDS,
        )
        copy.start()
        sent.append(copy)

    def take(dst, slot):
        pltpu.make_async_remote_copy(
            src_ref=dst, dst_ref=dst, send_sem=ssem.at[0], recv_sem=rsem.at[slot],
            device_id=to_core, device_id_type=MESH_IDS,
        ).wait_recv()

    gain_a = to_column(r.ga[...].astype(F32))
    gain_f = to_column(r.gf[...].astype(F32))
    tok = r.tok
    r.SEG[c] = jnp.broadcast_to(r.seg[...].astype(F32), (8, LENGTH))
    r.BK[...] = jnp.zeros(r.BK.shape, jnp.int32)
    r.BK[:, : 2 * LENGTH - 1] = r.buckets[...]
    for h in range(CS):
        for p in range(PAIRS):
            for j, w_ref in enumerate((r.wq, r.wk, r.wv)):
                lanes = slice(HALF * h + 128 * p, HALF * h + 128 * p + 128)
                r.W_MINE[h, :, HALF * p + 128 * j : HALF * p + 128 * j + 128] = (
                    w_ref[:, lanes].astype(F32) * gain_a
                )
        r.W_MINE[h, :, 3 * HALF :] = r.wo[:, HALF * h : HALF * h + HALF].astype(F32)

    pl.semaphore_wait(barrier, len(friends))

    put(r.W_MINE.at[co], r.W_CORE.at[c], to_core, k.wc)
    for j, who in enumerate(to_z):
        put(tok, r.X.at[c, z, x], who, k.xz + z)
    put(tok, r.X.at[c, z, x], to_x, k.xx + z)
    put(r.SEG.at[c], r.SEG.at[c], to_core, k.segc)
    put(tok, r.X.at[c, z, x], to_core, k.xc + s)
    r.X[c, z, x] = tok[...]

    parts = split_quarters(r.wg[...].astype(F32) * gain_f)
    for q in range(BATCH_DEVICES):
        r.U_MINE[q, :, :QUARTER] = parts[q]
    parts = split_quarters(r.wu[...].astype(F32) * gain_f)
    for q in range(BATCH_DEVICES):
        r.U_MINE[q, :, QUARTER:] = parts[q]

    take(r.W_CORE.at[co], k.wc)
    r.W_CORE[c] = r.W_MINE[c]
    block = r.W_CORE[...].reshape(CHIP_ROWS, 4 * HALF).astype(BF16)
    for ch in range(PAIRS):
        r.WA[ch, z, x, y] = block[:, HALF * ch : HALF * ch + HALF]
    r.WO[c, z, x, y] = block[:, 3 * HALF :]

    def weight(ch):
        return r.WA.at[ch] if ch < PAIRS else r.WO.at[c]

    for ch in range(CHUNKS):
        for who in to_z:
            put(weight(ch).at[z, x, y], weight(ch).at[z, x, y], who, k.wz + 4 * ch + z)
    for q_y, q_c, who in ((y, co, to_core), (yo, c, to_y), (yo, co, to_diag)):
        put(r.U_MINE.at[CS * q_y + q_c], r.U_ALL.at[b], who, k.u + b)
    r.U_ALL[b] = r.U_MINE[b]

    onehot = (
        lax.broadcasted_iota(jnp.int32, (32, SPAN), 0)
        == r.BK[:, pl.ds(pl.multiple_of(LENGTH - TOK - TOK * s, 128), SPAN)]
    )
    r.PH[...] = dot(r.table[...], onehot.astype(BF16))
    for p in range(PAIRS):
        for hh in range(2):
            line = r.PH[pl.ds(HEADS_HERE * c + 2 * p + hh, 1), :]
            skewed = pltpu.roll(
                jnp.broadcast_to(line, (TOK, SPAN)), SPAN - TOK + 1, 1, stride=1, stride_axis=0
            )
            r.BIAS[p, TOK * hh : TOK * hh + TOK, :] = skewed[:, :LENGTH]
    take(r.SEG.at[co], k.segc)
    for q in range(CS):
        col = to_column(r.SEG[q, 0:1, pl.ds(pl.multiple_of(TOK * s, 128), TOK)])
        r.MASK[q] = jnp.where(col == r.SEG[q, 0:1, :], 0.0, NEGATIVE)

    for q_y, q_c in ((y, co), (yo, c), (yo, co)):
        src = CS * q_y + q_c
        take(r.U_ALL.at[src], k.u + src)
    r.WG[z, x] = r.U_ALL[...].reshape(GROUP_ROWS, 2 * QUARTER).astype(BF16)
    r.WD[z, x] = r.wd[...]
    for who in to_z:
        put(r.WG.at[z, x], r.WG.at[z, x], who, k.gz + z)
    for who in to_z:
        put(r.WD.at[z, x], r.WD.at[z, x], who, k.dz + z)

    def norm_block(q, zz, xx, own=False):
        value = unit_rows(r.X[q, zz, xx].astype(F32))[0].astype(BF16)
        r.N1[q, zz, xx] = value
        if own:
            r.N1O[q] = value

    norm_block(c, z, x, own=True)
    for zz in zo:
        take(r.X.at[c, zz, x], k.xz + zz)
        put(r.X.at[c, zz, x], r.X.at[c, zz, x], to_x, k.xx + zz)
        put(r.X.at[c, zz, x], r.X.at[c, zz, x], to_core, k.xc + XS * zz + x)
        norm_block(c, zz, x)

    def weight_from_z(ch):
        for zz in zo:
            take(weight(ch).at[zz, x, y], k.wz + 4 * ch + zz)
        put(weight(ch).at[:, x, y], weight(ch).at[:, x, y], to_x, k.wx + ch)
        put(weight(ch).at[:, x, y], weight(ch).at[:, x, y], to_y, k.wy + 2 * ch)

    def weight_from_x(ch):
        take(weight(ch).at[:, xo, y], k.wx + ch)
        put(weight(ch).at[:, xo, y], weight(ch).at[:, xo, y], to_y, k.wy + 2 * ch + 1)

    def weight_from_y(ch):
        take(weight(ch).at[:, x, yo], k.wy + 2 * ch)
        take(weight(ch).at[:, xo, yo], k.wy + 2 * ch + 1)

    weight_from_z(0)
    for zz in [z] + zo:
        take(r.X.at[c, zz, xo], k.xx + zz)
        put(r.X.at[c, zz, xo], r.X.at[c, zz, xo], to_core, k.xc + XS * zz + xo)
        norm_block(c, zz, xo)
    weight_from_x(0)
    weight_from_z(1)
    weight_from_x(1)
    weight_from_z(2)
    for zz in [z] + zo:
        for xx in (x, xo):
            take(r.X.at[co, zz, xx], k.xc + XS * zz + xx)
            norm_block(co, zz, xx, own=zz is z and xx is x)
    weight_from_x(2)
    put(r.cot, r.COT.at[y, c], to_core, k.cotc + 0)
    put(r.cot, r.COT.at[y, c], to_y, k.coty)
    r.COT[y, c] = r.cot[...]

    def attention_pair(p):
        w_pair = r.WA.at[p]

        def one_sequence(q, carry):
            w = w_pair[...].reshape(DIM, HALF)
            n1 = r.N1[q].reshape(LENGTH, DIM)
            kv = dot(n1, w[:, 128:]).astype(BF16)
            r.KV[p, q] = kv
            stacked = stack_heads(dot(r.N1O[q], w[:, :128]))
            r.QS[p, q] = stacked
            mask = r.MASK[q]
            scores = dot_tb(stacked, kv[:, :128]) + r.BIAS[p] + jnp.concatenate((mask, mask), axis=0)
            weights = jnp.exp(scores - jnp.max(scores, axis=1, keepdims=True))
            probs = (weights * (1.0 / jnp.sum(weights, axis=1, keepdims=True))).astype(BF16)
            r.PS[p, q] = probs
            r.ATT[c, q, :, 128 * p : 128 * p + 128] = unstack_heads(dot(probs, kv[:, 128:])).astype(BF16)
            return carry

        lax.fori_loop(0, CS, one_sequence, 0)

    def gate_from_z():
        for zz in zo:
            take(r.WG.at[zz, x], k.gz + zz)
            put(r.WG.at[zz, x], r.WG.at[zz, x], to_x, k.gx + zz)

    weight_from_y(0)
    attention_pair(0)
    weight_from_z(PAIRS)
    put(r.WG.at[z, x], r.WG.at[z, x], to_x, k.gx + z)
    weight_from_y(1)
    attention_pair(1)
    weight_from_x(PAIRS)
    gate_from_z()
    take(r.COT.at[yo, c], k.coty)
    put(r.COT.at[yo, c], r.COT.at[yo, c], to_core, k.cotc + 1)
    weight_from_y(2)
    attention_pair(2)
    for zz in zo:
        take(r.WD.at[zz, x], k.dz + zz)
    put(r.WD.at[:, x], r.WD.at[:, x], to_x, k.dx)
    weight_from_y(PAIRS)
    put(r.WO.at[c], r.WO.at[c], to_core, k.woc)
    put(r.ATT.at[c], r.ATT.at[c], to_core, k.att)
    take(r.WO.at[co], k.woc)
    take(r.ATT.at[co], k.att)

    att_own = jnp.concatenate((r.ATT[0, c], r.ATT[1, c]), axis=1)
    tokens_f = tok[...].astype(F32)
    r.H[...] = tokens_f + jnp.concatenate(
        (dot(att_own, r.WO[0].reshape(DIM, HALF)), dot(att_own, r.WO[1].reshape(DIM, HALF))), axis=1
    )
    r.N2[y, c] = unit_rows(r.H[...])[0].astype(BF16)
    put(r.N2.at[y, c], r.N2.at[y, c], to_core, k.n2c + 0)
    put(r.N2.at[y, c], r.N2.at[y, c], to_y, k.n2y)

    for zz in [z] + zo:
        take(r.WG.at[zz, xo], k.gx + zz)
    take(r.WD.at[:, xo], k.dx)
    take(r.COT.at[y, co], k.cotc + 0)
    take(r.COT.at[yo, co], k.cotc + 1)
    take(r.N2.at[y, co], k.n2c + 0)

    def feed_forward(yy):
        w_gu = r.WG[...].reshape(DIM, 2 * QUARTER)
        w_d = r.WD[...].reshape(QUARTER, DIM)
        n2 = r.N2[yy].reshape(2 * TOK, DIM)
        g = r.COT[yy].reshape(2 * TOK, DIM)
        gate = dot(n2, w_gu[:, :QUARTER])
        up = dot(n2, w_gu[:, QUARTER:])
        d_act = dot_tb(g, w_d)
        square = gate * gate
        inner = math.sqrt(2 / math.pi) * gate * (1.0 + 0.044715 * square)
        tanh = jnp.tanh(inner)
        half_open = 0.5 * (1.0 + tanh)
        gelu = gate * half_open
        slope = half_open + 0.5 * gate * (1.0 - tanh * tanh) * (
            math.sqrt(2 / math.pi) * (1.0 + 3 * 0.044715 * square)
        )
        act = (gelu * up).astype(BF16)
        r.ACT[yy] = act
        d_gu = jnp.concatenate(
            ((slope * (up * d_act)).astype(BF16), (gelu * d_act).astype(BF16)), axis=1
        )
        r.DGU[yy] = d_gu
        r.E2[yy] = dot_tb(d_gu, w_gu).astype(BF16).reshape(CS, TOK, DIM)
        put(r.E2.at[yy, co], r.E2C.at[yy], to_core, k.e2c + yy)
        r.MX[yy] = dot(act, w_d).astype(BF16).reshape(CS, TOK, DIM)
        put(r.MX.at[yy, co], r.MXC.at[yy], to_core, k.mxc + yy)

    feed_forward(y)
    take(r.N2.at[yo, c], k.n2y)
    put(r.N2.at[yo, c], r.N2.at[yo, c], to_core, k.n2c + 1)
    take(r.N2.at[yo, co], k.n2c + 1)
    feed_forward(yo)
    take(r.E2C.at[yo], k.e2c + yo)
    r.E2S[...] = (r.E2[yo, c].astype(F32) + r.E2C[yo].astype(F32)).astype(BF16)
    put(r.E2S, r.E2Y, to_y, k.e2y)
    take(r.MXC.at[yo], k.mxc + yo)
    r.MXS[...] = (r.MX[yo, c].astype(F32) + r.MXC[yo].astype(F32)).astype(BF16)
    put(r.MXS, r.MXY, to_y, k.mxy)

    cot_all = r.COT[...].reshape(4 * TOK, DIM)
    r.GD[...] = dot_ta(r.ACT[...].reshape(4 * TOK, QUARTER), cot_all).astype(BF16).reshape(
        ZS, XS, DOWN_ROWS, DIM
    )
    for zz in zo + [z]:
        put(r.GD.at[zz, xo], r.GDX.at[zz], to_x, k.rdx + zz)
    n2_all = r.N2[...].reshape(4 * TOK, DIM)
    d_gu_all = r.DGU[...].reshape(4 * TOK, 2 * QUARTER)
    r.GG[...] = dot_ta(n2_all, d_gu_all).astype(BF16).reshape(ZS, XS, GROUP_ROWS, 2 * QUARTER)
    for zz in zo + [z]:
        put(r.GG.at[zz, xo], r.GGX.at[zz], to_x, k.rgx + zz)

    def grad_from_x(full, part, got, slot, back):
        for j, zz in enumerate(zo + [z]):
            take(part.at[zz], slot + zz)
            total = full[zz, x].astype(F32) + part[zz].astype(F32)
            full[zz, x] = total.astype(BF16)
            if j < ZS - 1:
                put(full.at[zz, x], got.at[z], to_z[j], back + z)

    def sum_z(own, got, slot):
        total = own.astype(F32)
        for zz in zo:
            take(got.at[zz], slot + zz)
            total = total + got[zz].astype(F32)
        return total

    take(r.E2C.at[y], k.e2c + y)
    take(r.E2Y, k.e2y)
    e2 = r.E2[y, c].astype(F32) + r.E2C[y].astype(F32) + r.E2Y[...].astype(F32)
    n2_own, r2 = unit_rows(r.H[...])
    r.DH[...] = r.cot[...].astype(F32) + r2 * (e2 - n2_own * jnp.mean(e2 * n2_own, axis=1, keepdims=True))
    r.DB[c] = r.DH[...].astype(BF16)
    put(r.DB.at[c], r.DB.at[c], to_core, k.db)
    take(r.MXC.at[y], k.mxc + y)
    take(r.MXY, k.mxy)
    r.mixed[...] = (
        r.H[...] + r.MX[y, c].astype(F32) + r.MXC[y].astype(F32) + r.MXY[...].astype(F32)
    ).astype(BF16)
    take(r.DB.at[co], k.db)
    db_all = r.DB[...].reshape(CS * TOK, DIM)
    rows = [r.WO[h, pl.ds(2 * c, 2)].reshape(HALF, HALF) for h in range(CS)]
    d_att = dot_tb(db_all[:, :HALF], rows[0]) + dot_tb(db_all[:, HALF:], rows[1])
    r.DO[...] = d_att.astype(BF16).reshape(CS, TOK, HALF)
    att_all = jnp.concatenate(
        [jnp.concatenate((r.ATT[0, q], r.ATT[1, q]), axis=1) for q in range(CS)], axis=0
    )
    db_cols = r.DB[:, :, pl.ds(pl.multiple_of(HALF * c, 128), HALF)].reshape(CS * TOK, HALF)

    def chip_grad(ch, value):
        r.GA[ch] = value.astype(BF16).reshape(ZS, XS, YS, CHIP_ROWS, HALF)
        put(r.GA.at[ch, :, :, yo], r.GAY.at[ch], to_y, k.ray + ch)

    chip_grad(PAIRS, dot_ta(att_all, db_cols))

    def chip_from_y(ch):
        take(r.GAY.at[ch], k.ray + ch)
        r.GA[ch, :, :, y] = (r.GA[ch, :, :, y].astype(F32) + r.GAY[ch].astype(F32)).astype(BF16)
        put(r.GA.at[ch, :, xo, y], r.GAX.at[ch], to_x, k.rax + ch)

    def chip_from_x(ch):
        take(r.GAX.at[ch], k.rax + ch)
        r.GA[ch, :, x, y] = (r.GA[ch, :, x, y].astype(F32) + r.GAX[ch].astype(F32)).astype(BF16)
        for j, zz in enumerate(zo):
            put(r.GA.at[ch, zz, x, y], r.GAZ.at[ch, z], to_z[j], k.raz + 4 * ch + z)

    def chip_from_z(ch):
        total = r.GA[ch, z, x, y].astype(F32)
        for zz in zo:
            take(r.GAZ.at[ch, zz], k.raz + 4 * ch + zz)
            total = total + r.GAZ[ch, zz].astype(F32)
        r.FA[:, :, HALF * ch : HALF * ch + HALF] = total.reshape(CS, SHARD, HALF)

    reverse = (
        lax.broadcasted_iota(jnp.int32, (TOK, TOK), 0) + lax.broadcasted_iota(jnp.int32, (TOK, TOK), 1)
        == TOK - 1
    ).astype(BF16)
    reverse2 = jnp.concatenate((reverse, reverse), axis=1)

    def attention_pair_back(p):
        def one_sequence(q, carry):
            d_out = stack_heads(r.DO[q, :, 128 * p : 128 * p + 128].astype(F32))
            kv = r.KV.at[p, q]
            probs = r.PS[p, q]
            weighted = probs.astype(F32) * dot_tb(d_out, kv[:, 128:])
            delta = jnp.sum(weighted, axis=1, keepdims=True)
            d_scores = (weighted - probs.astype(F32) * delta).astype(BF16)
            r.DS[q] = d_scores
            r.DQ[p, q] = unstack_heads(dot(d_scores, kv[:, :128])).astype(BF16)
            r.DKV[p, q, :128] = dot_ta(r.QS[p, q], d_scores).astype(BF16)
            r.DKV[p, q, 128:] = dot_ta(d_out, probs).astype(BF16)
            return carry

        lax.fori_loop(0, CS, one_sequence, 0)
        for hh in range(2):
            both = r.DS[:, TOK * hh : TOK * hh + TOK, :].reshape(CS * TOK, LENGTH)
            padded = jnp.concatenate((dot(reverse2, both), jnp.zeros((TOK, TOK), F32)), axis=1)
            placed = pltpu.roll(padded, 0, 1, stride=1, stride_axis=0)
            r.DG[2 * p + hh : 2 * p + hh + 1, :] = jnp.sum(placed, axis=0, keepdims=True)
        kv_grad = dot(r.DKV[p, 0], r.N1[0].reshape(LENGTH, DIM)) + dot(
            r.DKV[p, 1], r.N1[1].reshape(LENGTH, DIM)
        )
        own_rows = r.N1O[...].reshape(CS * TOK, DIM)
        q_grad = dot_ta(r.DQ[p].reshape(CS * TOK, 128), own_rows)
        chip_grad(p, jnp.concatenate((q_grad, kv_grad), axis=0).astype(BF16).T)

    attention_pair_back(0)
    grad_from_x(r.GD, r.GDX, r.GDZ, k.rdx, k.rdz)
    chip_from_y(PAIRS)
    attention_pair_back(1)
    grad_from_x(r.GG, r.GGX, r.GGZ, k.rgx, k.rgz)
    chip_from_x(PAIRS)
    chip_from_y(0)
    attention_pair_back(2)
    chip_from_x(0)
    chip_from_y(1)

    r.DG[HEADS_HERE:, :] = jnp.zeros((8 - HEADS_HERE, SPAN), F32)
    onehot_back = (
        lax.broadcasted_iota(jnp.int32, (128, SPAN), 0)
        == r.BK[:, pl.ds(pl.multiple_of(LENGTH - TOK - TOK * s, 128), SPAN)]
    ).astype(F32)
    r.T1[...] = lax.dot_general(
        r.DG[...], onehot_back, (((1,), (1,)), ((), ())), precision=HIGHEST, preferred_element_type=F32
    )
    put(r.T1, r.TY, to_y, k.ty)

    w_kv = jnp.concatenate([r.WA[p].reshape(DIM, HALF)[:, 128:] for p in range(PAIRS)], axis=1)

    def token_grad(q, zz):
        lanes = pl.ds(pl.multiple_of(XS * TOK * zz, 128), XS * TOK)
        d_kv = r.DKV[:, q, :, lanes].reshape(PAIRS * 256, XS * TOK)
        out = dot(w_kv, d_kv)
        return [out[:, :TOK], out[:, TOK:]]

    def query_part(q):
        total = dot_tb(r.WA[0].reshape(DIM, HALF)[:, :128], r.DQ[0, q])
        for p in range(1, PAIRS):
            total = total + dot_tb(r.WA[p].reshape(DIM, HALF)[:, :128], r.DQ[p, q])
        return total

    for zz in zo + [z]:
        both = token_grad(co, zz)
        for xx in range(XS):
            r.DN[co, zz, xx] = both[xx].astype(BF16)
        if zz is z:
            r.DN[co, z, x] = (r.DN[co, z, x].astype(F32) + query_part(co)).astype(BF16)
        put(r.DN.at[co, zz], r.DNC.at[zz], to_core, k.dnc + zz)
    for zz in zo + [z]:
        both = token_grad(c, zz)
        for xx in range(XS):
            r.DN[c, zz, xx] = both[xx].astype(BF16)
        if zz is z:
            r.DN[c, z, x] = (r.DN[c, z, x].astype(F32) + query_part(c)).astype(BF16)
        take(r.DNC.at[zz], k.dnc + zz)
        r.DN[c, zz] = (r.DN[c, zz].astype(F32) + r.DNC[zz].astype(F32)).astype(BF16)
        put(r.DN.at[c, zz, xo], r.DNX.at[zz], to_x, k.dnx + zz)

    chip_from_x(1)
    chip_from_y(2)
    take(r.TY, k.ty)
    r.T2[...] = r.T1[...] + r.TY[...]
    put(r.T2, r.TX, to_x, k.tx)
    for j, zz in enumerate(zo + [z]):
        take(r.DNX.at[zz], k.dnx + zz)
        r.DN[c, zz, x] = (r.DN[c, zz, x].astype(F32) + r.DNX[zz].astype(F32)).astype(BF16)
        if j < ZS - 1:
            put(r.DN.at[c, zz, x], r.DNZ.at[z], to_z[j], k.dnz + z)
    chip_from_x(2)
    take(r.TX, k.tx)
    r.T3[...] = r.T2[...] + r.TX[...]
    for who in to_z:
        put(r.T3, r.TZ.at[z], who, k.tz + z)
    r.TZ[z] = r.T3[...]

    r.gwd[...] = sum_z(r.GD[z, x], r.GDZ, k.rdz)
    r.F4S[...] = sum_z(r.GG[z, x], r.GGZ, k.rgz).reshape(BATCH_DEVICES, SHARD, 2 * QUARTER)
    for q_y, q_c, who in ((y, co, to_core), (yo, c, to_y), (yo, co, to_diag)):
        put(r.F4S.at[CS * q_y + q_c], r.F4.at[b], who, k.f4 + b)
    r.F4[b] = r.F4S[b]
    chip_from_z(PAIRS)
    chip_from_z(0)
    chip_from_z(1)
    for q_y, q_c in ((y, co), (yo, c), (yo, co)):
        src = CS * q_y + q_c
        take(r.F4.at[src], k.f4 + src)
    gate_grad = join_quarters([r.F4[q, :, :QUARTER] for q in range(BATCH_DEVICES)])
    up_grad = join_quarters([r.F4[q, :, QUARTER:] for q in range(BATCH_DEVICES)])
    r.gwg[...] = gate_grad * gain_f
    r.gwu[...] = up_grad * gain_f
    r.ggf[...] = to_row(
        jnp.sum(gate_grad * r.wg[...].astype(F32) + up_grad * r.wu[...].astype(F32), axis=1, keepdims=True)
    )
    chip_from_z(2)
    put(r.FA.at[co], r.F2.at[c], to_core, k.f2)
    r.F2[c] = r.FA[c]

    for zz in zo:
        take(r.TZ.at[zz], k.tz + zz)
    r.TO[c] = (r.TZ[0] + r.TZ[1]) + (r.TZ[2] + r.TZ[3])
    put(r.TO.at[c], r.TO.at[c], to_core, k.tc)

    e1 = sum_z(r.DN[c, z, x], r.DNZ, k.dnz).T
    n1_own, r1 = unit_rows(tokens_f)
    r.tg[...] = (
        r.DH[...] + r1 * (e1 - n1_own * jnp.mean(e1 * n1_own, axis=1, keepdims=True))
    ).astype(BF16)

    take(r.F2.at[co], k.f2)
    gain_total = jnp.zeros((SHARD, 1), F32)
    for j, (w_ref, out_ref) in enumerate(((r.wq, r.gwq), (r.wk, r.gwk), (r.wv, r.gwv))):
        for h in range(CS):
            for p in range(PAIRS):
                lanes = slice(HALF * h + 128 * p, HALF * h + 128 * p + 128)
                grad = r.F2[h, :, HALF * p + 128 * j : HALF * p + 128 * j + 128]
                gain_total = gain_total + jnp.sum(grad * w_ref[:, lanes].astype(F32), axis=1, keepdims=True)
                out_ref[:, lanes] = grad * gain_a
    r.gga[...] = to_row(gain_total)
    for h in range(CS):
        r.gwo[:, HALF * h : HALF * h + HALF] = r.F2[h, :, 3 * HALF :]
    take(r.TO.at[co], k.tc)
    for q in range(CS):
        r.gtab[HEADS_HERE * q : HEADS_HERE * q + HEADS_HERE, :] = r.TO[q, :HEADS_HERE, :32]
    for copy in sent:
        copy.wait_send()


def finish_kernel(*refs):
    count = len(refs) // 2
    for src, dst in zip(refs[:count], refs[count:]):
        dst[...] = src[...]


def fused_device(
    tokens, segments, buckets, gain_attn, w_query, w_key, w_value, w_output,
    gain_ffn, w_gate, w_up, w_down, bucket_bias_matrix, cotangent,
):
    operands = (
        tokens.reshape(TOK, DIM),
        cotangent.reshape(TOK, DIM),
        segments.reshape(1, LENGTH),
        buckets.reshape(1, 2 * LENGTH - 1),
        bucket_bias_matrix.T,
        gain_attn.reshape(1, SHARD),
        gain_ffn.reshape(1, SHARD),
        w_query, w_key, w_value, w_output, w_gate, w_up, w_down,
    )
    out_shape = [jax.ShapeDtypeStruct(shape, dtype) for shape, dtype in OUTPUTS.values()]
    in_vmem = pl.BlockSpec(memory_space=pltpu.VMEM)
    outs = pl.pallas_call(
        layer_kernel,
        out_shape=out_shape,
        in_specs=[in_vmem] * len(operands),
        out_specs=[in_vmem] * len(out_shape),
        scratch_shapes=[pltpu.VMEM(shape, dtype) for shape, dtype in SCRATCH.values()]
        + [pltpu.SemaphoreType.DMA((SEND_COUNT,)), pltpu.SemaphoreType.DMA((RECV_COUNT,))],
        compiler_params=pltpu.CompilerParams(
            collective_id=0, has_side_effects=True, vmem_limit_bytes=63 * 2**20
        ),
        name="layer",
    )(*operands)
    outs = pl.pallas_call(
        finish_kernel,
        out_shape=out_shape,
        in_specs=[in_vmem] * len(out_shape),
        out_specs=[in_vmem] * len(out_shape),
        name="finish",
    )(*outs)
    mixed, tokens_grad, gga, gwq, gwk, gwv, gwo, ggf, gwg, gwu, gwd, table_grad = outs
    return (
        mixed.reshape(tokens.shape), tokens_grad.reshape(tokens.shape), gga.reshape(SHARD),
        gwq, gwk, gwv, gwo, ggf.reshape(SHARD), gwg, gwu, gwd, table_grad.T,
    )


def fits_fused(mesh):
    return mesh.shape["seq"] == SEQ_DEVICES and mesh.shape["batch"] == BATCH_DEVICES


def solution(mesh):
    return jax.shard_map(
        fused_device if fits_fused(mesh) else on_device,
        mesh=mesh,
        in_specs=(
            P("seq", "batch", None),
            P(None, "batch"),
            P(),
            P(("seq", "batch")),
            P(("seq", "batch"), None),
            P(("seq", "batch"), None),
            P(("seq", "batch"), None),
            P(("seq", "batch"), None),
            P(("seq", "batch")),
            P(("seq", "batch"), None),
            P(("seq", "batch"), None),
            P(("seq", "batch"), None),
            P(),
            P("seq", "batch", None),
        ),
        out_specs=(
            P("seq", "batch", None),
            P("seq", "batch", None),
            P(("seq", "batch")),
            P(("seq", "batch"), None),
            P(("seq", "batch"), None),
            P(("seq", "batch"), None),
            P(("seq", "batch"), None),
            P(("seq", "batch")),
            P(("seq", "batch"), None),
            P(("seq", "batch"), None),
            P(("seq", "batch"), None),
            P(),
        ),
        check_vma=False,
    )
```

```python
from functools import partial
import math
from types import SimpleNamespace

import jax
import jax.numpy as jnp
from jax import lax
from jax.experimental import pallas as pl
from jax.experimental.pallas import tpu as pltpu
from jax.sharding import PartitionSpec as P

EPSILON = 1e-06
NEGATIVE = -1e30
HIGHEST = lax.Precision.HIGHEST


def normalize(hidden_state, scale_vec):
    return (
        hidden_state
        * lax.rsqrt(jnp.mean(hidden_state * hidden_state, axis=-1, keepdims=True) + EPSILON)
        * scale_vec
    )


def gelu_tanh(gate_vals):
    return jax.nn.gelu(gate_vals, approximate=True)


def project(left_side, weight):
    return jnp.einsum("tsk,kn->tsn", left_side, weight, preferred_element_type=jnp.float32)


def project_back(grad_rows, weight):
    return jnp.einsum("tsn,kn->tsk", grad_rows, weight, preferred_element_type=jnp.float32)


def weight_grad(left_side, grad_rows):
    return jnp.einsum("tsk,tsn->kn", left_side, grad_rows, preferred_element_type=jnp.float32)


def position_bias(
    buckets, bucket_bias_matrix, query_start, key_start, query_rows, key_rows, seq_length
):
    span = query_rows + key_rows - 1
    head_count = bucket_bias_matrix.shape[1]
    first = key_start - query_start + seq_length - query_rows
    chosen = lax.dynamic_slice_in_dim(buckets, first, span, 0)
    onehot = (
        chosen[:, None] == jnp.arange(bucket_bias_matrix.shape[0], dtype=jnp.int32)[None, :]
    ).astype(jnp.float32)
    per_offset = jnp.dot(onehot, bucket_bias_matrix.astype(jnp.float32), precision=HIGHEST)
    padded = jnp.concatenate((per_offset.T, jnp.zeros((head_count, 1), jnp.float32)), axis=1)
    tiled = jnp.broadcast_to(padded[:, None, :], (head_count, query_rows, span + 1)).reshape(
        head_count, query_rows * (span + 1)
    )
    skewed = tiled[:, : query_rows * span].reshape(head_count, query_rows, span)
    return (onehot, skewed[:, :, query_rows - 1 : query_rows - 1 + key_rows])


def table_term(onehot, score_gradient):
    summed = jnp.sum(score_gradient.astype(jnp.float32), axis=0)
    head_count, query_rows, key_rows = summed.shape
    span = query_rows + key_rows - 1
    placed = jnp.pad(summed, ((0, 0), (0, 0), (query_rows - 1, 0))).reshape(
        head_count, query_rows * span
    )
    placed = jnp.pad(placed, ((0, 0), (0, query_rows)))
    diagonal_sums = jnp.sum(placed.reshape(head_count, query_rows, span + 1), axis=1)[:, :span]
    return jnp.dot(onehot.T, diagonal_sums.T, precision=HIGHEST)


def pair_scores(table_set, query_block, query_segs, query_start, key_block, key_segs, key_start):
    buckets, bucket_bias_matrix, seq_length = table_set
    onehot, bias_contributions = position_bias(
        buckets,
        bucket_bias_matrix,
        query_start,
        key_start,
        query_block.shape[0],
        key_block.shape[0],
        seq_length,
    )
    scores = (
        jnp.einsum("qshd,kshd->shqk", query_block, key_block, preferred_element_type=jnp.float32)
        + bias_contributions[None]
    )
    allowed = (query_segs.T[:, :, None] == key_segs.T[:, None, :])[:, None]
    return (onehot, scores, allowed)


def pair_grads(
    table_set,
    query_block,
    query_segs,
    query_start,
    dout_block,
    log_sums,
    deltas,
    key_block,
    value_block,
    key_segs,
    key_start,
):
    onehot, scores, allowed = pair_scores(
        table_set, query_block, query_segs, query_start, key_block, key_segs, key_start
    )
    probabilities = jnp.where(allowed, jnp.exp(scores - log_sums[..., None]), 0.0)
    dprobs = jnp.einsum(
        "qshd,kshd->shqk", dout_block, value_block, preferred_element_type=jnp.float32
    )
    score_gradient = (probabilities * (dprobs - deltas[..., None])).astype(jnp.bfloat16)
    return (onehot, probabilities, score_gradient)


def attend_block(setting, carried, blocks, key_start):
    table_set, segments, query_heads, query_segs, query_start = setting
    running_max, running_sum, accum = carried
    key_block, value_block = blocks
    key_segs = lax.dynamic_slice_in_dim(segments, key_start, key_block.shape[0], 0)
    _, scores, allowed = pair_scores(
        table_set, query_heads, query_segs, query_start, key_block, key_segs, key_start
    )
    new_max = jnp.maximum(running_max, jnp.max(jnp.where(allowed, scores, NEGATIVE), axis=-1))
    weights_raw = jnp.where(allowed, jnp.exp(scores - new_max[..., None]), 0.0)
    factor = jnp.exp(running_max - new_max)
    running_sum = running_sum * factor + jnp.sum(weights_raw, axis=-1)
    accum = accum * jnp.transpose(factor, (2, 0, 1))[..., None] + jnp.einsum(
        "shqk,kshd->qshd",
        weights_raw.astype(jnp.bfloat16),
        value_block,
        preferred_element_type=jnp.float32,
    )
    return (new_max, running_sum, accum)


def merged_block(setting, extras, carried, scan_item):
    table_set, segments, query_heads, query_segs, query_start = setting
    dout_heads, log_sums, deltas = extras
    dquery, dtable = carried
    key_start, key_block, value_block = scan_item
    key_rows = key_block.shape[0]
    seq_count = key_block.shape[1]
    key_segs = lax.dynamic_slice_in_dim(segments, key_start, key_rows, 0)
    onehot, probabilities, score_gradient = pair_grads(
        table_set,
        query_heads,
        query_segs,
        query_start,
        dout_heads,
        log_sums,
        deltas,
        key_block,
        value_block,
        key_segs,
        key_start,
    )
    dquery = dquery + jnp.einsum(
        "shqk,kshd->qshd", score_gradient, key_block, preferred_element_type=jnp.float32
    )
    dtable = dtable + table_term(onehot, score_gradient)
    key_gradient = jnp.einsum(
        "shqk,qshd->kshd", score_gradient, query_heads, preferred_element_type=jnp.float32
    )
    dvalue = jnp.einsum(
        "shqk,qshd->kshd",
        probabilities.astype(jnp.bfloat16),
        dout_heads,
        preferred_element_type=jnp.float32,
    )
    joined = jnp.concatenate(
        (key_gradient.reshape(key_rows, seq_count, -1), dvalue.reshape(key_rows, seq_count, -1)),
        axis=2,
    )
    return ((dquery, dtable), joined)


def fold_blocks(step_fn, carried, pieces):
    piece_rows = pieces[0].shape[0]
    block_rows = math.gcd(piece_rows, 512)
    block_count = piece_rows // block_rows
    stacked = tuple(
        (piece.reshape((block_count, block_rows) + piece.shape[1:]) for piece in pieces)
    )

    def advance(state_now, scan_item):
        block_index, blocks = scan_item
        return (step_fn(state_now, blocks, block_index * block_rows), None)

    result, _ = lax.scan(advance, carried, (jnp.arange(block_count, dtype=jnp.int32), stacked))
    return result


def on_device(
    tokens,
    segments,
    buckets,
    gain_attn,
    w_query,
    w_key,
    w_value,
    w_output,
    gain_ffn,
    w_gate,
    w_up,
    w_down,
    bucket_bias_matrix,
    cotangent,
):
    tok_rows, seq_count, _ = tokens.shape
    head_count = bucket_bias_matrix.shape[1]
    inner_width = w_query.shape[1]
    head_width = inner_width // head_count
    head_shape = (tok_rows, seq_count, head_count, head_width)
    seq_length = (buckets.shape[0] + 1) // 2
    query_start = lax.axis_index("seq") * tok_rows
    (
        full_gain_attn,
        full_query,
        full_key,
        full_value,
        full_output,
        full_gain_ffn,
        full_gate,
        full_up,
        full_down,
    ) = (
        lax.all_gather(gain_attn, ("seq", "batch"), axis=0, tiled=True),
        lax.all_gather(w_query, ("seq", "batch"), axis=0, tiled=True),
        lax.all_gather(w_key, ("seq", "batch"), axis=0, tiled=True),
        lax.all_gather(w_value, ("seq", "batch"), axis=0, tiled=True),
        lax.all_gather(w_output, ("seq", "batch"), axis=0, tiled=True),
        lax.all_gather(gain_ffn, ("seq", "batch"), axis=0, tiled=True),
        lax.all_gather(w_gate, ("seq", "batch"), axis=0, tiled=True),
        lax.all_gather(w_up, ("seq", "batch"), axis=0, tiled=True),
        lax.all_gather(w_down, ("seq", "batch"), axis=0, tiled=True),
    )
    tokens_full = tokens.astype(jnp.float32)
    normed1 = normalize(tokens_full, full_gain_attn.astype(jnp.float32)).astype(jnp.bfloat16)
    query_heads = project(normed1, full_query).astype(jnp.bfloat16).reshape(head_shape)
    key_heads = project(normed1, full_key).astype(jnp.bfloat16).reshape(head_shape)
    value_heads = project(normed1, full_value).astype(jnp.bfloat16).reshape(head_shape)
    query_segs = lax.dynamic_slice_in_dim(segments, query_start, tok_rows, 0)
    table_set = (buckets, bucket_bias_matrix, seq_length)
    setting = (table_set, segments, query_heads, query_segs, query_start)
    start_state = (
        jnp.full((seq_count, head_count, tok_rows), NEGATIVE, jnp.float32),
        jnp.zeros((seq_count, head_count, tok_rows), jnp.float32),
        jnp.zeros(head_shape, jnp.float32),
    )
    step_forward = partial(attend_block, setting)
    running_max, running_sum, accum = fold_blocks(
        step_forward,
        start_state,
        (
            lax.all_gather(key_heads, "seq", axis=0, tiled=True),
            lax.all_gather(value_heads, "seq", axis=0, tiled=True),
        ),
    )
    attended_full = accum / jnp.transpose(running_sum, (2, 0, 1))[..., None]
    log_sums = running_max + jnp.log(running_sum)
    attended = attended_full.astype(jnp.bfloat16).reshape(tok_rows, seq_count, inner_width)
    hidden1 = tokens_full + project(attended, full_output)
    normed2 = normalize(hidden1, full_gain_ffn.astype(jnp.float32)).astype(jnp.bfloat16)
    gate = project(normed2, full_gate)
    up_val = project(normed2, full_up)
    gelu_out, gelu_pull = jax.vjp(gelu_tanh, gate)
    activated = (gelu_out * up_val).astype(jnp.bfloat16)
    mixed = (hidden1 + project(activated, full_down)).astype(jnp.bfloat16)
    (
        full_gain_attn,
        full_query,
        full_key,
        full_value,
        full_output,
        full_gain_ffn,
        full_gate,
        full_up,
        full_down,
    ) = (
        lax.all_gather(gain_attn, ("seq", "batch"), axis=0, tiled=True),
        lax.all_gather(w_query, ("seq", "batch"), axis=0, tiled=True),
        lax.all_gather(w_key, ("seq", "batch"), axis=0, tiled=True),
        lax.all_gather(w_value, ("seq", "batch"), axis=0, tiled=True),
        lax.all_gather(w_output, ("seq", "batch"), axis=0, tiled=True),
        lax.all_gather(gain_ffn, ("seq", "batch"), axis=0, tiled=True),
        lax.all_gather(w_gate, ("seq", "batch"), axis=0, tiled=True),
        lax.all_gather(w_up, ("seq", "batch"), axis=0, tiled=True),
        lax.all_gather(w_down, ("seq", "batch"), axis=0, tiled=True),
    )
    grad_down = weight_grad(activated, cotangent)
    d_activated = project_back(cotangent, full_down)
    d_gate = gelu_pull(d_activated * up_val)[0].astype(jnp.bfloat16)
    d_up = (gelu_out * d_activated).astype(jnp.bfloat16)
    grad_gate = weight_grad(normed2, d_gate)
    grad_up = weight_grad(normed2, d_up)
    d_normed2 = project_back(d_gate, full_gate) + project_back(d_up, full_up)
    _, norm_pull2 = jax.vjp(normalize, hidden1, full_gain_ffn.astype(jnp.float32))
    d_hidden_part, grad_gain_ffn = norm_pull2(d_normed2)
    d_hidden1 = cotangent.astype(jnp.float32) + d_hidden_part
    d_branch = d_hidden1.astype(jnp.bfloat16)
    grad_output = weight_grad(attended, d_branch)
    dout_heads = project_back(d_branch, full_output).astype(jnp.bfloat16).reshape(head_shape)
    deltas = jnp.transpose(
        jnp.sum(dout_heads.astype(jnp.float32) * attended_full, axis=-1), (1, 2, 0)
    )
    extras = (dout_heads, log_sums, deltas)
    keys_all, values_all = (
        lax.all_gather(key_heads, "seq", axis=0, tiled=True),
        lax.all_gather(value_heads, "seq", axis=0, tiled=True),
    )
    block_rows = math.gcd(seq_length, 512)
    block_count = seq_length // block_rows
    stacked_keys = keys_all.reshape((block_count, block_rows) + keys_all.shape[1:])
    stacked_values = values_all.reshape((block_count, block_rows) + values_all.shape[1:])
    block_starts = jnp.arange(block_count, dtype=jnp.int32) * block_rows
    query_init = (
        jnp.zeros(head_shape, jnp.float32),
        jnp.zeros(bucket_bias_matrix.shape, jnp.float32),
    )
    (dquery, dtable), joined_all = lax.scan(
        partial(merged_block, setting, extras),
        query_init,
        (block_starts, stacked_keys, stacked_values),
    )
    every_key_contribution = joined_all.reshape(seq_length, seq_count, 2 * inner_width)
    key_sums = lax.psum_scatter(every_key_contribution, "seq", scatter_dimension=0, tiled=True)
    dkey_rows = key_sums[:, :, :inner_width].astype(jnp.bfloat16)
    dvalue_rows = key_sums[:, :, inner_width:].astype(jnp.bfloat16)
    dquery_rows = dquery.reshape(tok_rows, seq_count, inner_width).astype(jnp.bfloat16)
    grad_query = weight_grad(normed1, dquery_rows)
    grad_key = weight_grad(normed1, dkey_rows)
    grad_value = weight_grad(normed1, dvalue_rows)
    d_normed1 = (
        project_back(dquery_rows, full_query)
        + project_back(dkey_rows, full_key)
        + project_back(dvalue_rows, full_value)
    )
    _, norm_pull1 = jax.vjp(normalize, tokens_full, full_gain_attn.astype(jnp.float32))
    d_input_part, grad_gain_attn = norm_pull1(d_normed1)
    tokens_grad = (d_hidden1 + d_input_part).astype(jnp.bfloat16)
    owned = (
        lax.psum_scatter(grad_gain_attn, ("seq", "batch"), scatter_dimension=0, tiled=True),
        lax.psum_scatter(grad_query, ("seq", "batch"), scatter_dimension=0, tiled=True),
        lax.psum_scatter(grad_key, ("seq", "batch"), scatter_dimension=0, tiled=True),
        lax.psum_scatter(grad_value, ("seq", "batch"), scatter_dimension=0, tiled=True),
        lax.psum_scatter(grad_output, ("seq", "batch"), scatter_dimension=0, tiled=True),
        lax.psum_scatter(grad_gain_ffn, ("seq", "batch"), scatter_dimension=0, tiled=True),
        lax.psum_scatter(grad_gate, ("seq", "batch"), scatter_dimension=0, tiled=True),
        lax.psum_scatter(grad_up, ("seq", "batch"), scatter_dimension=0, tiled=True),
        lax.psum_scatter(grad_down, ("seq", "batch"), scatter_dimension=0, tiled=True),
    )
    table_total = lax.psum(dtable, ("seq", "batch"))
    return (
        mixed,
        tokens_grad,
        owned[0],
        owned[1],
        owned[2],
        owned[3],
        owned[4],
        owned[5],
        owned[6],
        owned[7],
        owned[8],
        table_total,
    )


BF16 = jnp.bfloat16
F32 = jnp.float32
MESH_IDS = pl.DeviceIdType.MESH

ZS, XS, YS, CS = 4, 2, 2, 2
SEQ_DEVICES = ZS * XS
BATCH_DEVICES = YS * CS
TOK = 128
LENGTH = SEQ_DEVICES * TOK
DIM = 768
HALF = DIM // CS
PAIRS = HALF // 128
SHARD = DIM // (SEQ_DEVICES * BATCH_DEVICES)
CHIP_ROWS = SHARD * CS
GROUP_ROWS = SHARD * BATCH_DEVICES
FF_ALL = 2048
QUARTER = FF_ALL // BATCH_DEVICES
DOWN_ROWS = FF_ALL // (SEQ_DEVICES * BATCH_DEVICES)
CHUNKS = PAIRS + 1
SPAN = LENGTH + TOK
HEADS_HERE = 2 * PAIRS


def dot(a, b):
    return lax.dot_general(a, b, (((1,), (0,)), ((), ())), preferred_element_type=F32)


def dot_tb(a, b):
    return lax.dot_general(a, b, (((1,), (1,)), ((), ())), preferred_element_type=F32)


def dot_ta(a, b):
    return lax.dot_general(a, b, (((0,), (0,)), ((), ())), preferred_element_type=F32)


def to_column(row):
    n = row.shape[1]
    eye = lax.broadcasted_iota(jnp.int32, (n, n), 0) == lax.broadcasted_iota(jnp.int32, (n, n), 1)
    return jnp.sum(jnp.where(eye, jnp.broadcast_to(row, (n, n)), 0.0), axis=1, keepdims=True)


def to_row(col):
    n = col.shape[0]
    eye = lax.broadcasted_iota(jnp.int32, (n, n), 0) == lax.broadcasted_iota(jnp.int32, (n, n), 1)
    return jnp.sum(jnp.where(eye, jnp.broadcast_to(col, (n, n)), 0.0), axis=0, keepdims=True)


def unit_rows(x):
    r = lax.rsqrt(jnp.mean(x * x, axis=1, keepdims=True) + EPSILON)
    return x * r, r


def stack_heads(pair):
    low = lax.broadcasted_iota(jnp.int32, pair.shape, 1) < 64
    return jnp.concatenate((jnp.where(low, pair, 0.0), jnp.where(low, 0.0, pair)), axis=0).astype(BF16)


def unstack_heads(stacked):
    rows = stacked.shape[0] // 2
    low = lax.broadcasted_iota(jnp.int32, (rows, 128), 1) < 64
    return jnp.where(low, stacked[:rows], stacked[rows:])


def split_quarters(whole):
    low = lax.broadcasted_iota(jnp.int32, (whole.shape[0], 128), 1) < 64
    parts = []
    for q in range(BATCH_DEVICES):
        cols = []
        for m in range(ZS):
            first = 4 * m + 2 * (q // 2)
            a = whole[:, 128 * first : 128 * first + 128]
            b = whole[:, 128 * (first + 1) : 128 * (first + 1) + 128]
            if q % 2 == 0:
                cols.append(jnp.where(low, a, pltpu.roll(b, 64, 1)))
            else:
                cols.append(jnp.where(low, pltpu.roll(a, 64, 1), b))
        parts.append(jnp.concatenate(cols, axis=1))
    return parts


def join_quarters(parts):
    low = lax.broadcasted_iota(jnp.int32, (parts[0].shape[0], 128), 1) < 64
    cols = []
    for block in range(FF_ALL // 128):
        m, xx, yy = block // 4, block // 2 % 2, block % 2
        lanes = slice(128 * m, 128 * m + 128)
        a, b = parts[2 * xx][:, lanes], parts[2 * xx + 1][:, lanes]
        if yy == 0:
            cols.append(jnp.where(low, a, pltpu.roll(b, 64, 1)))
        else:
            cols.append(jnp.where(low, pltpu.roll(a, 64, 1), b))
    return jnp.concatenate(cols, axis=1)


SCRATCH = dict(
    W_MINE=((CS, SHARD, 4 * HALF + 4 * QUARTER), F32),
    W_CORE=((CS, SHARD, 4 * HALF + 4 * QUARTER), F32),
    UB=((XS, CHIP_ROWS, 2 * QUARTER), BF16),
    WA=((PAIRS, ZS, XS, YS, CHIP_ROWS, HALF), BF16),
    WO=((CS, ZS, XS, YS, CHIP_ROWS, HALF), BF16),
    WG=((ZS, XS, YS, CHIP_ROWS, 2 * QUARTER), BF16),
    WD=((ZS, YS, DOWN_ROWS, DIM), BF16),
    X=((CS, ZS, XS, TOK, DIM), BF16),
    N1=((CS, ZS, XS, TOK, DIM), BF16),
    N1O=((CS, TOK, DIM), BF16),
    COT=((XS, CS, TOK, DIM), BF16),
    SEG=((CS, 8, LENGTH), F32),
    BK=((1, 2 * LENGTH), jnp.int32),
    PH=((2 * CS * PAIRS, SPAN), F32),
    BIAS=((PAIRS, 2 * TOK, LENGTH), F32),
    MASK=((CS, TOK, LENGTH), F32),
    KV=((PAIRS, CS, LENGTH, 256), BF16),
    QS=((PAIRS, CS, 2 * TOK, 128), BF16),
    PS=((PAIRS, CS, 2 * TOK, LENGTH), BF16),
    ATT=((CS, CS, TOK, HALF), BF16),
    H=((TOK, DIM), F32),
    N2=((XS, CS, TOK, DIM), BF16),
    ACT=((XS, 2 * TOK, QUARTER), BF16),
    DGU=((XS, 2 * TOK, 2 * QUARTER), BF16),
    MX=((XS, CS, TOK, DIM), BF16),
    MXC=((XS, TOK, DIM), BF16),
    MXS=((TOK, DIM), BF16),
    MXX=((TOK, DIM), BF16),
    E2=((XS, CS, TOK, DIM), BF16),
    E2C=((XS, TOK, DIM), BF16),
    E2S=((TOK, DIM), BF16),
    E2X=((TOK, DIM), BF16),
    GG=((ZS, XS, YS, CHIP_ROWS, 2 * QUARTER), BF16),
    GGY=((ZS, XS, CHIP_ROWS, 2 * QUARTER), BF16),
    GGZ=((ZS, XS, CHIP_ROWS, 2 * QUARTER), BF16),
    GGC=((XS, CHIP_ROWS, 2 * QUARTER), BF16),
    GD=((ZS, YS, DOWN_ROWS, DIM), BF16),
    GDY=((ZS, DOWN_ROWS, DIM), BF16),
    GDZ=((ZS, DOWN_ROWS, DIM), BF16),
    GDC=((DOWN_ROWS, DIM), BF16),
    F4S=((XS, CHIP_ROWS, 2 * QUARTER), BF16),
    F4X=((CHIP_ROWS, 2 * QUARTER), BF16),
    F4S2=((CS, XS, SHARD, 2 * QUARTER), F32),
    F4=((CS, XS, SHARD, 2 * QUARTER), F32),
    DH=((TOK, DIM), F32),
    DB=((CS, TOK, DIM), BF16),
    DO=((CS, TOK, HALF), BF16),
    DS=((CS, 2 * TOK, LENGTH), BF16),
    DQ=((PAIRS, CS, TOK, 128), BF16),
    DKV=((PAIRS, CS, 256, LENGTH), BF16),
    DG=((8, SPAN), F32),
    GA=((CHUNKS, ZS, XS, YS, CHIP_ROWS, HALF), BF16),
    GA1=((CHUNKS, ZS, 2, CHIP_ROWS, HALF), BF16),
    GA2=((CHUNKS, ZS, CHIP_ROWS, HALF), BF16),
    GAZ=((CHUNKS, ZS, CHIP_ROWS, HALF), BF16),
    GAC=((CHUNKS, CHIP_ROWS, HALF), BF16),
    FA=((CS, SHARD, 4 * HALF), F32),
    F2=((CS, SHARD, 4 * HALF), F32),
    DN=((CS, ZS, XS, DIM, TOK), BF16),
    DNC=((ZS, XS, DIM, TOK), BF16),
    DNX=((ZS, DIM, TOK), BF16),
    DNZ=((ZS, DIM, TOK), BF16),
    DNT=((DIM, TOK), BF16),
    T1=((8, 128), F32),
    TY=((8, 128), F32),
    T2=((8, 128), F32),
    TX=((8, 128), F32),
    T3=((8, 128), F32),
    TZ=((ZS, 8, 128), F32),
    TO=((CS, 8, 128), F32),
)
SEND_COUNT = 224
SLOTS = dict(
    segc=1, wc=1, u=1, xz=4, xx=4, xc=8, wz=4 * CHUNKS, wx=4 * CHUNKS, wy=4 * CHUNKS, wr=CHUNKS, woc=1,
    gz=8, gy=8, dz=4, dy=4, cotx=1, cotc=2, att=1, n2x=1, n2c=2, mxc=2, mxx=1, e2c=2, e2x=1,
    rdy=4, rdz=4, rdc=1, rgy=4, rgz=4, rgc=1, f4x=1, f4=1, db=1,
    ra1=CHUNKS, ra2=CHUNKS, raz=4 * CHUNKS, rac=CHUNKS, f2=1,
    dnc=4, dnx=4, dnz=4, dnt=1, ty=1, tx=1, tz=4, tc=1,
)
RECV_COUNT = sum(SLOTS.values())


def slot_bases():
    bases, used = {}, 0
    for name, count in SLOTS.items():
        bases[name] = used
        used += count
    return SimpleNamespace(**bases)


INPUTS = dict(
    tok=0, cot=0, seg=0, buckets=0, table=0, ga=0, gf=0, wq=0, wk=0, wv=0, wo=0, wg=0, wu=0, wd=0
)
OUTPUTS = dict(
    mixed=((TOK, DIM), BF16), tg=((TOK, DIM), BF16), gga=((1, SHARD), F32),
    gwq=((SHARD, DIM), F32), gwk=((SHARD, DIM), F32), gwv=((SHARD, DIM), F32), gwo=((SHARD, DIM), F32),
    ggf=((1, SHARD), F32), gwg=((SHARD, FF_ALL), F32), gwu=((SHARD, FF_ALL), F32),
    gwd=((DOWN_ROWS, DIM), F32), gtab=((2 * CS * PAIRS, 32), F32),
)


RELAY_TO_Y = (True, True, True, True)
HEAVY_X = (True, True, True, True)


def layer_kernel(*refs):
    names = (*INPUTS, *OUTPUTS, *SCRATCH)
    r = SimpleNamespace(**dict(zip(names, refs[:-2], strict=True)))
    ssem, rsem = refs[-2:]
    k = slot_bases()
    s, b = lax.axis_index("seq"), lax.axis_index("batch")
    z, x = s // XS, s % XS
    y, c = b // CS, b % CS
    xo, yo, co = 1 - x, 1 - y, 1 - c
    side = z // 2
    m = z + side * (3 - 2 * z)
    at_end, beside = m == 0, m == 1
    zord = [near + side * (3 - 2 * near) for near in (1 - m, 2, 3)]

    def at(zz, xx, yy, cc):
        return (XS * zz + xx, CS * yy + cc)

    to_core, to_x, to_y = at(z, x, y, co), at(z, xo, y, c), at(z, x, yo, c)
    to_z = [at(zz, x, y, c) for zz in zord]

    barrier = pltpu.get_barrier_semaphore()
    friends = [to_core, to_x, to_y] + to_z
    for who in friends:
        pl.semaphore_signal(barrier, inc=1, device_id=who, device_id_type=MESH_IDS)

    sent = []

    def put(src, dst, who, slot, when=None):
        copy = pltpu.make_async_remote_copy(
            src_ref=src, dst_ref=dst, send_sem=ssem.at[len(sent)], recv_sem=rsem.at[slot],
            device_id=who, device_id_type=MESH_IDS,
        )
        if when is None:
            copy.start()
        else:
            pl.when(when)(copy.start)
        sent.append((copy, when))

    def take(dst, slot, when=None):
        wait = pltpu.make_async_remote_copy(
            src_ref=dst, dst_ref=dst, send_sem=ssem.at[0], recv_sem=rsem.at[slot],
            device_id=to_core, device_id_type=MESH_IDS,
        ).wait_recv
        if when is None:
            wait()
        else:
            pl.when(when)(wait)

    def z_send(src, dst, slot):
        put(src, dst, to_z[0], slot + z)
        put(src, dst, to_z[1], slot + z)
        put(src, dst, to_z[2], slot + z, when=beside)

    def z_take(block, slot, i):
        zz = zord[i]
        take(block(zz), slot + zz)
        if i == 2:
            put(block(zz), block(zz), to_z[0], slot + zz, when=beside)

    def z_scatter(part, land, chain, slot, chain_slot, i):
        if i == 2:
            put(part(zord[2]), chain, to_z[0], chain_slot, when=at_end)
        else:
            put(part(zord[i]), land.at[z], to_z[i], slot + z)

    def z_chain(part, land, chain, slot, chain_slot):
        @pl.when(beside)
        def _():
            take(chain, chain_slot)
            mine = part(zord[2])
            mine[...] = (mine[...].astype(F32) + chain[...].astype(F32)).astype(BF16)

        put(part(zord[2]), land.at[z], to_z[2], slot + z, when=beside)

    def z_zero(land):
        @pl.when(at_end)
        def _():
            land[zord[2]] = jnp.zeros(land.shape[1:], land.dtype)

    def z_sum(own, land, slot):
        take(land.at[zord[0]], slot + zord[0])
        take(land.at[zord[1]], slot + zord[1])
        take(land.at[zord[2]], slot + zord[2], when=beside)
        total = own.astype(F32)
        for zz in zord:
            total = total + land[zz].astype(F32)
        return total

    gain_a = to_column(r.ga[...].astype(F32))
    gain_f = to_column(r.gf[...].astype(F32))
    tok = r.tok
    r.SEG[c] = jnp.broadcast_to(r.seg[...].astype(F32), (8, LENGTH))
    for h in range(CS):
        for p in range(PAIRS):
            for j, w_ref in enumerate((r.wq, r.wk, r.wv)):
                lanes = slice(HALF * h + 128 * p, HALF * h + 128 * p + 128)
                r.W_MINE[h, :, HALF * p + 128 * j : HALF * p + 128 * j + 128] = (
                    w_ref[:, lanes].astype(F32) * gain_a
                )
        r.W_MINE[h, :, 3 * HALF : 4 * HALF] = r.wo[:, HALF * h : HALF * h + HALF].astype(F32)
    for j, w_ref in enumerate((r.wg, r.wu)):
        for q, part in enumerate(split_quarters(w_ref[...].astype(F32) * gain_f)):
            first = 4 * HALF + 2 * QUARTER * (q // CS) + QUARTER * j
            r.W_MINE[q % CS, :, first : first + QUARTER] = part

    pl.semaphore_wait(barrier, len(friends))

    put(r.W_MINE.at[co], r.W_CORE.at[c], to_core, k.wc)
    put(tok, r.X.at[c, z, x], to_x, k.xx + z)
    put(r.SEG.at[c], r.SEG.at[c], to_core, k.segc)
    put(tok, r.X.at[c, z, x], to_core, k.xc + s)
    put(r.wd, r.WD.at[z, y], to_y, k.dy + z)
    r.X[c, z, x] = tok[...]
    r.WD[z, y] = r.wd[...]
    r.W_CORE[c] = r.W_MINE[c]
    z_send(r.wd, r.WD.at[z, y], k.dz)

    def weight(ch):
        return r.WA.at[ch] if ch < PAIRS else r.WO.at[c]

    def weight_start(ch):
        own = weight(ch).at[z, x, y]
        z_send(own, own, k.wz + 4 * ch)
        put(own, own, to_y, k.wy + 4 * ch + z)
        put(own, own, to_x, k.wx + 4 * ch + z)

    def norm_block(q, zz, xx, own=False):
        value = unit_rows(r.X[q, zz, xx].astype(F32))[0].astype(BF16)
        r.N1[q, zz, xx] = value
        if own:
            r.N1O[q] = value

    def token_from_z(i):
        z_take(lambda zz: r.X.at[c, zz, x], k.xz, i)
        zz = zord[i]
        put(r.X.at[c, zz, x], r.X.at[c, zz, x], to_x, k.xx + zz)
        put(r.X.at[c, zz, x], r.X.at[c, zz, x], to_core, k.xc + XS * zz + x)
        norm_block(c, zz, x)

    def token_from_x(zz):
        take(r.X.at[c, zz, xo], k.xx + zz)
        put(r.X.at[c, zz, xo], r.X.at[c, zz, xo], to_core, k.xc + XS * zz + xo)
        norm_block(c, zz, xo)

    def token_from_core(zz, xx):
        take(r.X.at[co, zz, xx], k.xc + XS * zz + xx)
        norm_block(co, zz, xx, own=zz is z and xx is x)

    def bias_lines():
        r.BK[...] = jnp.zeros(r.BK.shape, jnp.int32)
        r.BK[:, : 2 * LENGTH - 1] = r.buckets[...]
        onehot = (
            lax.broadcasted_iota(jnp.int32, (32, SPAN), 0)
            == r.BK[:, pl.ds(pl.multiple_of(LENGTH - TOK - TOK * s, 128), SPAN)]
        )
        r.PH[...] = dot(r.table[...], onehot.astype(BF16))

    def bias_pair(p):
        for hh in range(2):
            line = r.PH[pl.ds(HEADS_HERE * c + 2 * p + hh, 1), :]
            skewed = pltpu.roll(
                jnp.broadcast_to(line, (TOK, SPAN)), SPAN - TOK + 1, 1, stride=1, stride_axis=0
            )
            r.BIAS[p, TOK * hh : TOK * hh + TOK, :] = skewed[:, :LENGTH]

    def masks():
        take(r.SEG.at[co], k.segc)
        for q in range(CS):
            col = to_column(r.SEG[q, 0:1, pl.ds(pl.multiple_of(TOK * s, 128), TOK)])
            r.MASK[q] = jnp.where(col == r.SEG[q, 0:1, :], 0.0, NEGATIVE)

    def weight_from_z(ch, i):
        w = weight(ch)
        z_take(lambda zz: w.at[zz, x, y], k.wz + 4 * ch, i)
        arrived = w.at[zord[i], x, y]
        put(arrived, arrived, to_y, k.wy + 4 * ch + zord[i])
        put(arrived, arrived, to_x, k.wx + 4 * ch + zord[i])

    def weight_relay(ch):
        w = weight(ch)
        for zz in [z] + zord:
            if RELAY_TO_Y[ch]:
                take(w.at[zz, xo, y], k.wx + 4 * ch + zz)
            else:
                take(w.at[zz, x, yo], k.wy + 4 * ch + zz)
        if RELAY_TO_Y[ch]:
            put(w.at[:, xo, y], w.at[:, xo, y], to_y, k.wr + ch)
        else:
            put(w.at[:, x, yo], w.at[:, x, yo], to_x, k.wr + ch)

    def weight_end(ch):
        w = weight(ch)
        for zz in [z] + zord:
            if RELAY_TO_Y[ch]:
                take(w.at[zz, x, yo], k.wy + 4 * ch + zz)
            else:
                take(w.at[zz, xo, y], k.wx + 4 * ch + zz)
        take(w.at[:, xo, yo], k.wr + ch)

    def gate_send(xx):
        own = r.WG.at[z, xx, y]
        z_send(own, own, k.gz + 4 * xx)
        put(own, own, to_y, k.gy + 4 * xx + z)

    def gate_from_z(xx, i):
        z_take(lambda zz: r.WG.at[zz, xx, y], k.gz + 4 * xx, i)
        arrived = r.WG.at[zord[i], xx, y]
        put(arrived, arrived, to_y, k.gy + 4 * xx + zord[i])

    def down_from_z(i):
        z_take(lambda zz: r.WD.at[zz, y], k.dz, i)
        put(r.WD.at[zord[i], y], r.WD.at[zord[i], y], to_y, k.dy + zord[i])

    take(r.W_CORE.at[co], k.wc)
    shard = r.W_CORE[...].reshape(CHIP_ROWS, 4 * HALF + 4 * QUARTER).astype(BF16)
    for ch in range(PAIRS):
        r.WA[ch, z, x, y] = shard[:, HALF * ch : HALF * ch + HALF]
    r.WO[c, z, x, y] = shard[:, 3 * HALF : 4 * HALF]
    for xx in range(XS):
        first = 4 * HALF + 2 * QUARTER * xx
        r.UB[xx] = shard[:, first : first + 2 * QUARTER]
    weight_start(0)
    put(r.UB.at[xo], r.WG.at[z, x, y], to_x, k.u)
    weight_start(1)
    weight_start(2)
    r.WG[z, x, y] = r.UB[x]
    z_send(tok, r.X.at[c, z, x], k.xz)
    weight_start(PAIRS)
    gate_send(x)

    def gate_other():
        take(r.WG.at[z, xo, y], k.u)
        gate_send(xo)

    def cot_send():
        put(r.cot, r.COT.at[x, c], to_core, k.cotc + 0)
        put(r.cot, r.COT.at[x, c], to_x, k.cotx)
        r.COT[x, c] = r.cot[...]

    def cot_from_x():
        take(r.COT.at[xo, c], k.cotx)
        put(r.COT.at[xo, c], r.COT.at[xo, c], to_core, k.cotc + 1)

    def output_send():
        put(r.WO.at[c], r.WO.at[c], to_core, k.woc)

    zall = [z] + zord

    def attention_pair(p):
        w_pair = r.WA.at[p]

        def one_sequence(q, carry):
            w = w_pair[...].reshape(DIM, HALF)
            n1 = r.N1[q].reshape(LENGTH, DIM)
            kv = dot(n1, w[:, 128:]).astype(BF16)
            r.KV[p, q] = kv
            stacked = stack_heads(dot(r.N1O[q], w[:, :128]))
            r.QS[p, q] = stacked
            mask = r.MASK[q]
            scores = dot_tb(stacked, kv[:, :128]) + r.BIAS[p] + jnp.concatenate((mask, mask), axis=0)
            weights = jnp.exp(scores - jnp.max(scores, axis=1, keepdims=True))
            probs = (weights * (1.0 / jnp.sum(weights, axis=1, keepdims=True))).astype(BF16)
            r.PS[p, q] = probs
            r.ATT[c, q, :, 128 * p : 128 * p + 128] = unstack_heads(dot(probs, kv[:, 128:])).astype(BF16)
            return carry

        lax.fori_loop(0, CS, one_sequence, 0)

    def attended_send():
        put(r.ATT.at[c], r.ATT.at[c], to_core, k.att)

    token_from_core(z, x)
    bias_lines()
    gate_other()
    weight_from_z(0, 1)
    masks()
    cot_send()
    weight_from_z(1, 0)
    bias_pair(2)
    bias_pair(1)
    down_from_z(1)
    token_from_z(0)
    weight_from_z(2, 0)
    token_from_x(z)
    weight_from_z(0, 0)
    bias_pair(0)
    weight_from_z(1, 1)
    weight_from_z(2, 1)
    token_from_core(zord[0], x)
    down_from_z(0)
    weight_from_z(1, 2)
    token_from_core(z, xo)
    down_from_z(2)
    weight_from_z(0, 2)
    token_from_x(zord[0])
    weight_from_z(2, 2)
    norm_block(c, z, x, own=True)
    token_from_z(1)
    weight_relay(0)
    weight_relay(1)
    weight_relay(2)
    token_from_core(zord[0], xo)
    token_from_z(2)
    token_from_x(zord[1])
    token_from_core(zord[2], x)
    weight_end(0)
    token_from_x(zord[2])
    weight_from_z(PAIRS, 2)
    token_from_core(zord[1], x)
    weight_end(1)
    gate_from_z(x, 0)
    weight_from_z(PAIRS, 0)
    weight_from_z(PAIRS, 1)
    weight_end(2)
    token_from_core(zord[2], xo)
    token_from_core(zord[1], xo)
    gate_from_z(xo, 0)
    attention_pair(2)
    weight_relay(PAIRS)
    attention_pair(0)
    gate_from_z(xo, 2)
    cot_from_x()
    gate_from_z(xo, 1)
    weight_end(PAIRS)
    attention_pair(1)
    output_send()
    gate_from_z(x, 2)
    attended_send()
    gate_from_z(x, 1)
    take(r.WO.at[co], k.woc)
    take(r.ATT.at[co], k.att)

    att_own = jnp.concatenate((r.ATT[0, c], r.ATT[1, c]), axis=1)
    tokens_f = tok[...].astype(F32)
    r.H[...] = tokens_f + jnp.concatenate(
        (dot(att_own, r.WO[0].reshape(DIM, HALF)), dot(att_own, r.WO[1].reshape(DIM, HALF))), axis=1
    )
    r.N2[x, c] = unit_rows(r.H[...])[0].astype(BF16)
    put(r.N2.at[x, c], r.N2.at[x, c], to_core, k.n2c + 0)
    put(r.N2.at[x, c], r.N2.at[x, c], to_x, k.n2x)

    for zz in [z] + zord:
        for xx in range(XS):
            take(r.WG.at[zz, xx, yo], k.gy + 4 * xx + zz)
        take(r.WD.at[zz, yo], k.dy + zz)
    take(r.COT.at[x, co], k.cotc + 0)
    take(r.COT.at[xo, co], k.cotc + 1)
    take(r.N2.at[x, co], k.n2c + 0)

    def feed_forward(xx):
        w_gu = r.WG[...].reshape(DIM, 2 * QUARTER)
        w_d = r.WD[...].reshape(QUARTER, DIM)
        n2 = r.N2[xx].reshape(2 * TOK, DIM)
        g = r.COT[xx].reshape(2 * TOK, DIM)
        gate = dot(n2, w_gu[:, :QUARTER])
        up = dot(n2, w_gu[:, QUARTER:])
        d_act = dot_tb(g, w_d)
        square = gate * gate
        inner = math.sqrt(2 / math.pi) * gate * (1.0 + 0.044715 * square)
        tanh = jnp.tanh(inner)
        half_open = 0.5 * (1.0 + tanh)
        gelu = gate * half_open
        slope = half_open + 0.5 * gate * (1.0 - tanh * tanh) * (
            math.sqrt(2 / math.pi) * (1.0 + 3 * 0.044715 * square)
        )
        act = (gelu * up).astype(BF16)
        r.ACT[xx] = act
        d_gu = jnp.concatenate(
            ((slope * (up * d_act)).astype(BF16), (gelu * d_act).astype(BF16)), axis=1
        )
        r.DGU[xx] = d_gu
        r.E2[xx] = dot_tb(d_gu, w_gu).astype(BF16).reshape(CS, TOK, DIM)
        put(r.E2.at[xx, co], r.E2C.at[xx], to_core, k.e2c + xx)
        r.MX[xx] = dot(act, w_d).astype(BF16).reshape(CS, TOK, DIM)
        put(r.MX.at[xx, co], r.MXC.at[xx], to_core, k.mxc + xx)

    feed_forward(x)
    take(r.N2.at[xo, c], k.n2x)
    put(r.N2.at[xo, c], r.N2.at[xo, c], to_core, k.n2c + 1)
    take(r.N2.at[xo, co], k.n2c + 1)
    feed_forward(xo)
    take(r.E2C.at[xo], k.e2c + xo)
    r.E2S[...] = (r.E2[xo, c].astype(F32) + r.E2C[xo].astype(F32)).astype(BF16)
    put(r.E2S, r.E2X, to_x, k.e2x)

    far_first = [zord[2], zord[1], zord[0], z]

    def down_grad(zz):
        return r.GD.at[zz, y]

    def gate_grad(zz):
        return r.GG.at[zz, :, y]

    def grad_from_y(part, got, slot, scatter, i):
        zz = far_first[i]
        take(got.at[zz], slot + zz)
        mine = part(zz)
        mine[...] = (mine[...].astype(F32) + got[zz].astype(F32)).astype(BF16)
        if i < 3:
            z_scatter(part, *scatter, 2 - i)

    down_scatter = (r.GDZ, r.GDC, k.rdz, k.rdc)
    gate_scatter = (r.GGZ, r.GGC, k.rgz, k.rgc)

    def down_from_y(i):
        grad_from_y(down_grad, r.GDY, k.rdy, down_scatter, i)

    def gate_from_y(i):
        grad_from_y(gate_grad, r.GGY, k.rgy, gate_scatter, i)

    def down_chain():
        z_chain(down_grad, *down_scatter)

    def gate_chain():
        z_chain(gate_grad, *gate_scatter)

    def chip_grad(ch, value):
        r.GA[ch] = value.astype(BF16).reshape(ZS, XS, YS, CHIP_ROWS, HALF)
        if HEAVY_X[ch]:
            put(r.GA.at[ch, :, xo], r.GA1.at[ch], to_x, k.ra1 + ch)
        else:
            put(r.GA.at[ch, :, :, yo], r.GA1.at[ch], to_y, k.ra1 + ch)

    def chip_step1(ch):
        take(r.GA1.at[ch], k.ra1 + ch)
        if HEAVY_X[ch]:
            r.GA[ch, :, x] = (r.GA[ch, :, x].astype(F32) + r.GA1[ch].astype(F32)).astype(BF16)
            put(r.GA.at[ch, :, x, yo], r.GA2.at[ch], to_y, k.ra2 + ch)
        else:
            r.GA[ch, :, :, y] = (r.GA[ch, :, :, y].astype(F32) + r.GA1[ch].astype(F32)).astype(BF16)
            put(r.GA.at[ch, :, xo, y], r.GA2.at[ch], to_x, k.ra2 + ch)

    def chip_scatter(ch):
        return (lambda zz: r.GA.at[ch, zz, x, y]), r.GAZ.at[ch], r.GAC.at[ch], k.raz + 4 * ch, k.rac + ch

    def chip_step2(ch):
        take(r.GA2.at[ch], k.ra2 + ch)
        r.GA[ch, :, x, y] = (r.GA[ch, :, x, y].astype(F32) + r.GA2[ch].astype(F32)).astype(BF16)
        for i in (2, 1, 0):
            z_scatter(*chip_scatter(ch), i)

    def chip_chain(ch):
        z_chain(*chip_scatter(ch))

    def chip_end(ch):
        total = z_sum(r.GA[ch, z, x, y], r.GAZ.at[ch], k.raz + 4 * ch)
        r.FA[:, :, HALF * ch : HALF * ch + HALF] = total.reshape(CS, SHARD, HALF)

    reverse = (
        lax.broadcasted_iota(jnp.int32, (TOK, TOK), 0) + lax.broadcasted_iota(jnp.int32, (TOK, TOK), 1)
        == TOK - 1
    ).astype(BF16)
    reverse2 = jnp.concatenate((reverse, reverse), axis=1)

    def attention_pair_back(p):
        def one_sequence(q, carry):
            d_out = stack_heads(r.DO[q, :, 128 * p : 128 * p + 128].astype(F32))
            kv = r.KV.at[p, q]
            probs = r.PS[p, q]
            weighted = probs.astype(F32) * dot_tb(d_out, kv[:, 128:])
            delta = jnp.sum(weighted, axis=1, keepdims=True)
            d_scores = (weighted - probs.astype(F32) * delta).astype(BF16)
            r.DS[q] = d_scores
            r.DQ[p, q] = unstack_heads(dot(d_scores, kv[:, :128])).astype(BF16)
            r.DKV[p, q, :128] = dot_ta(r.QS[p, q], d_scores).astype(BF16)
            r.DKV[p, q, 128:] = dot_ta(d_out, probs).astype(BF16)
            return carry

        lax.fori_loop(0, CS, one_sequence, 0)
        kv_grad = dot(r.DKV[p, 0], r.N1[0].reshape(LENGTH, DIM)) + dot(
            r.DKV[p, 1], r.N1[1].reshape(LENGTH, DIM)
        )
        own_rows = r.N1O[...].reshape(CS * TOK, DIM)
        q_grad = dot_ta(r.DQ[p].reshape(CS * TOK, 128), own_rows)
        chip_grad(p, jnp.concatenate((q_grad, kv_grad), axis=0).astype(BF16).T)
        for hh in range(2):
            both = r.DS[:, TOK * hh : TOK * hh + TOK, :].reshape(CS * TOK, LENGTH)
            padded = jnp.concatenate((dot(reverse2, both), jnp.zeros((TOK, TOK), F32)), axis=1)
            placed = pltpu.roll(padded, 0, 1, stride=1, stride_axis=0)
            r.DG[2 * p + hh : 2 * p + hh + 1, :] = jnp.sum(placed, axis=0, keepdims=True)

    w_kv = jnp.concatenate([r.WA[p].reshape(DIM, HALF)[:, 128:] for p in range(PAIRS)], axis=1)

    def token_grad(q, zz):
        lanes = pl.ds(pl.multiple_of(XS * TOK * zz, 128), XS * TOK)
        d_kv = r.DKV[:, q, :, lanes].reshape(PAIRS * 256, XS * TOK)
        out = dot(w_kv, d_kv)
        for xx in range(XS):
            r.DN[q, zz, xx] = out[:, TOK * xx : TOK * xx + TOK].astype(BF16)
        if zz is z:
            total = r.DN[q, z, x].astype(F32)
            for p in range(PAIRS):
                total = total + dot_tb(r.WA[p].reshape(DIM, HALF)[:, :128], r.DQ[p, q])
            r.DN[q, z, x] = total.astype(BF16)

    def token_exchange(zz):
        token_grad(co, zz)
        put(r.DN.at[co, zz], r.DNC.at[zz], to_core, k.dnc + zz)
        token_grad(c, zz)

    def token_to_x(zz):
        take(r.DNC.at[zz], k.dnc + zz)
        r.DN[c, zz] = (r.DN[c, zz].astype(F32) + r.DNC[zz].astype(F32)).astype(BF16)
        put(r.DN.at[c, zz, xo], r.DNX.at[zz], to_x, k.dnx + zz)

    def token_part(zz):
        return r.DN.at[c, zz, x]

    token_scatter = (r.DNZ, r.DNT, k.dnz, k.dnt)

    def token_chain():
        z_chain(token_part, *token_scatter)

    def token_to_z(i):
        zz = far_first[i]
        take(r.DNX.at[zz], k.dnx + zz)
        r.DN[c, zz, x] = (r.DN[c, zz, x].astype(F32) + r.DNX[zz].astype(F32)).astype(BF16)
        if i < 3:
            z_scatter(token_part, *token_scatter, 2 - i)

    def grads_down():
        cot_all = r.COT[...].reshape(4 * TOK, DIM)
        r.GD[...] = dot_ta(r.ACT[...].reshape(4 * TOK, QUARTER), cot_all).astype(BF16).reshape(
            ZS, YS, DOWN_ROWS, DIM
        )
        for zz in far_first:
            put(r.GD.at[zz, yo], r.GDY.at[zz], to_y, k.rdy + zz)

    def grads_gate():
        n2_all = r.N2[...].reshape(4 * TOK, DIM)
        d_gu_all = r.DGU[...].reshape(4 * TOK, 2 * QUARTER)
        r.GG[...] = dot_ta(n2_all, d_gu_all).astype(BF16).reshape(ZS, XS, YS, CHIP_ROWS, 2 * QUARTER)
        for zz in far_first:
            put(r.GG.at[zz, :, yo], r.GGY.at[zz], to_y, k.rgy + zz)

    def zeros():
        z_zero(r.GDZ)
        z_zero(r.GGZ)
        z_zero(r.DNZ)
        for ch in range(CHUNKS):
            z_zero(r.GAZ.at[ch])

    def hidden_back():
        take(r.E2C.at[x], k.e2c + x)
        take(r.E2X, k.e2x)
        e2 = r.E2[x, c].astype(F32) + r.E2C[x].astype(F32) + r.E2X[...].astype(F32)
        n2_own, r2 = unit_rows(r.H[...])
        r.DH[...] = r.cot[...].astype(F32) + r2 * (
            e2 - n2_own * jnp.mean(e2 * n2_own, axis=1, keepdims=True)
        )
        r.DB[c] = r.DH[...].astype(BF16)
        put(r.DB.at[c], r.DB.at[c], to_core, k.db)

    def mixed_send():
        take(r.MXC.at[xo], k.mxc + xo)
        r.MXS[...] = (r.MX[xo, c].astype(F32) + r.MXC[xo].astype(F32)).astype(BF16)
        put(r.MXS, r.MXX, to_x, k.mxx)

    def mixed_end():
        take(r.MXC.at[x], k.mxc + x)
        take(r.MXX, k.mxx)
        r.mixed[...] = (
            r.H[...] + r.MX[x, c].astype(F32) + r.MXC[x].astype(F32) + r.MXX[...].astype(F32)
        ).astype(BF16)

    def attended_back():
        take(r.DB.at[co], k.db)
        db_all = r.DB[...].reshape(CS * TOK, DIM)
        rows = [r.WO[h, pl.ds(2 * c, 2)].reshape(HALF, HALF) for h in range(CS)]
        d_att = dot_tb(db_all[:, :HALF], rows[0]) + dot_tb(db_all[:, HALF:], rows[1])
        r.DO[...] = d_att.astype(BF16).reshape(CS, TOK, HALF)

    def grads_output():
        att_all = jnp.concatenate(
            [jnp.concatenate((r.ATT[0, q], r.ATT[1, q]), axis=1) for q in range(CS)], axis=0
        )
        db_cols = r.DB[:, :, pl.ds(pl.multiple_of(HALF * c, 128), HALF)].reshape(CS * TOK, HALF)
        chip_grad(PAIRS, dot_ta(att_all, db_cols))

    def table_start():
        r.DG[HEADS_HERE:, :] = jnp.zeros((8 - HEADS_HERE, SPAN), F32)
        onehot_back = (
            lax.broadcasted_iota(jnp.int32, (128, SPAN), 0)
            == r.BK[:, pl.ds(pl.multiple_of(LENGTH - TOK - TOK * s, 128), SPAN)]
        ).astype(F32)
        r.T1[...] = lax.dot_general(
            r.DG[...], onehot_back, (((1,), (1,)), ((), ())), precision=HIGHEST, preferred_element_type=F32
        )
        put(r.T1, r.TY, to_y, k.ty)

    def table_to_x():
        take(r.TY, k.ty)
        r.T2[...] = r.T1[...] + r.TY[...]
        put(r.T2, r.TX, to_x, k.tx)

    def table_to_z():
        take(r.TX, k.tx)
        r.T3[...] = r.T2[...] + r.TX[...]
        for who in to_z:
            put(r.T3, r.TZ.at[z], who, k.tz + z)
        r.TZ[z] = r.T3[...]

    def table_to_core():
        for zz in zord:
            take(r.TZ.at[zz], k.tz + zz)
        r.TO[c] = (r.TZ[0] + r.TZ[1]) + (r.TZ[2] + r.TZ[3])
        put(r.TO.at[c], r.TO.at[c], to_core, k.tc)

    def table_end():
        take(r.TO.at[co], k.tc)
        for q in range(CS):
            r.gtab[HEADS_HERE * q : HEADS_HERE * q + HEADS_HERE, :] = r.TO[q, :HEADS_HERE, :32]

    def down_end():
        r.gwd[...] = z_sum(r.GD[z, y], r.GDZ, k.rdz)

    def gate_to_x():
        total = z_sum(r.GG[z, :, y], r.GGZ, k.rgz)
        r.F4S[...] = total.astype(BF16)
        put(r.F4S.at[xo], r.F4X, to_x, k.f4x)

    def gate_to_core():
        take(r.F4X, k.f4x)
        r.F4S2[:, x] = r.F4S[x].astype(F32).reshape(CS, SHARD, 2 * QUARTER)
        r.F4S2[:, xo] = r.F4X[...].astype(F32).reshape(CS, SHARD, 2 * QUARTER)
        put(r.F4S2.at[co], r.F4.at[c], to_core, k.f4)
        r.F4[c] = r.F4S2[c]

    def gate_end():
        take(r.F4.at[co], k.f4)
        quarters = [r.F4[q % CS, q // CS] for q in range(BATCH_DEVICES)]
        gate_total = join_quarters([quarter[:, :QUARTER] for quarter in quarters])
        up_total = join_quarters([quarter[:, QUARTER:] for quarter in quarters])
        r.gwg[...] = gate_total * gain_f
        r.gwu[...] = up_total * gain_f
        r.ggf[...] = to_row(
            jnp.sum(
                gate_total * r.wg[...].astype(F32) + up_total * r.wu[...].astype(F32), axis=1, keepdims=True
            )
        )

    def token_end():
        e1 = z_sum(r.DN[c, z, x], r.DNZ, k.dnz).T
        n1_own, r1 = unit_rows(tok[...].astype(F32))
        r.tg[...] = (
            r.DH[...] + r1 * (e1 - n1_own * jnp.mean(e1 * n1_own, axis=1, keepdims=True))
        ).astype(BF16)

    def chips_to_core():
        put(r.FA.at[co], r.F2.at[c], to_core, k.f2)
        r.F2[c] = r.FA[c]

    def chips_end():
        take(r.F2.at[co], k.f2)
        gain_total = jnp.zeros((SHARD, 1), F32)
        for j, (w_ref, out_ref) in enumerate(((r.wq, r.gwq), (r.wk, r.gwk), (r.wv, r.gwv))):
            for h in range(CS):
                for p in range(PAIRS):
                    lanes = slice(HALF * h + 128 * p, HALF * h + 128 * p + 128)
                    grad = r.F2[h, :, HALF * p + 128 * j : HALF * p + 128 * j + 128]
                    gain_total = gain_total + jnp.sum(
                        grad * w_ref[:, lanes].astype(F32), axis=1, keepdims=True
                    )
                    out_ref[:, lanes] = grad * gain_a
        r.gga[...] = to_row(gain_total)
        for h in range(CS):
            r.gwo[:, HALF * h : HALF * h + HALF] = r.F2[h, :, 3 * HALF :]

    grads_down()
    grads_gate()
    mixed_send()
    hidden_back()
    down_from_y(1)
    attended_back()
    down_from_y(0)
    grads_output()
    attention_pair_back(2)
    chip_step1(PAIRS)
    zeros()
    gate_from_y(0)
    gate_from_y(1)
    down_chain()
    attention_pair_back(0)
    gate_from_y(2)
    down_from_y(2)
    attention_pair_back(1)
    token_exchange(far_first[3])
    token_exchange(far_first[0])
    table_start()
    chip_step1(2)
    chip_step2(PAIRS)
    chip_step1(0)
    gate_chain()
    token_to_x(far_first[0])
    token_exchange(far_first[1])
    token_exchange(far_first[2])
    table_to_x()
    chip_step2(2)
    chip_chain(PAIRS)
    token_to_x(far_first[1])
    chip_step2(0)
    chip_step1(1)
    down_from_y(3)
    gate_from_y(3)
    chip_step2(1)
    mixed_end()
    token_to_z(0)
    down_end()
    chip_chain(2)
    chip_chain(0)
    chip_end(PAIRS)
    table_to_z()
    token_to_x(far_first[2])
    gate_to_x()
    token_to_z(1)
    token_to_x(far_first[3])
    chip_chain(1)
    chip_end(0)
    token_to_z(2)
    chip_end(2)
    token_chain()
    gate_to_core()
    chip_end(1)
    table_to_core()
    chips_to_core()
    gate_end()
    table_end()
    token_to_z(3)
    chips_end()
    token_end()
    for copy, when in sent:
        if when is None:
            copy.wait_send()
        else:
            pl.when(when)(copy.wait_send)


def finish_kernel(*refs):
    count = len(refs) // 2
    for src, dst in zip(refs[:count], refs[count:]):
        dst[...] = src[...]


def fused_device(
    tokens, segments, buckets, gain_attn, w_query, w_key, w_value, w_output,
    gain_ffn, w_gate, w_up, w_down, bucket_bias_matrix, cotangent,
):
    operands = (
        tokens.reshape(TOK, DIM),
        cotangent.reshape(TOK, DIM),
        segments.reshape(1, LENGTH),
        buckets.reshape(1, 2 * LENGTH - 1),
        bucket_bias_matrix.T,
        gain_attn.reshape(1, SHARD),
        gain_ffn.reshape(1, SHARD),
        w_query, w_key, w_value, w_output, w_gate, w_up, w_down,
    )
    out_shape = [jax.ShapeDtypeStruct(shape, dtype) for shape, dtype in OUTPUTS.values()]
    in_vmem = pl.BlockSpec(memory_space=pltpu.VMEM)
    outs = pl.pallas_call(
        layer_kernel,
        out_shape=out_shape,
        in_specs=[in_vmem] * len(operands),
        out_specs=[in_vmem] * len(out_shape),
        scratch_shapes=[pltpu.VMEM(shape, dtype) for shape, dtype in SCRATCH.values()]
        + [pltpu.SemaphoreType.DMA((SEND_COUNT,)), pltpu.SemaphoreType.DMA((RECV_COUNT,))],
        compiler_params=pltpu.CompilerParams(
            collective_id=0, has_side_effects=True, vmem_limit_bytes=63 * 2**20
        ),
        name="layer",
    )(*operands)
    outs = pl.pallas_call(
        finish_kernel,
        out_shape=out_shape,
        in_specs=[in_vmem] * len(out_shape),
        out_specs=[in_vmem] * len(out_shape),
        name="finish",
    )(*outs)
    mixed, tokens_grad, gga, gwq, gwk, gwv, gwo, ggf, gwg, gwu, gwd, table_grad = outs
    return (
        mixed.reshape(tokens.shape), tokens_grad.reshape(tokens.shape), gga.reshape(SHARD),
        gwq, gwk, gwv, gwo, ggf.reshape(SHARD), gwg, gwu, gwd, table_grad.T,
    )


def fits_fused(mesh):
    return mesh.shape["seq"] == SEQ_DEVICES and mesh.shape["batch"] == BATCH_DEVICES


def solution(mesh):
    return jax.shard_map(
        fused_device if fits_fused(mesh) else on_device,
        mesh=mesh,
        in_specs=(
            P("seq", "batch", None),
            P(None, "batch"),
            P(),
            P(("seq", "batch")),
            P(("seq", "batch"), None),
            P(("seq", "batch"), None),
            P(("seq", "batch"), None),
            P(("seq", "batch"), None),
            P(("seq", "batch")),
            P(("seq", "batch"), None),
            P(("seq", "batch"), None),
            P(("seq", "batch"), None),
            P(),
            P("seq", "batch", None),
        ),
        out_specs=(
            P("seq", "batch", None),
            P("seq", "batch", None),
            P(("seq", "batch")),
            P(("seq", "batch"), None),
            P(("seq", "batch"), None),
            P(("seq", "batch"), None),
            P(("seq", "batch"), None),
            P(("seq", "batch")),
            P(("seq", "batch"), None),
            P(("seq", "batch"), None),
            P(("seq", "batch"), None),
            P(),
        ),
        check_vma=False,
    )
```

```python
from functools import partial
import math
from types import SimpleNamespace

import jax
import jax.numpy as jnp
from jax import lax
from jax.experimental import pallas as pl
from jax.experimental.pallas import tpu as pltpu
from jax.sharding import PartitionSpec as P

EPSILON = 1e-06
NEGATIVE = -1e30
HIGHEST = lax.Precision.HIGHEST


def normalize(hidden_state, scale_vec):
    return (
        hidden_state
        * lax.rsqrt(jnp.mean(hidden_state * hidden_state, axis=-1, keepdims=True) + EPSILON)
        * scale_vec
    )


def gelu_tanh(gate_vals):
    return jax.nn.gelu(gate_vals, approximate=True)


def project(left_side, weight):
    return jnp.einsum("tsk,kn->tsn", left_side, weight, preferred_element_type=jnp.float32)


def project_back(grad_rows, weight):
    return jnp.einsum("tsn,kn->tsk", grad_rows, weight, preferred_element_type=jnp.float32)


def weight_grad(left_side, grad_rows):
    return jnp.einsum("tsk,tsn->kn", left_side, grad_rows, preferred_element_type=jnp.float32)


def position_bias(
    buckets, bucket_bias_matrix, query_start, key_start, query_rows, key_rows, seq_length
):
    span = query_rows + key_rows - 1
    head_count = bucket_bias_matrix.shape[1]
    first = key_start - query_start + seq_length - query_rows
    chosen = lax.dynamic_slice_in_dim(buckets, first, span, 0)
    onehot = (
        chosen[:, None] == jnp.arange(bucket_bias_matrix.shape[0], dtype=jnp.int32)[None, :]
    ).astype(jnp.float32)
    per_offset = jnp.dot(onehot, bucket_bias_matrix.astype(jnp.float32), precision=HIGHEST)
    padded = jnp.concatenate((per_offset.T, jnp.zeros((head_count, 1), jnp.float32)), axis=1)
    tiled = jnp.broadcast_to(padded[:, None, :], (head_count, query_rows, span + 1)).reshape(
        head_count, query_rows * (span + 1)
    )
    skewed = tiled[:, : query_rows * span].reshape(head_count, query_rows, span)
    return (onehot, skewed[:, :, query_rows - 1 : query_rows - 1 + key_rows])


def table_term(onehot, score_gradient):
    summed = jnp.sum(score_gradient.astype(jnp.float32), axis=0)
    head_count, query_rows, key_rows = summed.shape
    span = query_rows + key_rows - 1
    placed = jnp.pad(summed, ((0, 0), (0, 0), (query_rows - 1, 0))).reshape(
        head_count, query_rows * span
    )
    placed = jnp.pad(placed, ((0, 0), (0, query_rows)))
    diagonal_sums = jnp.sum(placed.reshape(head_count, query_rows, span + 1), axis=1)[:, :span]
    return jnp.dot(onehot.T, diagonal_sums.T, precision=HIGHEST)


def pair_scores(table_set, query_block, query_segs, query_start, key_block, key_segs, key_start):
    buckets, bucket_bias_matrix, seq_length = table_set
    onehot, bias_contributions = position_bias(
        buckets,
        bucket_bias_matrix,
        query_start,
        key_start,
        query_block.shape[0],
        key_block.shape[0],
        seq_length,
    )
    scores = (
        jnp.einsum("qshd,kshd->shqk", query_block, key_block, preferred_element_type=jnp.float32)
        + bias_contributions[None]
    )
    allowed = (query_segs.T[:, :, None] == key_segs.T[:, None, :])[:, None]
    return (onehot, scores, allowed)


def pair_grads(
    table_set,
    query_block,
    query_segs,
    query_start,
    dout_block,
    log_sums,
    deltas,
    key_block,
    value_block,
    key_segs,
    key_start,
):
    onehot, scores, allowed = pair_scores(
        table_set, query_block, query_segs, query_start, key_block, key_segs, key_start
    )
    probabilities = jnp.where(allowed, jnp.exp(scores - log_sums[..., None]), 0.0)
    dprobs = jnp.einsum(
        "qshd,kshd->shqk", dout_block, value_block, preferred_element_type=jnp.float32
    )
    score_gradient = (probabilities * (dprobs - deltas[..., None])).astype(jnp.bfloat16)
    return (onehot, probabilities, score_gradient)


def attend_block(setting, carried, blocks, key_start):
    table_set, segments, query_heads, query_segs, query_start = setting
    running_max, running_sum, accum = carried
    key_block, value_block = blocks
    key_segs = lax.dynamic_slice_in_dim(segments, key_start, key_block.shape[0], 0)
    _, scores, allowed = pair_scores(
        table_set, query_heads, query_segs, query_start, key_block, key_segs, key_start
    )
    new_max = jnp.maximum(running_max, jnp.max(jnp.where(allowed, scores, NEGATIVE), axis=-1))
    weights_raw = jnp.where(allowed, jnp.exp(scores - new_max[..., None]), 0.0)
    factor = jnp.exp(running_max - new_max)
    running_sum = running_sum * factor + jnp.sum(weights_raw, axis=-1)
    accum = accum * jnp.transpose(factor, (2, 0, 1))[..., None] + jnp.einsum(
        "shqk,kshd->qshd",
        weights_raw.astype(jnp.bfloat16),
        value_block,
        preferred_element_type=jnp.float32,
    )
    return (new_max, running_sum, accum)


def merged_block(setting, extras, carried, scan_item):
    table_set, segments, query_heads, query_segs, query_start = setting
    dout_heads, log_sums, deltas = extras
    dquery, dtable = carried
    key_start, key_block, value_block = scan_item
    key_rows = key_block.shape[0]
    seq_count = key_block.shape[1]
    key_segs = lax.dynamic_slice_in_dim(segments, key_start, key_rows, 0)
    onehot, probabilities, score_gradient = pair_grads(
        table_set,
        query_heads,
        query_segs,
        query_start,
        dout_heads,
        log_sums,
        deltas,
        key_block,
        value_block,
        key_segs,
        key_start,
    )
    dquery = dquery + jnp.einsum(
        "shqk,kshd->qshd", score_gradient, key_block, preferred_element_type=jnp.float32
    )
    dtable = dtable + table_term(onehot, score_gradient)
    key_gradient = jnp.einsum(
        "shqk,qshd->kshd", score_gradient, query_heads, preferred_element_type=jnp.float32
    )
    dvalue = jnp.einsum(
        "shqk,qshd->kshd",
        probabilities.astype(jnp.bfloat16),
        dout_heads,
        preferred_element_type=jnp.float32,
    )
    joined = jnp.concatenate(
        (key_gradient.reshape(key_rows, seq_count, -1), dvalue.reshape(key_rows, seq_count, -1)),
        axis=2,
    )
    return ((dquery, dtable), joined)


def fold_blocks(step_fn, carried, pieces):
    piece_rows = pieces[0].shape[0]
    block_rows = math.gcd(piece_rows, 512)
    block_count = piece_rows // block_rows
    stacked = tuple(
        (piece.reshape((block_count, block_rows) + piece.shape[1:]) for piece in pieces)
    )

    def advance(state_now, scan_item):
        block_index, blocks = scan_item
        return (step_fn(state_now, blocks, block_index * block_rows), None)

    result, _ = lax.scan(advance, carried, (jnp.arange(block_count, dtype=jnp.int32), stacked))
    return result


def on_device(
    tokens,
    segments,
    buckets,
    gain_attn,
    w_query,
    w_key,
    w_value,
    w_output,
    gain_ffn,
    w_gate,
    w_up,
    w_down,
    bucket_bias_matrix,
    cotangent,
):
    tok_rows, seq_count, _ = tokens.shape
    head_count = bucket_bias_matrix.shape[1]
    inner_width = w_query.shape[1]
    head_width = inner_width // head_count
    head_shape = (tok_rows, seq_count, head_count, head_width)
    seq_length = (buckets.shape[0] + 1) // 2
    query_start = lax.axis_index("seq") * tok_rows
    (
        full_gain_attn,
        full_query,
        full_key,
        full_value,
        full_output,
        full_gain_ffn,
        full_gate,
        full_up,
        full_down,
    ) = (
        lax.all_gather(gain_attn, ("seq", "batch"), axis=0, tiled=True),
        lax.all_gather(w_query, ("seq", "batch"), axis=0, tiled=True),
        lax.all_gather(w_key, ("seq", "batch"), axis=0, tiled=True),
        lax.all_gather(w_value, ("seq", "batch"), axis=0, tiled=True),
        lax.all_gather(w_output, ("seq", "batch"), axis=0, tiled=True),
        lax.all_gather(gain_ffn, ("seq", "batch"), axis=0, tiled=True),
        lax.all_gather(w_gate, ("seq", "batch"), axis=0, tiled=True),
        lax.all_gather(w_up, ("seq", "batch"), axis=0, tiled=True),
        lax.all_gather(w_down, ("seq", "batch"), axis=0, tiled=True),
    )
    tokens_full = tokens.astype(jnp.float32)
    normed1 = normalize(tokens_full, full_gain_attn.astype(jnp.float32)).astype(jnp.bfloat16)
    query_heads = project(normed1, full_query).astype(jnp.bfloat16).reshape(head_shape)
    key_heads = project(normed1, full_key).astype(jnp.bfloat16).reshape(head_shape)
    value_heads = project(normed1, full_value).astype(jnp.bfloat16).reshape(head_shape)
    query_segs = lax.dynamic_slice_in_dim(segments, query_start, tok_rows, 0)
    table_set = (buckets, bucket_bias_matrix, seq_length)
    setting = (table_set, segments, query_heads, query_segs, query_start)
    start_state = (
        jnp.full((seq_count, head_count, tok_rows), NEGATIVE, jnp.float32),
        jnp.zeros((seq_count, head_count, tok_rows), jnp.float32),
        jnp.zeros(head_shape, jnp.float32),
    )
    step_forward = partial(attend_block, setting)
    running_max, running_sum, accum = fold_blocks(
        step_forward,
        start_state,
        (
            lax.all_gather(key_heads, "seq", axis=0, tiled=True),
            lax.all_gather(value_heads, "seq", axis=0, tiled=True),
        ),
    )
    attended_full = accum / jnp.transpose(running_sum, (2, 0, 1))[..., None]
    log_sums = running_max + jnp.log(running_sum)
    attended = attended_full.astype(jnp.bfloat16).reshape(tok_rows, seq_count, inner_width)
    hidden1 = tokens_full + project(attended, full_output)
    normed2 = normalize(hidden1, full_gain_ffn.astype(jnp.float32)).astype(jnp.bfloat16)
    gate = project(normed2, full_gate)
    up_val = project(normed2, full_up)
    gelu_out, gelu_pull = jax.vjp(gelu_tanh, gate)
    activated = (gelu_out * up_val).astype(jnp.bfloat16)
    mixed = (hidden1 + project(activated, full_down)).astype(jnp.bfloat16)
    (
        full_gain_attn,
        full_query,
        full_key,
        full_value,
        full_output,
        full_gain_ffn,
        full_gate,
        full_up,
        full_down,
    ) = (
        lax.all_gather(gain_attn, ("seq", "batch"), axis=0, tiled=True),
        lax.all_gather(w_query, ("seq", "batch"), axis=0, tiled=True),
        lax.all_gather(w_key, ("seq", "batch"), axis=0, tiled=True),
        lax.all_gather(w_value, ("seq", "batch"), axis=0, tiled=True),
        lax.all_gather(w_output, ("seq", "batch"), axis=0, tiled=True),
        lax.all_gather(gain_ffn, ("seq", "batch"), axis=0, tiled=True),
        lax.all_gather(w_gate, ("seq", "batch"), axis=0, tiled=True),
        lax.all_gather(w_up, ("seq", "batch"), axis=0, tiled=True),
        lax.all_gather(w_down, ("seq", "batch"), axis=0, tiled=True),
    )
    grad_down = weight_grad(activated, cotangent)
    d_activated = project_back(cotangent, full_down)
    d_gate = gelu_pull(d_activated * up_val)[0].astype(jnp.bfloat16)
    d_up = (gelu_out * d_activated).astype(jnp.bfloat16)
    grad_gate = weight_grad(normed2, d_gate)
    grad_up = weight_grad(normed2, d_up)
    d_normed2 = project_back(d_gate, full_gate) + project_back(d_up, full_up)
    _, norm_pull2 = jax.vjp(normalize, hidden1, full_gain_ffn.astype(jnp.float32))
    d_hidden_part, grad_gain_ffn = norm_pull2(d_normed2)
    d_hidden1 = cotangent.astype(jnp.float32) + d_hidden_part
    d_branch = d_hidden1.astype(jnp.bfloat16)
    grad_output = weight_grad(attended, d_branch)
    dout_heads = project_back(d_branch, full_output).astype(jnp.bfloat16).reshape(head_shape)
    deltas = jnp.transpose(
        jnp.sum(dout_heads.astype(jnp.float32) * attended_full, axis=-1), (1, 2, 0)
    )
    extras = (dout_heads, log_sums, deltas)
    keys_all, values_all = (
        lax.all_gather(key_heads, "seq", axis=0, tiled=True),
        lax.all_gather(value_heads, "seq", axis=0, tiled=True),
    )
    block_rows = math.gcd(seq_length, 512)
    block_count = seq_length // block_rows
    stacked_keys = keys_all.reshape((block_count, block_rows) + keys_all.shape[1:])
    stacked_values = values_all.reshape((block_count, block_rows) + values_all.shape[1:])
    block_starts = jnp.arange(block_count, dtype=jnp.int32) * block_rows
    query_init = (
        jnp.zeros(head_shape, jnp.float32),
        jnp.zeros(bucket_bias_matrix.shape, jnp.float32),
    )
    (dquery, dtable), joined_all = lax.scan(
        partial(merged_block, setting, extras),
        query_init,
        (block_starts, stacked_keys, stacked_values),
    )
    every_key_contribution = joined_all.reshape(seq_length, seq_count, 2 * inner_width)
    key_sums = lax.psum_scatter(every_key_contribution, "seq", scatter_dimension=0, tiled=True)
    dkey_rows = key_sums[:, :, :inner_width].astype(jnp.bfloat16)
    dvalue_rows = key_sums[:, :, inner_width:].astype(jnp.bfloat16)
    dquery_rows = dquery.reshape(tok_rows, seq_count, inner_width).astype(jnp.bfloat16)
    grad_query = weight_grad(normed1, dquery_rows)
    grad_key = weight_grad(normed1, dkey_rows)
    grad_value = weight_grad(normed1, dvalue_rows)
    d_normed1 = (
        project_back(dquery_rows, full_query)
        + project_back(dkey_rows, full_key)
        + project_back(dvalue_rows, full_value)
    )
    _, norm_pull1 = jax.vjp(normalize, tokens_full, full_gain_attn.astype(jnp.float32))
    d_input_part, grad_gain_attn = norm_pull1(d_normed1)
    tokens_grad = (d_hidden1 + d_input_part).astype(jnp.bfloat16)
    owned = (
        lax.psum_scatter(grad_gain_attn, ("seq", "batch"), scatter_dimension=0, tiled=True),
        lax.psum_scatter(grad_query, ("seq", "batch"), scatter_dimension=0, tiled=True),
        lax.psum_scatter(grad_key, ("seq", "batch"), scatter_dimension=0, tiled=True),
        lax.psum_scatter(grad_value, ("seq", "batch"), scatter_dimension=0, tiled=True),
        lax.psum_scatter(grad_output, ("seq", "batch"), scatter_dimension=0, tiled=True),
        lax.psum_scatter(grad_gain_ffn, ("seq", "batch"), scatter_dimension=0, tiled=True),
        lax.psum_scatter(grad_gate, ("seq", "batch"), scatter_dimension=0, tiled=True),
        lax.psum_scatter(grad_up, ("seq", "batch"), scatter_dimension=0, tiled=True),
        lax.psum_scatter(grad_down, ("seq", "batch"), scatter_dimension=0, tiled=True),
    )
    table_total = lax.psum(dtable, ("seq", "batch"))
    return (
        mixed,
        tokens_grad,
        owned[0],
        owned[1],
        owned[2],
        owned[3],
        owned[4],
        owned[5],
        owned[6],
        owned[7],
        owned[8],
        table_total,
    )


BF16 = jnp.bfloat16
F32 = jnp.float32
MESH_IDS = pl.DeviceIdType.MESH

ZS, XS, YS, CS = 4, 2, 2, 2
SEQ_DEVICES = ZS * XS
BATCH_DEVICES = YS * CS
TOK = 128
LENGTH = SEQ_DEVICES * TOK
DIM = 768
HALF = DIM // CS
PAIRS = HALF // 128
SHARD = DIM // (SEQ_DEVICES * BATCH_DEVICES)
CHIP_ROWS = SHARD * CS
GROUP_ROWS = SHARD * BATCH_DEVICES
FF_ALL = 2048
QUARTER = FF_ALL // BATCH_DEVICES
DOWN_ROWS = FF_ALL // (SEQ_DEVICES * BATCH_DEVICES)
CHUNKS = PAIRS + 1
SPAN = LENGTH + TOK
HEADS_HERE = 2 * PAIRS


def dot(a, b):
    return lax.dot_general(a, b, (((1,), (0,)), ((), ())), preferred_element_type=F32)


def dot_tb(a, b):
    return lax.dot_general(a, b, (((1,), (1,)), ((), ())), preferred_element_type=F32)


def dot_ta(a, b):
    return lax.dot_general(a, b, (((0,), (0,)), ((), ())), preferred_element_type=F32)


def to_column(row):
    n = row.shape[1]
    eye = lax.broadcasted_iota(jnp.int32, (n, n), 0) == lax.broadcasted_iota(jnp.int32, (n, n), 1)
    return jnp.sum(jnp.where(eye, jnp.broadcast_to(row, (n, n)), 0.0), axis=1, keepdims=True)


def to_row(col):
    n = col.shape[0]
    eye = lax.broadcasted_iota(jnp.int32, (n, n), 0) == lax.broadcasted_iota(jnp.int32, (n, n), 1)
    return jnp.sum(jnp.where(eye, jnp.broadcast_to(col, (n, n)), 0.0), axis=0, keepdims=True)


def unit_rows(x):
    r = lax.rsqrt(jnp.mean(x * x, axis=1, keepdims=True) + EPSILON)
    return x * r, r


def stack_heads(pair):
    low = lax.broadcasted_iota(jnp.int32, pair.shape, 1) < 64
    return jnp.concatenate((jnp.where(low, pair, 0.0), jnp.where(low, 0.0, pair)), axis=0).astype(BF16)


def unstack_heads(stacked):
    rows = stacked.shape[0] // 2
    low = lax.broadcasted_iota(jnp.int32, (rows, 128), 1) < 64
    return jnp.where(low, stacked[:rows], stacked[rows:])


def split_quarters(whole):
    low = lax.broadcasted_iota(jnp.int32, (whole.shape[0], 128), 1) < 64
    parts = []
    for q in range(BATCH_DEVICES):
        cols = []
        for m in range(ZS):
            first = 4 * m + 2 * (q // 2)
            a = whole[:, 128 * first : 128 * first + 128]
            b = whole[:, 128 * (first + 1) : 128 * (first + 1) + 128]
            if q % 2 == 0:
                cols.append(jnp.where(low, a, pltpu.roll(b, 64, 1)))
            else:
                cols.append(jnp.where(low, pltpu.roll(a, 64, 1), b))
        parts.append(jnp.concatenate(cols, axis=1))
    return parts


def join_quarters(parts):
    low = lax.broadcasted_iota(jnp.int32, (parts[0].shape[0], 128), 1) < 64
    cols = []
    for block in range(FF_ALL // 128):
        m, xx, yy = block // 4, block // 2 % 2, block % 2
        lanes = slice(128 * m, 128 * m + 128)
        a, b = parts[2 * xx][:, lanes], parts[2 * xx + 1][:, lanes]
        if yy == 0:
            cols.append(jnp.where(low, a, pltpu.roll(b, 64, 1)))
        else:
            cols.append(jnp.where(low, pltpu.roll(a, 64, 1), b))
    return jnp.concatenate(cols, axis=1)


SCRATCH = dict(
    W_MINE=((CS, SHARD, 4 * HALF + 4 * QUARTER), F32),
    W_CORE=((CS, SHARD, 4 * HALF + 4 * QUARTER), F32),
    UB=((XS, CHIP_ROWS, 2 * QUARTER), BF16),
    WA=((PAIRS, ZS, XS, YS, CHIP_ROWS, HALF), BF16),
    WO=((CS, ZS, XS, YS, CHIP_ROWS, HALF), BF16),
    WG=((ZS, XS, YS, CHIP_ROWS, 2 * QUARTER), BF16),
    WD=((ZS, YS, DOWN_ROWS, DIM), BF16),
    X=((CS, ZS, XS, TOK, DIM), BF16),
    N1=((CS, ZS, XS, TOK, DIM), BF16),
    N1O=((CS, TOK, DIM), BF16),
    COT=((XS, CS, TOK, DIM), BF16),
    SEG=((CS, 8, LENGTH), F32),
    BK=((1, 2 * LENGTH), jnp.int32),
    PH=((2 * CS * PAIRS, SPAN), F32),
    BIAS=((PAIRS, 2 * TOK, LENGTH), F32),
    MASK=((CS, TOK, LENGTH), F32),
    KV=((PAIRS, CS, LENGTH, 256), BF16),
    QS=((PAIRS, CS, 2 * TOK, 128), BF16),
    PS=((PAIRS, CS, 2 * TOK, LENGTH), BF16),
    ATT=((CS, CS, TOK, HALF), BF16),
    H=((TOK, DIM), F32),
    N2=((XS, CS, TOK, DIM), BF16),
    ACT=((XS, 2 * TOK, QUARTER), BF16),
    DGU=((XS, 2 * TOK, 2 * QUARTER), BF16),
    MX=((XS, CS, TOK, DIM), BF16),
    MXC=((XS, TOK, DIM), BF16),
    MXS=((TOK, DIM), BF16),
    MXX=((TOK, DIM), BF16),
    E2=((XS, CS, TOK, DIM), BF16),
    E2C=((XS, TOK, DIM), BF16),
    E2S=((TOK, DIM), BF16),
    E2X=((TOK, DIM), BF16),
    GG=((ZS, XS, YS, CHIP_ROWS, 2 * QUARTER), BF16),
    GGY=((ZS, XS, CHIP_ROWS, 2 * QUARTER), BF16),
    GGZ=((ZS, XS, CHIP_ROWS, 2 * QUARTER), BF16),
    GGC=((XS, CHIP_ROWS, 2 * QUARTER), BF16),
    GD=((ZS, YS, DOWN_ROWS, DIM), BF16),
    GDY=((ZS, DOWN_ROWS, DIM), BF16),
    GDZ=((ZS, DOWN_ROWS, DIM), BF16),
    GDC=((DOWN_ROWS, DIM), BF16),
    F4S=((XS, CHIP_ROWS, 2 * QUARTER), BF16),
    F4X=((CHIP_ROWS, 2 * QUARTER), BF16),
    F4S2=((CS, XS, SHARD, 2 * QUARTER), F32),
    F4=((CS, XS, SHARD, 2 * QUARTER), F32),
    DH=((TOK, DIM), F32),
    DB=((CS, TOK, DIM), BF16),
    DO=((CS, TOK, HALF), BF16),
    DS=((PAIRS, CS, 2 * TOK, LENGTH), BF16),
    DQ=((PAIRS, CS, TOK, 128), BF16),
    DKV=((PAIRS, CS, 256, LENGTH), BF16),
    DG=((8, SPAN), F32),
    GA=((CHUNKS, ZS, XS, YS, CHIP_ROWS, HALF), BF16),
    GA1=((CHUNKS, ZS, 2, CHIP_ROWS, HALF), BF16),
    GA2=((CHUNKS, ZS, CHIP_ROWS, HALF), BF16),
    GAZ=((CHUNKS, ZS, CHIP_ROWS, HALF), BF16),
    GAC=((CHUNKS, CHIP_ROWS, HALF), BF16),
    FA=((CS, SHARD, 4 * HALF), F32),
    F2=((CS, SHARD, 4 * HALF), F32),
    DN=((CS, ZS, XS, DIM, TOK), BF16),
    DNC=((ZS, XS, DIM, TOK), BF16),
    DNX=((ZS, DIM, TOK), BF16),
    DNZ=((ZS, DIM, TOK), BF16),
    DNT=((DIM, TOK), BF16),
    T1=((8, 128), F32),
    TY=((8, 128), F32),
    T2=((8, 128), F32),
    TX=((8, 128), F32),
    T3=((8, 128), F32),
    TZ=((ZS, 8, 128), F32),
    TO=((CS, 8, 128), F32),
)
SEND_RING = 72
SLOTS = dict(
    segc=1, wc=1, u=1, xz=4, xx=4, xc=8, wz=4 * CHUNKS, wx=4 * CHUNKS, wy=4 * CHUNKS, wr=CHUNKS, woc=1,
    gz=8, gy=8, dz=4, dy=4, cotx=1, cotc=2, att=1, n2x=1, n2c=2, mxc=2, mxx=1, e2c=2, e2x=1,
    rdy=4, rdz=4, rdc=1, rgy=4, rgz=4, rgc=1, f4x=1, f4=1, db=1,
    ra1=CHUNKS, ra2=CHUNKS, raz=4 * CHUNKS, rac=CHUNKS, f2=1,
    dnc=4, dnx=4, dnz=4, dnt=1, ty=1, tx=1, tz=4, tc=1,
)
RECV_COUNT = sum(SLOTS.values())


def slot_bases():
    bases, used = {}, 0
    for name, count in SLOTS.items():
        bases[name] = used
        used += count
    return SimpleNamespace(**bases)


INPUTS = dict(
    tok=0, cot=0, seg=0, buckets=0, table=0, ga=0, gf=0, wq=0, wk=0, wv=0, wo=0, wg=0, wu=0, wd=0
)
OUTPUTS = dict(
    mixed=((TOK, DIM), BF16), tg=((TOK, DIM), BF16), gga=((1, SHARD), F32),
    gwq=((SHARD, DIM), F32), gwk=((SHARD, DIM), F32), gwv=((SHARD, DIM), F32), gwo=((SHARD, DIM), F32),
    ggf=((1, SHARD), F32), gwg=((SHARD, FF_ALL), F32), gwu=((SHARD, FF_ALL), F32),
    gwd=((DOWN_ROWS, DIM), F32), gtab=((2 * CS * PAIRS, 32), F32),
)


RELAY_TO_Y = (True, True, False, False)
HEAVY_X = (False, False, True, True)
FAR_DIRECT_CHIP = (False, False, False, False)
FAR_DIRECT_TOKEN = False
SPREAD_TOKEN = False
SPREAD_CHIP = (False, False, False, False)
SPREAD_GATE = False
SPREAD_DOWN = False


def layer_kernel(*refs):
    names = (*INPUTS, *OUTPUTS, *SCRATCH)
    r = SimpleNamespace(**dict(zip(names, refs[:-2], strict=True)))
    ssem, rsem = refs[-2:]
    k = slot_bases()
    s, b = lax.axis_index("seq"), lax.axis_index("batch")
    z, x = s // XS, s % XS
    y, c = b // CS, b % CS
    xo, yo, co = 1 - x, 1 - y, 1 - c
    side = z // 2
    m = z + side * (3 - 2 * z)
    at_end, beside = m == 0, m == 1
    zord = [near + side * (3 - 2 * near) for near in (1 - m, 2, 3)]

    def at(zz, xx, yy, cc):
        return (XS * zz + xx, CS * yy + cc)

    to_core, to_x, to_y = at(z, x, y, co), at(z, xo, y, c), at(z, x, yo, c)
    to_z = [at(zz, x, y, c) for zz in zord]

    barrier = pltpu.get_barrier_semaphore()
    friends = [to_core, to_x, to_y] + to_z
    for who in friends:
        pl.semaphore_signal(barrier, inc=1, device_id=who, device_id_type=MESH_IDS)

    sent = []

    def sent_wait(i):
        copy, when = sent[i]
        if when is None:
            copy.wait_send()
        else:
            pl.when(when)(copy.wait_send)

    def put(src, dst, who, slot, when=None):
        if len(sent) >= SEND_RING:
            sent_wait(len(sent) - SEND_RING)
        copy = pltpu.make_async_remote_copy(
            src_ref=src, dst_ref=dst, send_sem=ssem.at[len(sent) % SEND_RING], recv_sem=rsem.at[slot],
            device_id=who, device_id_type=MESH_IDS,
        )
        if when is None:
            copy.start()
        else:
            pl.when(when)(copy.start)
        sent.append((copy, when))

    def take(dst, slot, when=None):
        wait = pltpu.make_async_remote_copy(
            src_ref=dst, dst_ref=dst, send_sem=ssem.at[0], recv_sem=rsem.at[slot],
            device_id=to_core, device_id_type=MESH_IDS,
        ).wait_recv
        if when is None:
            wait()
        else:
            pl.when(when)(wait)

    def z_send(src, dst, slot, direct):
        put(src, dst, to_z[0], slot + z)
        put(src, dst, to_z[1], slot + z)
        put(src, dst, to_z[2], slot + z, when=None if direct else beside)

    def z_take(block, slot, i, direct):
        zz = zord[i]
        take(block(zz), slot + zz)
        if i == 2 and not direct:
            put(block(zz), block(zz), to_z[0], slot + zz, when=beside)

    def z_scatter(part, land, chain, slot, chain_slot, i):
        if i == 2 and chain is None:
            put(part(zord[2]), land.at[z], to_z[2], slot + z)
        elif i == 2:
            put(part(zord[2]), chain, to_z[0], chain_slot, when=at_end)
        else:
            put(part(zord[i]), land.at[z], to_z[i], slot + z)

    def z_chain(part, land, chain, slot, chain_slot):
        @pl.when(beside)
        def _():
            take(chain, chain_slot)
            mine = part(zord[2])
            mine[...] = (mine[...].astype(F32) + chain[...].astype(F32)).astype(BF16)

        put(part(zord[2]), land.at[z], to_z[2], slot + z, when=beside)

    def z_zero(land):
        @pl.when(at_end)
        def _():
            land[zord[2]] = jnp.zeros(land.shape[1:], land.dtype)

    def z_sum(own, land, slot, direct=False):
        take(land.at[zord[0]], slot + zord[0])
        take(land.at[zord[1]], slot + zord[1])
        take(land.at[zord[2]], slot + zord[2], when=None if direct else beside)
        total = own.astype(F32)
        for zz in zord:
            total = total + land[zz].astype(F32)
        return total

    gain_a = to_column(r.ga[...].astype(F32))
    gain_f = to_column(r.gf[...].astype(F32))
    tok = r.tok
    r.SEG[c] = jnp.broadcast_to(r.seg[...].astype(F32), (8, LENGTH))
    for h in range(CS):
        for p in range(PAIRS):
            for j, w_ref in enumerate((r.wq, r.wk, r.wv)):
                lanes = slice(HALF * h + 128 * p, HALF * h + 128 * p + 128)
                r.W_MINE[h, :, HALF * p + 128 * j : HALF * p + 128 * j + 128] = (
                    w_ref[:, lanes].astype(F32) * gain_a
                )
        r.W_MINE[h, :, 3 * HALF : 4 * HALF] = r.wo[:, HALF * h : HALF * h + HALF].astype(F32)
    for j, w_ref in enumerate((r.wg, r.wu)):
        for q, part in enumerate(split_quarters(w_ref[...].astype(F32) * gain_f)):
            first = 4 * HALF + 2 * QUARTER * (q // CS) + QUARTER * j
            r.W_MINE[q % CS, :, first : first + QUARTER] = part

    pl.semaphore_wait(barrier, len(friends))

    put(r.W_MINE.at[co], r.W_CORE.at[c], to_core, k.wc)
    put(tok, r.X.at[c, z, x], to_x, k.xx + z)
    put(r.SEG.at[c], r.SEG.at[c], to_core, k.segc)
    put(tok, r.X.at[c, z, x], to_core, k.xc + s)
    r.X[c, z, x] = tok[...]
    r.WD[z, y] = r.wd[...]
    r.W_CORE[c] = r.W_MINE[c]

    def weight(ch):
        return r.WA.at[ch] if ch < PAIRS else r.WO.at[c]

    def weight_start(ch):
        own = weight(ch).at[z, x, y]
        z_send(own, own, k.wz + 4 * ch, SPREAD_CHIP[ch])
        put(own, own, to_y, k.wy + 4 * ch + z)
        put(own, own, to_x, k.wx + 4 * ch + z)

    def norm_block(q, zz, xx, own=False):
        value = unit_rows(r.X[q, zz, xx].astype(F32))[0].astype(BF16)
        r.N1[q, zz, xx] = value
        if own:
            r.N1O[q] = value

    def token_from_z(i):
        z_take(lambda zz: r.X.at[c, zz, x], k.xz, i, SPREAD_TOKEN)
        zz = zord[i]
        put(r.X.at[c, zz, x], r.X.at[c, zz, x], to_x, k.xx + zz)
        put(r.X.at[c, zz, x], r.X.at[c, zz, x], to_core, k.xc + XS * zz + x)
        norm_block(c, zz, x)

    def token_from_x(zz):
        take(r.X.at[c, zz, xo], k.xx + zz)
        put(r.X.at[c, zz, xo], r.X.at[c, zz, xo], to_core, k.xc + XS * zz + xo)
        norm_block(c, zz, xo)

    def token_from_core(zz, xx):
        take(r.X.at[co, zz, xx], k.xc + XS * zz + xx)
        norm_block(co, zz, xx, own=zz is z and xx is x)

    def bias_lines():
        r.BK[...] = jnp.zeros(r.BK.shape, jnp.int32)
        r.BK[:, : 2 * LENGTH - 1] = r.buckets[...]
        onehot = (
            lax.broadcasted_iota(jnp.int32, (32, SPAN), 0)
            == r.BK[:, pl.ds(pl.multiple_of(LENGTH - TOK - TOK * s, 128), SPAN)]
        )
        r.PH[...] = dot(r.table[...], onehot.astype(BF16))

    def bias_pair(p):
        for hh in range(2):
            line = r.PH[pl.ds(HEADS_HERE * c + 2 * p + hh, 1), :]
            skewed = pltpu.roll(
                jnp.broadcast_to(line, (TOK, SPAN)), SPAN - TOK + 1, 1, stride=1, stride_axis=0
            )
            r.BIAS[p, TOK * hh : TOK * hh + TOK, :] = skewed[:, :LENGTH]

    def masks():
        take(r.SEG.at[co], k.segc)
        for q in range(CS):
            col = to_column(r.SEG[q, 0:1, pl.ds(pl.multiple_of(TOK * s, 128), TOK)])
            r.MASK[q] = jnp.where(col == r.SEG[q, 0:1, :], 0.0, NEGATIVE)

    def weight_from_z(ch, i):
        w = weight(ch)
        z_take(lambda zz: w.at[zz, x, y], k.wz + 4 * ch, i, SPREAD_CHIP[ch])
        arrived = w.at[zord[i], x, y]
        put(arrived, arrived, to_y, k.wy + 4 * ch + zord[i])
        put(arrived, arrived, to_x, k.wx + 4 * ch + zord[i])

    def weight_relay(ch):
        w = weight(ch)
        for zz in [z] + zord:
            if RELAY_TO_Y[ch]:
                take(w.at[zz, xo, y], k.wx + 4 * ch + zz)
            else:
                take(w.at[zz, x, yo], k.wy + 4 * ch + zz)
        if RELAY_TO_Y[ch]:
            put(w.at[:, xo, y], w.at[:, xo, y], to_y, k.wr + ch)
        else:
            put(w.at[:, x, yo], w.at[:, x, yo], to_x, k.wr + ch)

    def weight_end(ch):
        w = weight(ch)
        for zz in [z] + zord:
            if RELAY_TO_Y[ch]:
                take(w.at[zz, x, yo], k.wy + 4 * ch + zz)
            else:
                take(w.at[zz, xo, y], k.wx + 4 * ch + zz)
        take(w.at[:, xo, yo], k.wr + ch)

    def gate_send(xx):
        own = r.WG.at[z, xx, y]
        z_send(own, own, k.gz + 4 * xx, SPREAD_GATE)
        put(own, own, to_y, k.gy + 4 * xx + z)

    def gate_from_z(xx, i):
        z_take(lambda zz: r.WG.at[zz, xx, y], k.gz + 4 * xx, i, SPREAD_GATE)
        arrived = r.WG.at[zord[i], xx, y]
        put(arrived, arrived, to_y, k.gy + 4 * xx + zord[i])

    def down_from_z(i):
        z_take(lambda zz: r.WD.at[zz, y], k.dz, i, SPREAD_DOWN)
        put(r.WD.at[zord[i], y], r.WD.at[zord[i], y], to_y, k.dy + zord[i])

    def tokens_send():
        z_send(tok, r.X.at[c, z, x], k.xz, SPREAD_TOKEN)

    def down_send():
        put(r.wd, r.WD.at[z, y], to_y, k.dy + z)
        z_send(r.wd, r.WD.at[z, y], k.dz, SPREAD_DOWN)

    def shards():
        take(r.W_CORE.at[co], k.wc)
        shard = r.W_CORE[...].reshape(CHIP_ROWS, 4 * HALF + 4 * QUARTER).astype(BF16)
        for ch in range(PAIRS):
            r.WA[ch, z, x, y] = shard[:, HALF * ch : HALF * ch + HALF]
        r.WO[c, z, x, y] = shard[:, 3 * HALF : 4 * HALF]
        for xx in range(XS):
            first = 4 * HALF + 2 * QUARTER * xx
            r.UB[xx] = shard[:, first : first + 2 * QUARTER]
        r.WG[z, x, y] = r.UB[x]

    def gate_exchange():
        put(r.UB.at[xo], r.WG.at[z, x, y], to_x, k.u)

    def gate_other():
        take(r.WG.at[z, xo, y], k.u)
        gate_send(xo)

    def cot_send():
        put(r.cot, r.COT.at[x, c], to_core, k.cotc + 0)
        put(r.cot, r.COT.at[x, c], to_x, k.cotx)
        r.COT[x, c] = r.cot[...]

    def cot_from_x():
        take(r.COT.at[xo, c], k.cotx)
        put(r.COT.at[xo, c], r.COT.at[xo, c], to_core, k.cotc + 1)

    def output_send():
        put(r.WO.at[c], r.WO.at[c], to_core, k.woc)

    zall = [z] + zord

    def keys_values(q, zz):
        w = jnp.concatenate([r.WA[p].reshape(DIM, HALF)[:, 128:] for p in range(PAIRS)], axis=1)
        kv = dot(r.N1[q, zz].reshape(XS * TOK, DIM), w).astype(BF16)
        for p in range(PAIRS):
            r.KV[p, q, pl.ds(pl.multiple_of(XS * TOK * zz, 128), XS * TOK), :] = kv[:, 256 * p : 256 * p + 256]

    def queries(q):
        for p in range(PAIRS):
            r.QS[p, q] = stack_heads(dot(r.N1O[q], r.WA[p].reshape(DIM, HALF)[:, :128]))

    def attend(p, q):
        kv = r.KV.at[p, q]
        stacked = r.QS[p, q]
        mask = r.MASK[q]
        scores = dot_tb(stacked, kv[:, :128]) + r.BIAS[p] + jnp.concatenate((mask, mask), axis=0)
        weights = jnp.exp(scores - jnp.max(scores, axis=1, keepdims=True))
        probs = (weights * (1.0 / jnp.sum(weights, axis=1, keepdims=True))).astype(BF16)
        r.PS[p, q] = probs
        r.ATT[c, q, :, 128 * p : 128 * p + 128] = unstack_heads(dot(probs, kv[:, 128:])).astype(BF16)

    def attended_send():
        put(r.ATT.at[c], r.ATT.at[c], to_core, k.att)

    norm_block(c, z, x, own=True)
    tokens_send()
    cot_send()
    bias_lines()
    bias_pair(0)
    shards()
    weight_start(0)
    gate_exchange()
    weight_start(1)
    weight_start(2)
    gate_send(x)
    token_from_core(z, x)
    token_from_x(z)
    masks()
    token_from_z(0)
    token_from_core(z, xo)
    token_from_core(zord[0], x)
    cot_from_x()
    token_from_z(1)
    weight_from_z(1, 0)
    weight_from_z(0, 0)
    weight_start(PAIRS)
    bias_pair(2)
    gate_other()
    token_from_x(zord[0])
    gate_from_z(x, 0)
    weight_from_z(0, 1)
    token_from_core(zord[1], x)
    bias_pair(1)
    token_from_z(2)
    weight_from_z(2, 1)
    weight_from_z(0, 2)
    weight_from_z(2, 0)
    weight_from_z(1, 1)
    token_from_x(zord[1])
    weight_from_z(1, 2)
    weight_from_z(PAIRS, 0)
    down_send()
    weight_from_z(2, 2)
    token_from_core(zord[1], xo)
    weight_relay(0)
    weight_relay(2)
    weight_relay(1)
    token_from_x(zord[2])
    weight_from_z(PAIRS, 1)
    gate_from_z(xo, 0)
    weight_from_z(PAIRS, 2)
    token_from_core(zord[0], xo)
    down_from_z(0)
    gate_from_z(xo, 1)
    gate_from_z(x, 1)
    token_from_core(zord[2], x)
    weight_end(0)
    token_from_core(zord[2], xo)
    gate_from_z(x, 2)
    weight_end(2)
    weight_end(1)
    keys_values(co, zord[0])
    keys_values(c, zord[1])
    keys_values(co, z)
    keys_values(co, zord[2])
    keys_values(c, z)
    keys_values(co, zord[1])
    queries(1)
    keys_values(c, zord[0])
    queries(0)
    attend(0, co)
    down_from_z(1)
    weight_relay(PAIRS)
    keys_values(c, zord[2])
    attend(1, co)
    down_from_z(2)
    attend(0, c)
    attend(1, c)
    weight_end(PAIRS)
    output_send()
    attend(2, c)
    attend(2, co)
    attended_send()
    gate_from_z(xo, 2)
    take(r.WO.at[co], k.woc)
    take(r.ATT.at[co], k.att)

    att_own = jnp.concatenate((r.ATT[0, c], r.ATT[1, c]), axis=1)
    tokens_f = tok[...].astype(F32)
    r.H[...] = tokens_f + jnp.concatenate(
        (dot(att_own, r.WO[0].reshape(DIM, HALF)), dot(att_own, r.WO[1].reshape(DIM, HALF))), axis=1
    )
    r.N2[x, c] = unit_rows(r.H[...])[0].astype(BF16)
    put(r.N2.at[x, c], r.N2.at[x, c], to_core, k.n2c + 0)
    put(r.N2.at[x, c], r.N2.at[x, c], to_x, k.n2x)

    for zz in [z] + zord:
        for xx in range(XS):
            take(r.WG.at[zz, xx, yo], k.gy + 4 * xx + zz)
        take(r.WD.at[zz, yo], k.dy + zz)
    take(r.COT.at[x, co], k.cotc + 0)
    take(r.COT.at[xo, co], k.cotc + 1)
    take(r.N2.at[x, co], k.n2c + 0)

    def feed_forward(xx):
        w_gu = r.WG[...].reshape(DIM, 2 * QUARTER)
        w_d = r.WD[...].reshape(QUARTER, DIM)
        n2 = r.N2[xx].reshape(2 * TOK, DIM)
        g = r.COT[xx].reshape(2 * TOK, DIM)
        gate = dot(n2, w_gu[:, :QUARTER])
        up = dot(n2, w_gu[:, QUARTER:])
        d_act = dot_tb(g, w_d)
        square = gate * gate
        inner = math.sqrt(2 / math.pi) * gate * (1.0 + 0.044715 * square)
        tanh = jnp.tanh(inner)
        half_open = 0.5 * (1.0 + tanh)
        gelu = gate * half_open
        slope = half_open + 0.5 * gate * (1.0 - tanh * tanh) * (
            math.sqrt(2 / math.pi) * (1.0 + 3 * 0.044715 * square)
        )
        act = (gelu * up).astype(BF16)
        r.ACT[xx] = act
        d_gu = jnp.concatenate(
            ((slope * (up * d_act)).astype(BF16), (gelu * d_act).astype(BF16)), axis=1
        )
        r.DGU[xx] = d_gu
        r.E2[xx] = dot_tb(d_gu, w_gu).astype(BF16).reshape(CS, TOK, DIM)
        put(r.E2.at[xx, co], r.E2C.at[xx], to_core, k.e2c + xx)
        r.MX[xx] = dot(act, w_d).astype(BF16).reshape(CS, TOK, DIM)
        put(r.MX.at[xx, co], r.MXC.at[xx], to_core, k.mxc + xx)

    feed_forward(x)
    take(r.N2.at[xo, c], k.n2x)
    put(r.N2.at[xo, c], r.N2.at[xo, c], to_core, k.n2c + 1)
    take(r.N2.at[xo, co], k.n2c + 1)
    feed_forward(xo)
    far_first = [zord[2], zord[1], zord[0], z]

    def down_grad(zz):
        return r.GD.at[zz, y]

    def gate_grad(zz):
        return r.GG.at[zz, :, y]

    def grad_from_y(part, got, slot, scatter, i):
        zz = far_first[i]
        take(got.at[zz], slot + zz)
        mine = part(zz)
        mine[...] = (mine[...].astype(F32) + got[zz].astype(F32)).astype(BF16)
        if i < 3:
            z_scatter(part, *scatter, 2 - i)

    down_scatter = (r.GDZ, r.GDC, k.rdz, k.rdc)
    gate_scatter = (r.GGZ, r.GGC, k.rgz, k.rgc)

    def down_from_y(i):
        grad_from_y(down_grad, r.GDY, k.rdy, down_scatter, i)

    def gate_from_y(i):
        grad_from_y(gate_grad, r.GGY, k.rgy, gate_scatter, i)

    def down_chain():
        z_chain(down_grad, *down_scatter)

    def gate_chain():
        z_chain(gate_grad, *gate_scatter)

    def chip_grad(ch, value):
        r.GA[ch] = value.astype(BF16).reshape(ZS, XS, YS, CHIP_ROWS, HALF)
        if HEAVY_X[ch]:
            put(r.GA.at[ch, :, xo], r.GA1.at[ch], to_x, k.ra1 + ch)
        else:
            put(r.GA.at[ch, :, :, yo], r.GA1.at[ch], to_y, k.ra1 + ch)

    def chip_step1(ch):
        take(r.GA1.at[ch], k.ra1 + ch)
        if HEAVY_X[ch]:
            r.GA[ch, :, x] = (r.GA[ch, :, x].astype(F32) + r.GA1[ch].astype(F32)).astype(BF16)
            put(r.GA.at[ch, :, x, yo], r.GA2.at[ch], to_y, k.ra2 + ch)
        else:
            r.GA[ch, :, :, y] = (r.GA[ch, :, :, y].astype(F32) + r.GA1[ch].astype(F32)).astype(BF16)
            put(r.GA.at[ch, :, xo, y], r.GA2.at[ch], to_x, k.ra2 + ch)

    def chip_scatter(ch):
        chain = None if FAR_DIRECT_CHIP[ch] else r.GAC.at[ch]
        return (lambda zz: r.GA.at[ch, zz, x, y]), r.GAZ.at[ch], chain, k.raz + 4 * ch, k.rac + ch

    def chip_step2(ch):
        take(r.GA2.at[ch], k.ra2 + ch)
        r.GA[ch, :, x, y] = (r.GA[ch, :, x, y].astype(F32) + r.GA2[ch].astype(F32)).astype(BF16)
        for i in (2, 1, 0):
            z_scatter(*chip_scatter(ch), i)

    def chip_chain(ch):
        if not FAR_DIRECT_CHIP[ch]:
            z_chain(*chip_scatter(ch))

    def chip_end(ch):
        total = z_sum(r.GA[ch, z, x, y], r.GAZ.at[ch], k.raz + 4 * ch, FAR_DIRECT_CHIP[ch])
        r.FA[:, :, HALF * ch : HALF * ch + HALF] = total.reshape(CS, SHARD, HALF)

    reverse = (
        lax.broadcasted_iota(jnp.int32, (TOK, TOK), 0) + lax.broadcasted_iota(jnp.int32, (TOK, TOK), 1)
        == TOK - 1
    ).astype(BF16)
    reverse2 = jnp.concatenate((reverse, reverse), axis=1)

    def attend_back(p, q):
        d_out = stack_heads(r.DO[q, :, 128 * p : 128 * p + 128].astype(F32))
        kv = r.KV.at[p, q]
        probs = r.PS[p, q]
        weighted = probs.astype(F32) * dot_tb(d_out, kv[:, 128:])
        delta = jnp.sum(weighted, axis=1, keepdims=True)
        d_scores = (weighted - probs.astype(F32) * delta).astype(BF16)
        r.DS[p, q] = d_scores
        r.DQ[p, q] = unstack_heads(dot(d_scores, kv[:, :128])).astype(BF16)
        r.DKV[p, q, :128] = dot_ta(r.QS[p, q], d_scores).astype(BF16)
        r.DKV[p, q, 128:] = dot_ta(d_out, probs).astype(BF16)

    def grads_pair(p):
        kv_grad = dot(r.DKV[p, 0], r.N1[0].reshape(LENGTH, DIM)) + dot(
            r.DKV[p, 1], r.N1[1].reshape(LENGTH, DIM)
        )
        own_rows = r.N1O[...].reshape(CS * TOK, DIM)
        q_grad = dot_ta(r.DQ[p].reshape(CS * TOK, 128), own_rows)
        chip_grad(p, jnp.concatenate((q_grad, kv_grad), axis=0).astype(BF16).T)

    def grads_bias(p):
        for hh in range(2):
            both = r.DS[p, :, TOK * hh : TOK * hh + TOK, :].reshape(CS * TOK, LENGTH)
            padded = jnp.concatenate((dot(reverse2, both), jnp.zeros((TOK, TOK), F32)), axis=1)
            placed = pltpu.roll(padded, 0, 1, stride=1, stride_axis=0)
            r.DG[2 * p + hh : 2 * p + hh + 1, :] = jnp.sum(placed, axis=0, keepdims=True)

    w_kv = jnp.concatenate([r.WA[p].reshape(DIM, HALF)[:, 128:] for p in range(PAIRS)], axis=1)

    def token_grad(q, zz):
        lanes = pl.ds(pl.multiple_of(XS * TOK * zz, 128), XS * TOK)
        d_kv = r.DKV[:, q, :, lanes].reshape(PAIRS * 256, XS * TOK)
        out = dot(w_kv, d_kv)
        for xx in range(XS):
            r.DN[q, zz, xx] = out[:, TOK * xx : TOK * xx + TOK].astype(BF16)
        if zz is z:
            total = r.DN[q, z, x].astype(F32)
            for p in range(PAIRS):
                total = total + dot_tb(r.WA[p].reshape(DIM, HALF)[:, :128], r.DQ[p, q])
            r.DN[q, z, x] = total.astype(BF16)

    def token_exchange(zz):
        token_grad(co, zz)
        put(r.DN.at[co, zz], r.DNC.at[zz], to_core, k.dnc + zz)
        token_grad(c, zz)

    def token_to_x(zz):
        take(r.DNC.at[zz], k.dnc + zz)
        r.DN[c, zz] = (r.DN[c, zz].astype(F32) + r.DNC[zz].astype(F32)).astype(BF16)
        put(r.DN.at[c, zz, xo], r.DNX.at[zz], to_x, k.dnx + zz)

    def token_part(zz):
        return r.DN.at[c, zz, x]

    token_scatter = (r.DNZ, None if FAR_DIRECT_TOKEN else r.DNT, k.dnz, k.dnt)

    def token_chain():
        if not FAR_DIRECT_TOKEN:
            z_chain(token_part, *token_scatter)

    def token_to_z(i):
        zz = far_first[i]
        take(r.DNX.at[zz], k.dnx + zz)
        r.DN[c, zz, x] = (r.DN[c, zz, x].astype(F32) + r.DNX[zz].astype(F32)).astype(BF16)
        if i < 3:
            z_scatter(token_part, *token_scatter, 2 - i)

    def grads_down():
        cot_all = r.COT[...].reshape(4 * TOK, DIM)
        r.GD[...] = dot_ta(r.ACT[...].reshape(4 * TOK, QUARTER), cot_all).astype(BF16).reshape(
            ZS, YS, DOWN_ROWS, DIM
        )
        for zz in far_first:
            put(r.GD.at[zz, yo], r.GDY.at[zz], to_y, k.rdy + zz)

    def grads_gate():
        n2_all = r.N2[...].reshape(4 * TOK, DIM)
        d_gu_all = r.DGU[...].reshape(4 * TOK, 2 * QUARTER)
        r.GG[...] = dot_ta(n2_all, d_gu_all).astype(BF16).reshape(ZS, XS, YS, CHIP_ROWS, 2 * QUARTER)
        for zz in far_first:
            put(r.GG.at[zz, :, yo], r.GGY.at[zz], to_y, k.rgy + zz)

    def zeros():
        z_zero(r.GDZ)
        z_zero(r.GGZ)
        if not FAR_DIRECT_TOKEN:
            z_zero(r.DNZ)
        for ch in range(CHUNKS):
            if not FAR_DIRECT_CHIP[ch]:
                z_zero(r.GAZ.at[ch])

    def hidden_send():
        take(r.E2C.at[xo], k.e2c + xo)
        r.E2S[...] = (r.E2[xo, c].astype(F32) + r.E2C[xo].astype(F32)).astype(BF16)
        put(r.E2S, r.E2X, to_x, k.e2x)

    def hidden_back():
        take(r.E2C.at[x], k.e2c + x)
        take(r.E2X, k.e2x)
        e2 = r.E2[x, c].astype(F32) + r.E2C[x].astype(F32) + r.E2X[...].astype(F32)
        n2_own, r2 = unit_rows(r.H[...])
        r.DH[...] = r.cot[...].astype(F32) + r2 * (
            e2 - n2_own * jnp.mean(e2 * n2_own, axis=1, keepdims=True)
        )
        r.DB[c] = r.DH[...].astype(BF16)
        put(r.DB.at[c], r.DB.at[c], to_core, k.db)

    def mixed_send():
        take(r.MXC.at[xo], k.mxc + xo)
        r.MXS[...] = (r.MX[xo, c].astype(F32) + r.MXC[xo].astype(F32)).astype(BF16)
        put(r.MXS, r.MXX, to_x, k.mxx)

    def mixed_end():
        take(r.MXC.at[x], k.mxc + x)
        take(r.MXX, k.mxx)
        r.mixed[...] = (
            r.H[...] + r.MX[x, c].astype(F32) + r.MXC[x].astype(F32) + r.MXX[...].astype(F32)
        ).astype(BF16)

    def attended_back():
        take(r.DB.at[co], k.db)
        db_all = r.DB[...].reshape(CS * TOK, DIM)
        rows = [r.WO[h, pl.ds(2 * c, 2)].reshape(HALF, HALF) for h in range(CS)]
        d_att = dot_tb(db_all[:, :HALF], rows[0]) + dot_tb(db_all[:, HALF:], rows[1])
        r.DO[...] = d_att.astype(BF16).reshape(CS, TOK, HALF)

    def grads_output():
        att_all = jnp.concatenate(
            [jnp.concatenate((r.ATT[0, q], r.ATT[1, q]), axis=1) for q in range(CS)], axis=0
        )
        db_cols = r.DB[:, :, pl.ds(pl.multiple_of(HALF * c, 128), HALF)].reshape(CS * TOK, HALF)
        chip_grad(PAIRS, dot_ta(att_all, db_cols))

    def table_start():
        r.DG[HEADS_HERE:, :] = jnp.zeros((8 - HEADS_HERE, SPAN), F32)
        onehot_back = (
            lax.broadcasted_iota(jnp.int32, (128, SPAN), 0)
            == r.BK[:, pl.ds(pl.multiple_of(LENGTH - TOK - TOK * s, 128), SPAN)]
        ).astype(F32)
        r.T1[...] = lax.dot_general(
            r.DG[...], onehot_back, (((1,), (1,)), ((), ())), precision=HIGHEST, preferred_element_type=F32
        )
        put(r.T1, r.TY, to_y, k.ty)

    def table_to_x():
        take(r.TY, k.ty)
        r.T2[...] = r.T1[...] + r.TY[...]
        put(r.T2, r.TX, to_x, k.tx)

    def table_to_z():
        take(r.TX, k.tx)
        r.T3[...] = r.T2[...] + r.TX[...]
        for who in to_z:
            put(r.T3, r.TZ.at[z], who, k.tz + z)
        r.TZ[z] = r.T3[...]

    def table_to_core():
        for zz in zord:
            take(r.TZ.at[zz], k.tz + zz)
        r.TO[c] = (r.TZ[0] + r.TZ[1]) + (r.TZ[2] + r.TZ[3])
        put(r.TO.at[c], r.TO.at[c], to_core, k.tc)

    def table_end():
        take(r.TO.at[co], k.tc)
        for q in range(CS):
            r.gtab[HEADS_HERE * q : HEADS_HERE * q + HEADS_HERE, :] = r.TO[q, :HEADS_HERE, :32]

    def down_end():
        r.gwd[...] = z_sum(r.GD[z, y], r.GDZ, k.rdz)

    def gate_to_x():
        total = z_sum(r.GG[z, :, y], r.GGZ, k.rgz)
        r.F4S[...] = total.astype(BF16)
        put(r.F4S.at[xo], r.F4X, to_x, k.f4x)

    def gate_to_core():
        take(r.F4X, k.f4x)
        r.F4S2[:, x] = r.F4S[x].astype(F32).reshape(CS, SHARD, 2 * QUARTER)
        r.F4S2[:, xo] = r.F4X[...].astype(F32).reshape(CS, SHARD, 2 * QUARTER)
        put(r.F4S2.at[co], r.F4.at[c], to_core, k.f4)
        r.F4[c] = r.F4S2[c]

    def gate_end():
        take(r.F4.at[co], k.f4)
        quarters = [r.F4[q % CS, q // CS] for q in range(BATCH_DEVICES)]
        gate_total = join_quarters([quarter[:, :QUARTER] for quarter in quarters])
        up_total = join_quarters([quarter[:, QUARTER:] for quarter in quarters])
        r.gwg[...] = gate_total * gain_f
        r.gwu[...] = up_total * gain_f
        r.ggf[...] = to_row(
            jnp.sum(
                gate_total * r.wg[...].astype(F32) + up_total * r.wu[...].astype(F32), axis=1, keepdims=True
            )
        )

    def token_end():
        e1 = z_sum(r.DN[c, z, x], r.DNZ, k.dnz, FAR_DIRECT_TOKEN).T
        n1_own, r1 = unit_rows(tok[...].astype(F32))
        r.tg[...] = (
            r.DH[...] + r1 * (e1 - n1_own * jnp.mean(e1 * n1_own, axis=1, keepdims=True))
        ).astype(BF16)

    def chips_to_core():
        put(r.FA.at[co], r.F2.at[c], to_core, k.f2)
        r.F2[c] = r.FA[c]

    def chips_end():
        take(r.F2.at[co], k.f2)
        gain_total = jnp.zeros((SHARD, 1), F32)
        for j, (w_ref, out_ref) in enumerate(((r.wq, r.gwq), (r.wk, r.gwk), (r.wv, r.gwv))):
            for h in range(CS):
                for p in range(PAIRS):
                    lanes = slice(HALF * h + 128 * p, HALF * h + 128 * p + 128)
                    grad = r.F2[h, :, HALF * p + 128 * j : HALF * p + 128 * j + 128]
                    gain_total = gain_total + jnp.sum(
                        grad * w_ref[:, lanes].astype(F32), axis=1, keepdims=True
                    )
                    out_ref[:, lanes] = grad * gain_a
        r.gga[...] = to_row(gain_total)
        for h in range(CS):
            r.gwo[:, HALF * h : HALF * h + HALF] = r.F2[h, :, 3 * HALF :]

    grads_down()
    hidden_send()
    grads_gate()
    mixed_send()
    zeros()
    down_from_y(0)
    hidden_back()
    attended_back()
    grads_output()
    down_from_y(1)
    down_from_y(2)
    attend_back(2, 1)
    attend_back(1, 0)
    mixed_end()
    down_chain()
    attend_back(2, 0)
    grads_bias(2)
    attend_back(1, 1)
    grads_pair(2)
    gate_from_y(0)
    attend_back(0, 1)
    attend_back(0, 0)
    token_exchange(far_first[1])
    down_from_y(3)
    chip_step1(PAIRS)
    token_exchange(far_first[3])
    gate_from_y(1)
    down_end()
    token_exchange(far_first[2])
    grads_pair(1)
    token_to_x(far_first[1])
    gate_chain()
    grads_pair(0)
    token_exchange(far_first[0])
    chip_step1(2)
    gate_from_y(2)
    token_to_x(far_first[0])
    token_to_x(far_first[2])
    grads_bias(0)
    grads_bias(1)
    table_start()
    gate_from_y(3)
    token_to_z(1)
    token_to_z(0)
    token_to_x(far_first[3])
    chip_step2(PAIRS)
    token_to_z(2)
    chip_step1(1)
    gate_to_x()
    chip_chain(PAIRS)
    token_chain()
    token_to_z(3)
    chip_step1(0)
    chip_step2(1)
    gate_to_core()
    chip_chain(1)
    chip_step2(2)
    token_end()
    gate_end()
    chip_step2(0)
    chip_end(PAIRS)
    table_to_x()
    chip_chain(2)
    chip_chain(0)
    table_to_z()
    chip_end(1)
    chip_end(2)
    chip_end(0)
    chips_to_core()
    table_to_core()
    chips_end()
    table_end()
    for i in range(len(sent) - SEND_RING, len(sent)):
        sent_wait(i)


def finish_kernel(*refs):
    count = len(refs) // 2
    for src, dst in zip(refs[:count], refs[count:]):
        dst[...] = src[...]


def fused_device(
    tokens, segments, buckets, gain_attn, w_query, w_key, w_value, w_output,
    gain_ffn, w_gate, w_up, w_down, bucket_bias_matrix, cotangent,
):
    operands = (
        tokens.reshape(TOK, DIM),
        cotangent.reshape(TOK, DIM),
        segments.reshape(1, LENGTH),
        buckets.reshape(1, 2 * LENGTH - 1),
        bucket_bias_matrix.T,
        gain_attn.reshape(1, SHARD),
        gain_ffn.reshape(1, SHARD),
        w_query, w_key, w_value, w_output, w_gate, w_up, w_down,
    )
    out_shape = [jax.ShapeDtypeStruct(shape, dtype) for shape, dtype in OUTPUTS.values()]
    in_vmem = pl.BlockSpec(memory_space=pltpu.VMEM)
    outs = pl.pallas_call(
        layer_kernel,
        out_shape=out_shape,
        in_specs=[in_vmem] * len(operands),
        out_specs=[in_vmem] * len(out_shape),
        scratch_shapes=[pltpu.VMEM(shape, dtype) for shape, dtype in SCRATCH.values()]
        + [pltpu.SemaphoreType.DMA((SEND_RING,)), pltpu.SemaphoreType.DMA((RECV_COUNT,))],
        compiler_params=pltpu.CompilerParams(
            collective_id=0, has_side_effects=True, vmem_limit_bytes=63 * 2**20
        ),
        name="layer",
    )(*operands)
    outs = pl.pallas_call(
        finish_kernel,
        out_shape=out_shape,
        in_specs=[in_vmem] * len(out_shape),
        out_specs=[in_vmem] * len(out_shape),
        name="finish",
    )(*outs)
    mixed, tokens_grad, gga, gwq, gwk, gwv, gwo, ggf, gwg, gwu, gwd, table_grad = outs
    return (
        mixed.reshape(tokens.shape), tokens_grad.reshape(tokens.shape), gga.reshape(SHARD),
        gwq, gwk, gwv, gwo, ggf.reshape(SHARD), gwg, gwu, gwd, table_grad.T,
    )


def fits_fused(mesh):
    return mesh.shape["seq"] == SEQ_DEVICES and mesh.shape["batch"] == BATCH_DEVICES


def solution(mesh):
    return jax.shard_map(
        fused_device if fits_fused(mesh) else on_device,
        mesh=mesh,
        in_specs=(
            P("seq", "batch", None),
            P(None, "batch"),
            P(),
            P(("seq", "batch")),
            P(("seq", "batch"), None),
            P(("seq", "batch"), None),
            P(("seq", "batch"), None),
            P(("seq", "batch"), None),
            P(("seq", "batch")),
            P(("seq", "batch"), None),
            P(("seq", "batch"), None),
            P(("seq", "batch"), None),
            P(),
            P("seq", "batch", None),
        ),
        out_specs=(
            P("seq", "batch", None),
            P("seq", "batch", None),
            P(("seq", "batch")),
            P(("seq", "batch"), None),
            P(("seq", "batch"), None),
            P(("seq", "batch"), None),
            P(("seq", "batch"), None),
            P(("seq", "batch")),
            P(("seq", "batch"), None),
            P(("seq", "batch"), None),
            P(("seq", "batch"), None),
            P(),
        ),
        check_vma=False,
    )
```

```python
from functools import partial
import math
from types import SimpleNamespace

import jax
import jax.numpy as jnp
from jax import lax
from jax.experimental import pallas as pl
from jax.experimental.pallas import tpu as pltpu
from jax.sharding import PartitionSpec as P

EPSILON = 1e-06
NEGATIVE = -1e30
HIGHEST = lax.Precision.HIGHEST


def normalize(hidden_state, scale_vec):
    return (
        hidden_state
        * lax.rsqrt(jnp.mean(hidden_state * hidden_state, axis=-1, keepdims=True) + EPSILON)
        * scale_vec
    )


def gelu_tanh(gate_vals):
    return jax.nn.gelu(gate_vals, approximate=True)


def project(left_side, weight):
    return jnp.einsum("tsk,kn->tsn", left_side, weight, preferred_element_type=jnp.float32)


def project_back(grad_rows, weight):
    return jnp.einsum("tsn,kn->tsk", grad_rows, weight, preferred_element_type=jnp.float32)


def weight_grad(left_side, grad_rows):
    return jnp.einsum("tsk,tsn->kn", left_side, grad_rows, preferred_element_type=jnp.float32)


def position_bias(
    buckets, bucket_bias_matrix, query_start, key_start, query_rows, key_rows, seq_length
):
    span = query_rows + key_rows - 1
    head_count = bucket_bias_matrix.shape[1]
    first = key_start - query_start + seq_length - query_rows
    chosen = lax.dynamic_slice_in_dim(buckets, first, span, 0)
    onehot = (
        chosen[:, None] == jnp.arange(bucket_bias_matrix.shape[0], dtype=jnp.int32)[None, :]
    ).astype(jnp.float32)
    per_offset = jnp.dot(onehot, bucket_bias_matrix.astype(jnp.float32), precision=HIGHEST)
    padded = jnp.concatenate((per_offset.T, jnp.zeros((head_count, 1), jnp.float32)), axis=1)
    tiled = jnp.broadcast_to(padded[:, None, :], (head_count, query_rows, span + 1)).reshape(
        head_count, query_rows * (span + 1)
    )
    skewed = tiled[:, : query_rows * span].reshape(head_count, query_rows, span)
    return (onehot, skewed[:, :, query_rows - 1 : query_rows - 1 + key_rows])


def table_term(onehot, score_gradient):
    summed = jnp.sum(score_gradient.astype(jnp.float32), axis=0)
    head_count, query_rows, key_rows = summed.shape
    span = query_rows + key_rows - 1
    placed = jnp.pad(summed, ((0, 0), (0, 0), (query_rows - 1, 0))).reshape(
        head_count, query_rows * span
    )
    placed = jnp.pad(placed, ((0, 0), (0, query_rows)))
    diagonal_sums = jnp.sum(placed.reshape(head_count, query_rows, span + 1), axis=1)[:, :span]
    return jnp.dot(onehot.T, diagonal_sums.T, precision=HIGHEST)


def pair_scores(table_set, query_block, query_segs, query_start, key_block, key_segs, key_start):
    buckets, bucket_bias_matrix, seq_length = table_set
    onehot, bias_contributions = position_bias(
        buckets,
        bucket_bias_matrix,
        query_start,
        key_start,
        query_block.shape[0],
        key_block.shape[0],
        seq_length,
    )
    scores = (
        jnp.einsum("qshd,kshd->shqk", query_block, key_block, preferred_element_type=jnp.float32)
        + bias_contributions[None]
    )
    allowed = (query_segs.T[:, :, None] == key_segs.T[:, None, :])[:, None]
    return (onehot, scores, allowed)


def pair_grads(
    table_set,
    query_block,
    query_segs,
    query_start,
    dout_block,
    log_sums,
    deltas,
    key_block,
    value_block,
    key_segs,
    key_start,
):
    onehot, scores, allowed = pair_scores(
        table_set, query_block, query_segs, query_start, key_block, key_segs, key_start
    )
    probabilities = jnp.where(allowed, jnp.exp(scores - log_sums[..., None]), 0.0)
    dprobs = jnp.einsum(
        "qshd,kshd->shqk", dout_block, value_block, preferred_element_type=jnp.float32
    )
    score_gradient = (probabilities * (dprobs - deltas[..., None])).astype(jnp.bfloat16)
    return (onehot, probabilities, score_gradient)


def attend_block(setting, carried, blocks, key_start):
    table_set, segments, query_heads, query_segs, query_start = setting
    running_max, running_sum, accum = carried
    key_block, value_block = blocks
    key_segs = lax.dynamic_slice_in_dim(segments, key_start, key_block.shape[0], 0)
    _, scores, allowed = pair_scores(
        table_set, query_heads, query_segs, query_start, key_block, key_segs, key_start
    )
    new_max = jnp.maximum(running_max, jnp.max(jnp.where(allowed, scores, NEGATIVE), axis=-1))
    weights_raw = jnp.where(allowed, jnp.exp(scores - new_max[..., None]), 0.0)
    factor = jnp.exp(running_max - new_max)
    running_sum = running_sum * factor + jnp.sum(weights_raw, axis=-1)
    accum = accum * jnp.transpose(factor, (2, 0, 1))[..., None] + jnp.einsum(
        "shqk,kshd->qshd",
        weights_raw.astype(jnp.bfloat16),
        value_block,
        preferred_element_type=jnp.float32,
    )
    return (new_max, running_sum, accum)


def merged_block(setting, extras, carried, scan_item):
    table_set, segments, query_heads, query_segs, query_start = setting
    dout_heads, log_sums, deltas = extras
    dquery, dtable = carried
    key_start, key_block, value_block = scan_item
    key_rows = key_block.shape[0]
    seq_count = key_block.shape[1]
    key_segs = lax.dynamic_slice_in_dim(segments, key_start, key_rows, 0)
    onehot, probabilities, score_gradient = pair_grads(
        table_set,
        query_heads,
        query_segs,
        query_start,
        dout_heads,
        log_sums,
        deltas,
        key_block,
        value_block,
        key_segs,
        key_start,
    )
    dquery = dquery + jnp.einsum(
        "shqk,kshd->qshd", score_gradient, key_block, preferred_element_type=jnp.float32
    )
    dtable = dtable + table_term(onehot, score_gradient)
    key_gradient = jnp.einsum(
        "shqk,qshd->kshd", score_gradient, query_heads, preferred_element_type=jnp.float32
    )
    dvalue = jnp.einsum(
        "shqk,qshd->kshd",
        probabilities.astype(jnp.bfloat16),
        dout_heads,
        preferred_element_type=jnp.float32,
    )
    joined = jnp.concatenate(
        (key_gradient.reshape(key_rows, seq_count, -1), dvalue.reshape(key_rows, seq_count, -1)),
        axis=2,
    )
    return ((dquery, dtable), joined)


def fold_blocks(step_fn, carried, pieces):
    piece_rows = pieces[0].shape[0]
    block_rows = math.gcd(piece_rows, 512)
    block_count = piece_rows // block_rows
    stacked = tuple(
        (piece.reshape((block_count, block_rows) + piece.shape[1:]) for piece in pieces)
    )

    def advance(state_now, scan_item):
        block_index, blocks = scan_item
        return (step_fn(state_now, blocks, block_index * block_rows), None)

    result, _ = lax.scan(advance, carried, (jnp.arange(block_count, dtype=jnp.int32), stacked))
    return result


def on_device(
    tokens,
    segments,
    buckets,
    gain_attn,
    w_query,
    w_key,
    w_value,
    w_output,
    gain_ffn,
    w_gate,
    w_up,
    w_down,
    bucket_bias_matrix,
    cotangent,
):
    tok_rows, seq_count, _ = tokens.shape
    head_count = bucket_bias_matrix.shape[1]
    inner_width = w_query.shape[1]
    head_width = inner_width // head_count
    head_shape = (tok_rows, seq_count, head_count, head_width)
    seq_length = (buckets.shape[0] + 1) // 2
    query_start = lax.axis_index("seq") * tok_rows
    (
        full_gain_attn,
        full_query,
        full_key,
        full_value,
        full_output,
        full_gain_ffn,
        full_gate,
        full_up,
        full_down,
    ) = (
        lax.all_gather(gain_attn, ("seq", "batch"), axis=0, tiled=True),
        lax.all_gather(w_query, ("seq", "batch"), axis=0, tiled=True),
        lax.all_gather(w_key, ("seq", "batch"), axis=0, tiled=True),
        lax.all_gather(w_value, ("seq", "batch"), axis=0, tiled=True),
        lax.all_gather(w_output, ("seq", "batch"), axis=0, tiled=True),
        lax.all_gather(gain_ffn, ("seq", "batch"), axis=0, tiled=True),
        lax.all_gather(w_gate, ("seq", "batch"), axis=0, tiled=True),
        lax.all_gather(w_up, ("seq", "batch"), axis=0, tiled=True),
        lax.all_gather(w_down, ("seq", "batch"), axis=0, tiled=True),
    )
    tokens_full = tokens.astype(jnp.float32)
    normed1 = normalize(tokens_full, full_gain_attn.astype(jnp.float32)).astype(jnp.bfloat16)
    query_heads = project(normed1, full_query).astype(jnp.bfloat16).reshape(head_shape)
    key_heads = project(normed1, full_key).astype(jnp.bfloat16).reshape(head_shape)
    value_heads = project(normed1, full_value).astype(jnp.bfloat16).reshape(head_shape)
    query_segs = lax.dynamic_slice_in_dim(segments, query_start, tok_rows, 0)
    table_set = (buckets, bucket_bias_matrix, seq_length)
    setting = (table_set, segments, query_heads, query_segs, query_start)
    start_state = (
        jnp.full((seq_count, head_count, tok_rows), NEGATIVE, jnp.float32),
        jnp.zeros((seq_count, head_count, tok_rows), jnp.float32),
        jnp.zeros(head_shape, jnp.float32),
    )
    step_forward = partial(attend_block, setting)
    running_max, running_sum, accum = fold_blocks(
        step_forward,
        start_state,
        (
            lax.all_gather(key_heads, "seq", axis=0, tiled=True),
            lax.all_gather(value_heads, "seq", axis=0, tiled=True),
        ),
    )
    attended_full = accum / jnp.transpose(running_sum, (2, 0, 1))[..., None]
    log_sums = running_max + jnp.log(running_sum)
    attended = attended_full.astype(jnp.bfloat16).reshape(tok_rows, seq_count, inner_width)
    hidden1 = tokens_full + project(attended, full_output)
    normed2 = normalize(hidden1, full_gain_ffn.astype(jnp.float32)).astype(jnp.bfloat16)
    gate = project(normed2, full_gate)
    up_val = project(normed2, full_up)
    gelu_out, gelu_pull = jax.vjp(gelu_tanh, gate)
    activated = (gelu_out * up_val).astype(jnp.bfloat16)
    mixed = (hidden1 + project(activated, full_down)).astype(jnp.bfloat16)
    (
        full_gain_attn,
        full_query,
        full_key,
        full_value,
        full_output,
        full_gain_ffn,
        full_gate,
        full_up,
        full_down,
    ) = (
        lax.all_gather(gain_attn, ("seq", "batch"), axis=0, tiled=True),
        lax.all_gather(w_query, ("seq", "batch"), axis=0, tiled=True),
        lax.all_gather(w_key, ("seq", "batch"), axis=0, tiled=True),
        lax.all_gather(w_value, ("seq", "batch"), axis=0, tiled=True),
        lax.all_gather(w_output, ("seq", "batch"), axis=0, tiled=True),
        lax.all_gather(gain_ffn, ("seq", "batch"), axis=0, tiled=True),
        lax.all_gather(w_gate, ("seq", "batch"), axis=0, tiled=True),
        lax.all_gather(w_up, ("seq", "batch"), axis=0, tiled=True),
        lax.all_gather(w_down, ("seq", "batch"), axis=0, tiled=True),
    )
    grad_down = weight_grad(activated, cotangent)
    d_activated = project_back(cotangent, full_down)
    d_gate = gelu_pull(d_activated * up_val)[0].astype(jnp.bfloat16)
    d_up = (gelu_out * d_activated).astype(jnp.bfloat16)
    grad_gate = weight_grad(normed2, d_gate)
    grad_up = weight_grad(normed2, d_up)
    d_normed2 = project_back(d_gate, full_gate) + project_back(d_up, full_up)
    _, norm_pull2 = jax.vjp(normalize, hidden1, full_gain_ffn.astype(jnp.float32))
    d_hidden_part, grad_gain_ffn = norm_pull2(d_normed2)
    d_hidden1 = cotangent.astype(jnp.float32) + d_hidden_part
    d_branch = d_hidden1.astype(jnp.bfloat16)
    grad_output = weight_grad(attended, d_branch)
    dout_heads = project_back(d_branch, full_output).astype(jnp.bfloat16).reshape(head_shape)
    deltas = jnp.transpose(
        jnp.sum(dout_heads.astype(jnp.float32) * attended_full, axis=-1), (1, 2, 0)
    )
    extras = (dout_heads, log_sums, deltas)
    keys_all, values_all = (
        lax.all_gather(key_heads, "seq", axis=0, tiled=True),
        lax.all_gather(value_heads, "seq", axis=0, tiled=True),
    )
    block_rows = math.gcd(seq_length, 512)
    block_count = seq_length // block_rows
    stacked_keys = keys_all.reshape((block_count, block_rows) + keys_all.shape[1:])
    stacked_values = values_all.reshape((block_count, block_rows) + values_all.shape[1:])
    block_starts = jnp.arange(block_count, dtype=jnp.int32) * block_rows
    query_init = (
        jnp.zeros(head_shape, jnp.float32),
        jnp.zeros(bucket_bias_matrix.shape, jnp.float32),
    )
    (dquery, dtable), joined_all = lax.scan(
        partial(merged_block, setting, extras),
        query_init,
        (block_starts, stacked_keys, stacked_values),
    )
    every_key_contribution = joined_all.reshape(seq_length, seq_count, 2 * inner_width)
    key_sums = lax.psum_scatter(every_key_contribution, "seq", scatter_dimension=0, tiled=True)
    dkey_rows = key_sums[:, :, :inner_width].astype(jnp.bfloat16)
    dvalue_rows = key_sums[:, :, inner_width:].astype(jnp.bfloat16)
    dquery_rows = dquery.reshape(tok_rows, seq_count, inner_width).astype(jnp.bfloat16)
    grad_query = weight_grad(normed1, dquery_rows)
    grad_key = weight_grad(normed1, dkey_rows)
    grad_value = weight_grad(normed1, dvalue_rows)
    d_normed1 = (
        project_back(dquery_rows, full_query)
        + project_back(dkey_rows, full_key)
        + project_back(dvalue_rows, full_value)
    )
    _, norm_pull1 = jax.vjp(normalize, tokens_full, full_gain_attn.astype(jnp.float32))
    d_input_part, grad_gain_attn = norm_pull1(d_normed1)
    tokens_grad = (d_hidden1 + d_input_part).astype(jnp.bfloat16)
    owned = (
        lax.psum_scatter(grad_gain_attn, ("seq", "batch"), scatter_dimension=0, tiled=True),
        lax.psum_scatter(grad_query, ("seq", "batch"), scatter_dimension=0, tiled=True),
        lax.psum_scatter(grad_key, ("seq", "batch"), scatter_dimension=0, tiled=True),
        lax.psum_scatter(grad_value, ("seq", "batch"), scatter_dimension=0, tiled=True),
        lax.psum_scatter(grad_output, ("seq", "batch"), scatter_dimension=0, tiled=True),
        lax.psum_scatter(grad_gain_ffn, ("seq", "batch"), scatter_dimension=0, tiled=True),
        lax.psum_scatter(grad_gate, ("seq", "batch"), scatter_dimension=0, tiled=True),
        lax.psum_scatter(grad_up, ("seq", "batch"), scatter_dimension=0, tiled=True),
        lax.psum_scatter(grad_down, ("seq", "batch"), scatter_dimension=0, tiled=True),
    )
    table_total = lax.psum(dtable, ("seq", "batch"))
    return (
        mixed,
        tokens_grad,
        owned[0],
        owned[1],
        owned[2],
        owned[3],
        owned[4],
        owned[5],
        owned[6],
        owned[7],
        owned[8],
        table_total,
    )


BF16 = jnp.bfloat16
F32 = jnp.float32
MESH_IDS = pl.DeviceIdType.MESH

ZS, XS, YS, CS = 4, 2, 2, 2
SEQ_DEVICES = ZS * XS
BATCH_DEVICES = YS * CS
TOK = 128
LENGTH = SEQ_DEVICES * TOK
DIM = 768
HALF = DIM // CS
PAIRS = HALF // 128
SHARD = DIM // (SEQ_DEVICES * BATCH_DEVICES)
CHIP_ROWS = SHARD * CS
GROUP_ROWS = SHARD * BATCH_DEVICES
FF_ALL = 2048
QUARTER = FF_ALL // BATCH_DEVICES
DOWN_ROWS = FF_ALL // (SEQ_DEVICES * BATCH_DEVICES)
CHUNKS = PAIRS + 1
SPAN = LENGTH + TOK
HEADS_HERE = 2 * PAIRS


def dot(a, b):
    return lax.dot_general(a, b, (((1,), (0,)), ((), ())), preferred_element_type=F32)


def dot_tb(a, b):
    return lax.dot_general(a, b, (((1,), (1,)), ((), ())), preferred_element_type=F32)


def dot_ta(a, b):
    return lax.dot_general(a, b, (((0,), (0,)), ((), ())), preferred_element_type=F32)


def to_column(row):
    n = row.shape[1]
    eye = lax.broadcasted_iota(jnp.int32, (n, n), 0) == lax.broadcasted_iota(jnp.int32, (n, n), 1)
    return jnp.sum(jnp.where(eye, jnp.broadcast_to(row, (n, n)), 0.0), axis=1, keepdims=True)


def to_row(col):
    n = col.shape[0]
    eye = lax.broadcasted_iota(jnp.int32, (n, n), 0) == lax.broadcasted_iota(jnp.int32, (n, n), 1)
    return jnp.sum(jnp.where(eye, jnp.broadcast_to(col, (n, n)), 0.0), axis=0, keepdims=True)


def unit_rows(x):
    r = lax.rsqrt(jnp.mean(x * x, axis=1, keepdims=True) + EPSILON)
    return x * r, r


def stack_heads(pair):
    low = lax.broadcasted_iota(jnp.int32, pair.shape, 1) < 64
    return jnp.concatenate((jnp.where(low, pair, 0.0), jnp.where(low, 0.0, pair)), axis=0).astype(BF16)


def unstack_heads(stacked):
    rows = stacked.shape[0] // 2
    low = lax.broadcasted_iota(jnp.int32, (rows, 128), 1) < 64
    return jnp.where(low, stacked[:rows], stacked[rows:])


def split_quarters(whole):
    low = lax.broadcasted_iota(jnp.int32, (whole.shape[0], 128), 1) < 64
    parts = []
    for q in range(BATCH_DEVICES):
        cols = []
        for m in range(ZS):
            first = 4 * m + 2 * (q // 2)
            a = whole[:, 128 * first : 128 * first + 128]
            b = whole[:, 128 * (first + 1) : 128 * (first + 1) + 128]
            if q % 2 == 0:
                cols.append(jnp.where(low, a, pltpu.roll(b, 64, 1)))
            else:
                cols.append(jnp.where(low, pltpu.roll(a, 64, 1), b))
        parts.append(jnp.concatenate(cols, axis=1))
    return parts


def join_quarters(parts):
    low = lax.broadcasted_iota(jnp.int32, (parts[0].shape[0], 128), 1) < 64
    cols = []
    for block in range(FF_ALL // 128):
        m, xx, yy = block // 4, block // 2 % 2, block % 2
        lanes = slice(128 * m, 128 * m + 128)
        a, b = parts[2 * xx][:, lanes], parts[2 * xx + 1][:, lanes]
        if yy == 0:
            cols.append(jnp.where(low, a, pltpu.roll(b, 64, 1)))
        else:
            cols.append(jnp.where(low, pltpu.roll(a, 64, 1), b))
    return jnp.concatenate(cols, axis=1)


SCRATCH = dict(
    W_MINE=((CS, SHARD, 4 * HALF + 4 * QUARTER), F32),
    W_CORE=((CS, SHARD, 4 * HALF + 4 * QUARTER), F32),
    UB=((XS, CHIP_ROWS, 2 * QUARTER), BF16),
    WA=((PAIRS, ZS, XS, YS, CHIP_ROWS, HALF), BF16),
    WO=((CS, ZS, XS, YS, CHIP_ROWS, HALF), BF16),
    WG=((ZS, XS, YS, CHIP_ROWS, 2 * QUARTER), BF16),
    WD=((ZS, YS, DOWN_ROWS, DIM), BF16),
    X=((CS, ZS, XS, TOK, DIM), BF16),
    N1=((CS, ZS, XS, TOK, DIM), BF16),
    N1O=((CS, TOK, DIM), BF16),
    COT=((XS, CS, TOK, DIM), BF16),
    SEG=((CS, 8, LENGTH), F32),
    BK=((1, 2 * LENGTH), jnp.int32),
    PH=((2 * CS * PAIRS, SPAN), F32),
    BIAS=((PAIRS, 2 * TOK, LENGTH), BF16),
    MASK=((CS, TOK, LENGTH), BF16),
    KV=((PAIRS, CS, LENGTH, 256), BF16),
    QS=((PAIRS, CS, 2 * TOK, 128), BF16),
    PS=((PAIRS, CS, 2 * TOK, LENGTH), BF16),
    ATT=((CS, CS, TOK, HALF), BF16),
    H=((TOK, DIM), F32),
    N2=((XS, CS, TOK, DIM), BF16),
    ACT=((XS, 2 * TOK, QUARTER), BF16),
    DGU=((XS, 2 * TOK, 2 * QUARTER), BF16),
    MX=((XS, CS, TOK, DIM), BF16),
    MXC=((XS, TOK, DIM), BF16),
    MXS=((TOK, DIM), BF16),
    MXX=((TOK, DIM), BF16),
    E2=((XS, CS, TOK, DIM), BF16),
    E2C=((XS, TOK, DIM), BF16),
    E2S=((TOK, DIM), BF16),
    E2X=((TOK, DIM), BF16),
    GG=((ZS, XS, YS, CHIP_ROWS, 2 * QUARTER), BF16),
    GGY=((ZS, XS, CHIP_ROWS, 2 * QUARTER), BF16),
    GGZ=((ZS, XS, CHIP_ROWS, 2 * QUARTER), BF16),
    GGC=((XS, CHIP_ROWS, 2 * QUARTER), BF16),
    GD=((ZS, YS, DOWN_ROWS, DIM), BF16),
    GDY=((ZS, DOWN_ROWS, DIM), BF16),
    GDZ=((ZS, DOWN_ROWS, DIM), BF16),
    GDC=((DOWN_ROWS, DIM), BF16),
    F4S=((XS, CHIP_ROWS, 2 * QUARTER), BF16),
    F4X=((CHIP_ROWS, 2 * QUARTER), BF16),
    F4S2=((CS, XS, SHARD, 2 * QUARTER), F32),
    F4=((CS, XS, SHARD, 2 * QUARTER), F32),
    DH=((TOK, DIM), F32),
    DB=((CS, TOK, DIM), BF16),
    DO=((CS, TOK, HALF), BF16),
    DQ=((PAIRS, CS, TOK, 128), BF16),
    DKV=((PAIRS, CS, 256, LENGTH), BF16),
    DG=((8, SPAN), F32),
    GA=((CHUNKS, ZS, XS, YS, CHIP_ROWS, HALF), BF16),
    GA1=((CHUNKS, ZS, 2, CHIP_ROWS, HALF), BF16),
    GA2=((CHUNKS, ZS, CHIP_ROWS, HALF), BF16),
    GAZ=((CHUNKS, ZS, CHIP_ROWS, HALF), BF16),
    GAC=((CHUNKS, CHIP_ROWS, HALF), BF16),
    FA=((CHUNKS, CS, SHARD, HALF), F32),
    F2=((CHUNKS, CS, SHARD, HALF), F32),
    GT=((PAIRS, SHARD, 128), F32),
    DN=((CS, ZS, XS, DIM, TOK), BF16),
    DNC=((ZS, XS, DIM, TOK), BF16),
    DNX=((ZS, DIM, TOK), BF16),
    DNZ=((ZS, DIM, TOK), BF16),
    DNT=((DIM, TOK), BF16),
    T1=((8, 128), F32),
    TY=((8, 128), F32),
    T2=((8, 128), F32),
    TX=((8, 128), F32),
    T3=((8, 128), F32),
    TZ=((ZS, 8, 128), F32),
    TO=((CS, 8, 128), F32),
)
SEND_RING = 72
SLOTS = dict(
    segc=1, wc=1, u=1, xz=4, xx=4, xc=8, wz=4 * CHUNKS, wx=4 * CHUNKS, wy=4 * CHUNKS, wr=CHUNKS, woc=1,
    gz=8, gy=8, dz=4, dy=4, cotx=1, cotc=2, att=2, n2x=1, n2c=2, mxc=2, mxx=1, e2c=2, e2x=1,
    rdy=4, rdz=4, rdc=1, rgy=4, rgz=4, rgc=1, f4x=1, f4=1, db=1,
    ra1=CHUNKS, ra2=CHUNKS, raz=4 * CHUNKS, rac=CHUNKS, f2=CHUNKS,
    dnc=4, dnx=4, dnz=4, dnt=1, ty=1, tx=1, tz=4, tc=1,
)
RECV_COUNT = sum(SLOTS.values())


def slot_bases():
    bases, used = {}, 0
    for name, count in SLOTS.items():
        bases[name] = used
        used += count
    return SimpleNamespace(**bases)


INPUTS = dict(
    tok=0, cot=0, seg=0, buckets=0, table=0, ga=0, gf=0, wq=0, wk=0, wv=0, wo=0, wg=0, wu=0, wd=0
)
OUTPUTS = dict(
    mixed=((TOK, DIM), BF16), tg=((TOK, DIM), BF16), gga=((1, SHARD), F32),
    gwq=((SHARD, DIM), F32), gwk=((SHARD, DIM), F32), gwv=((SHARD, DIM), F32), gwo=((SHARD, DIM), F32),
    ggf=((1, SHARD), F32), gwg=((SHARD, FF_ALL), F32), gwu=((SHARD, FF_ALL), F32),
    gwd=((DOWN_ROWS, DIM), F32), gtab=((2 * CS * PAIRS, 32), F32),
)


RELAY_TO_Y = (True, True, False, False)
HEAVY_X = (False, False, True, True)
FAR_DIRECT_CHIP = (False, False, False, False)
FAR_DIRECT_TOKEN = False
SPREAD_TOKEN = False
SPREAD_CHIP = (False, False, False, False)
SPREAD_GATE = False
SPREAD_DOWN = False


def layer_kernel(*refs):
    names = (*INPUTS, *OUTPUTS, *SCRATCH)
    r = SimpleNamespace(**dict(zip(names, refs[:-2], strict=True)))
    ssem, rsem = refs[-2:]
    k = slot_bases()
    s, b = lax.axis_index("seq"), lax.axis_index("batch")
    z, x = s // XS, s % XS
    y, c = b // CS, b % CS
    xo, yo, co = 1 - x, 1 - y, 1 - c
    side = z // 2
    m = z + side * (3 - 2 * z)
    at_end, beside = m == 0, m == 1
    zord = [near + side * (3 - 2 * near) for near in (1 - m, 2, 3)]

    def at(zz, xx, yy, cc):
        return (XS * zz + xx, CS * yy + cc)

    to_core, to_x, to_y = at(z, x, y, co), at(z, xo, y, c), at(z, x, yo, c)
    to_z = [at(zz, x, y, c) for zz in zord]

    barrier = pltpu.get_barrier_semaphore()
    friends = [to_core, to_x, to_y] + to_z
    for who in friends:
        pl.semaphore_signal(barrier, inc=1, device_id=who, device_id_type=MESH_IDS)

    sent = []

    def sent_wait(i):
        copy, when = sent[i]
        if when is None:
            copy.wait_send()
        else:
            pl.when(when)(copy.wait_send)

    def put(src, dst, who, slot, when=None):
        if len(sent) >= SEND_RING:
            sent_wait(len(sent) - SEND_RING)
        copy = pltpu.make_async_remote_copy(
            src_ref=src, dst_ref=dst, send_sem=ssem.at[len(sent) % SEND_RING], recv_sem=rsem.at[slot],
            device_id=who, device_id_type=MESH_IDS,
        )
        if when is None:
            copy.start()
        else:
            pl.when(when)(copy.start)
        sent.append((copy, when))

    def take(dst, slot, when=None):
        wait = pltpu.make_async_remote_copy(
            src_ref=dst, dst_ref=dst, send_sem=ssem.at[0], recv_sem=rsem.at[slot],
            device_id=to_core, device_id_type=MESH_IDS,
        ).wait_recv
        if when is None:
            wait()
        else:
            pl.when(when)(wait)

    def z_send(src, dst, slot, direct):
        put(src, dst, to_z[0], slot + z)
        put(src, dst, to_z[1], slot + z)
        put(src, dst, to_z[2], slot + z, when=None if direct else beside)

    def z_take(block, slot, i, direct):
        zz = zord[i]
        take(block(zz), slot + zz)
        if i == 2 and not direct:
            put(block(zz), block(zz), to_z[0], slot + zz, when=beside)

    def z_scatter(part, land, chain, slot, chain_slot, i):
        if i == 2 and chain is None:
            put(part(zord[2]), land.at[z], to_z[2], slot + z)
        elif i == 2:
            put(part(zord[2]), chain, to_z[0], chain_slot, when=at_end)
        else:
            put(part(zord[i]), land.at[z], to_z[i], slot + z)

    def z_chain(part, land, chain, slot, chain_slot):
        @pl.when(beside)
        def _():
            take(chain, chain_slot)
            mine = part(zord[2])
            mine[...] = (mine[...].astype(F32) + chain[...].astype(F32)).astype(BF16)

        put(part(zord[2]), land.at[z], to_z[2], slot + z, when=beside)

    def z_zero(land):
        @pl.when(at_end)
        def _():
            land[zord[2]] = jnp.zeros(land.shape[1:], land.dtype)

    def z_sum(own, land, slot, direct=False):
        take(land.at[zord[0]], slot + zord[0])
        take(land.at[zord[1]], slot + zord[1])
        take(land.at[zord[2]], slot + zord[2], when=None if direct else beside)
        total = own.astype(F32)
        for zz in zord:
            total = total + land[zz].astype(F32)
        return total

    gain_a = to_column(r.ga[...].astype(F32))
    gain_f = to_column(r.gf[...].astype(F32))
    tok = r.tok
    r.SEG[c] = jnp.broadcast_to(r.seg[...].astype(F32), (8, LENGTH))
    for h in range(CS):
        for p in range(PAIRS):
            for j, w_ref in enumerate((r.wq, r.wk, r.wv)):
                lanes = slice(HALF * h + 128 * p, HALF * h + 128 * p + 128)
                r.W_MINE[h, :, HALF * p + 128 * j : HALF * p + 128 * j + 128] = (
                    w_ref[:, lanes].astype(F32) * gain_a
                )
        r.W_MINE[h, :, 3 * HALF : 4 * HALF] = r.wo[:, HALF * h : HALF * h + HALF].astype(F32)
    for j, w_ref in enumerate((r.wg, r.wu)):
        for q, part in enumerate(split_quarters(w_ref[...].astype(F32) * gain_f)):
            first = 4 * HALF + 2 * QUARTER * (q // CS) + QUARTER * j
            r.W_MINE[q % CS, :, first : first + QUARTER] = part

    pl.semaphore_wait(barrier, len(friends))

    put(r.W_MINE.at[co], r.W_CORE.at[c], to_core, k.wc)
    put(tok, r.X.at[c, z, x], to_x, k.xx + z)
    put(r.SEG.at[c], r.SEG.at[c], to_core, k.segc)
    put(tok, r.X.at[c, z, x], to_core, k.xc + s)
    r.X[c, z, x] = tok[...]
    r.WD[z, y] = r.wd[...]
    r.W_CORE[c] = r.W_MINE[c]

    def weight(ch):
        return r.WA.at[ch] if ch < PAIRS else r.WO.at[c]

    def weight_start(ch):
        own = weight(ch).at[z, x, y]
        z_send(own, own, k.wz + 4 * ch, SPREAD_CHIP[ch])
        put(own, own, to_y, k.wy + 4 * ch + z)
        put(own, own, to_x, k.wx + 4 * ch + z)

    def norm_block(q, zz, xx, own=False):
        value = unit_rows(r.X[q, zz, xx].astype(F32))[0].astype(BF16)
        r.N1[q, zz, xx] = value
        if own:
            r.N1O[q] = value

    def token_from_z(i):
        z_take(lambda zz: r.X.at[c, zz, x], k.xz, i, SPREAD_TOKEN)
        zz = zord[i]
        put(r.X.at[c, zz, x], r.X.at[c, zz, x], to_x, k.xx + zz)
        put(r.X.at[c, zz, x], r.X.at[c, zz, x], to_core, k.xc + XS * zz + x)
        norm_block(c, zz, x)

    def token_from_x(zz):
        take(r.X.at[c, zz, xo], k.xx + zz)
        put(r.X.at[c, zz, xo], r.X.at[c, zz, xo], to_core, k.xc + XS * zz + xo)
        norm_block(c, zz, xo)

    def token_from_core(zz, xx):
        take(r.X.at[co, zz, xx], k.xc + XS * zz + xx)
        norm_block(co, zz, xx, own=zz is z and xx is x)

    def bias_lines():
        r.BK[...] = jnp.zeros(r.BK.shape, jnp.int32)
        r.BK[:, : 2 * LENGTH - 1] = r.buckets[...]
        onehot = (
            lax.broadcasted_iota(jnp.int32, (32, SPAN), 0)
            == r.BK[:, pl.ds(pl.multiple_of(LENGTH - TOK - TOK * s, 128), SPAN)]
        )
        r.PH[...] = dot(r.table[...], onehot.astype(BF16))

    def bias_pair(p):
        for hh in range(2):
            line = r.PH[pl.ds(HEADS_HERE * c + 2 * p + hh, 1), :]
            skewed = pltpu.roll(
                jnp.broadcast_to(line, (TOK, SPAN)), SPAN - TOK + 1, 1, stride=1, stride_axis=0
            )
            r.BIAS[p, TOK * hh : TOK * hh + TOK, :] = skewed[:, :LENGTH].astype(BF16)

    def masks():
        take(r.SEG.at[co], k.segc)
        for q in range(CS):
            col = to_column(r.SEG[q, 0:1, pl.ds(pl.multiple_of(TOK * s, 128), TOK)])
            r.MASK[q] = jnp.where(col == r.SEG[q, 0:1, :], 0.0, NEGATIVE).astype(BF16)

    def weight_from_z(ch, i):
        w = weight(ch)
        z_take(lambda zz: w.at[zz, x, y], k.wz + 4 * ch, i, SPREAD_CHIP[ch])
        arrived = w.at[zord[i], x, y]
        put(arrived, arrived, to_y, k.wy + 4 * ch + zord[i])
        put(arrived, arrived, to_x, k.wx + 4 * ch + zord[i])

    def weight_relay(ch):
        w = weight(ch)
        for zz in [z] + zord:
            if RELAY_TO_Y[ch]:
                take(w.at[zz, xo, y], k.wx + 4 * ch + zz)
            else:
                take(w.at[zz, x, yo], k.wy + 4 * ch + zz)
        if RELAY_TO_Y[ch]:
            put(w.at[:, xo, y], w.at[:, xo, y], to_y, k.wr + ch)
        else:
            put(w.at[:, x, yo], w.at[:, x, yo], to_x, k.wr + ch)

    def weight_end(ch):
        w = weight(ch)
        for zz in [z] + zord:
            if RELAY_TO_Y[ch]:
                take(w.at[zz, x, yo], k.wy + 4 * ch + zz)
            else:
                take(w.at[zz, xo, y], k.wx + 4 * ch + zz)
        take(w.at[:, xo, yo], k.wr + ch)

    def gate_send(xx):
        own = r.WG.at[z, xx, y]
        z_send(own, own, k.gz + 4 * xx, SPREAD_GATE)
        put(own, own, to_y, k.gy + 4 * xx + z)

    def gate_from_z(xx, i):
        z_take(lambda zz: r.WG.at[zz, xx, y], k.gz + 4 * xx, i, SPREAD_GATE)
        arrived = r.WG.at[zord[i], xx, y]
        put(arrived, arrived, to_y, k.gy + 4 * xx + zord[i])

    def down_from_z(i):
        z_take(lambda zz: r.WD.at[zz, y], k.dz, i, SPREAD_DOWN)
        put(r.WD.at[zord[i], y], r.WD.at[zord[i], y], to_y, k.dy + zord[i])

    def tokens_send(i):
        far = beside if i == 2 and not SPREAD_TOKEN else None
        put(tok, r.X.at[c, z, x], to_z[i], k.xz + z, when=far)

    def down_send():
        put(r.wd, r.WD.at[z, y], to_y, k.dy + z)
        z_send(r.wd, r.WD.at[z, y], k.dz, SPREAD_DOWN)

    def shards():
        take(r.W_CORE.at[co], k.wc)
        shard = r.W_CORE[...].reshape(CHIP_ROWS, 4 * HALF + 4 * QUARTER).astype(BF16)
        for ch in range(PAIRS):
            r.WA[ch, z, x, y] = shard[:, HALF * ch : HALF * ch + HALF]
        r.WO[c, z, x, y] = shard[:, 3 * HALF : 4 * HALF]
        for xx in range(XS):
            first = 4 * HALF + 2 * QUARTER * xx
            r.UB[xx] = shard[:, first : first + 2 * QUARTER]
        r.WG[z, x, y] = r.UB[x]

    def gate_exchange():
        put(r.UB.at[xo], r.WG.at[z, x, y], to_x, k.u)

    def gate_other():
        take(r.WG.at[z, xo, y], k.u)
        gate_send(xo)

    def cot_send():
        put(r.cot, r.COT.at[x, c], to_core, k.cotc + 0)
        put(r.cot, r.COT.at[x, c], to_x, k.cotx)
        r.COT[x, c] = r.cot[...]

    def cot_from_x():
        take(r.COT.at[xo, c], k.cotx)
        put(r.COT.at[xo, c], r.COT.at[xo, c], to_core, k.cotc + 1)

    def output_send():
        put(r.WO.at[c], r.WO.at[c], to_core, k.woc)

    zall = [z] + zord

    def keys_values(q, zz):
        rows = r.N1[q, zz].reshape(XS * TOK, DIM)
        for p in range(PAIRS):
            kv = dot(rows, r.WA[p].reshape(DIM, HALF)[:, 128:])
            r.KV[p, q, pl.ds(pl.multiple_of(XS * TOK * zz, 128), XS * TOK), :] = kv.astype(BF16)

    def queries(q):
        for p in range(PAIRS):
            r.QS[p, q] = stack_heads(dot(r.N1O[q], r.WA[p].reshape(DIM, HALF)[:, :128]))

    def attend(p, q):
        kv = r.KV.at[p, q]
        stacked = r.QS[p, q]
        mask = r.MASK[q].astype(F32)
        scores = dot_tb(stacked, kv[:, :128]) + r.BIAS[p].astype(F32) + jnp.concatenate((mask, mask), axis=0)
        weights = jnp.exp(scores - jnp.max(scores, axis=1, keepdims=True))
        probs = (weights * (1.0 / jnp.sum(weights, axis=1, keepdims=True))).astype(BF16)
        r.PS[p, q] = probs
        r.ATT[c, q, :, 128 * p : 128 * p + 128] = unstack_heads(dot(probs, kv[:, 128:])).astype(BF16)

    def attended_send(q):
        put(r.ATT.at[c, q], r.ATT.at[c, q], to_core, k.att + (1 if q is c else 0))

    bias_lines()
    tokens_send(0)
    shards()
    gate_exchange()
    weight_start(PAIRS)
    token_from_core(z, x)
    weight_start(1)
    bias_pair(0)
    weight_start(2)
    bias_pair(2)
    masks()
    weight_from_z(PAIRS, 0)
    weight_start(0)
    token_from_z(0)
    tokens_send(1)
    tokens_send(2)
    gate_other()
    down_send()
    weight_from_z(PAIRS, 1)
    token_from_x(z)
    weight_from_z(2, 0)
    weight_from_z(2, 1)
    token_from_core(z, xo)
    weight_from_z(1, 0)
    weight_from_z(1, 1)
    weight_from_z(PAIRS, 2)
    weight_from_z(0, 1)
    norm_block(c, z, x, own=True)
    gate_send(x)
    weight_from_z(0, 0)
    bias_pair(1)
    token_from_x(zord[0])
    token_from_core(zord[0], x)
    token_from_core(zord[0], xo)
    weight_from_z(0, 2)
    weight_from_z(1, 2)
    weight_from_z(2, 2)
    token_from_z(1)
    weight_relay(0)
    weight_relay(1)
    token_from_core(zord[1], x)
    weight_relay(2)
    gate_from_z(x, 0)
    token_from_z(2)
    down_from_z(0)
    gate_from_z(xo, 0)
    token_from_x(zord[1])
    weight_relay(PAIRS)
    gate_from_z(xo, 1)
    weight_end(0)
    weight_end(1)
    weight_end(2)
    queries(1)
    keys_values(c, zord[0])
    keys_values(co, z)
    token_from_core(zord[1], xo)
    keys_values(c, zord[1])
    keys_values(c, z)
    down_from_z(1)
    token_from_core(zord[2], x)
    queries(0)
    token_from_x(zord[2])
    keys_values(c, zord[2])
    keys_values(co, zord[1])
    cot_send()
    keys_values(co, zord[0])
    gate_from_z(xo, 2)
    weight_end(PAIRS)
    token_from_core(zord[2], xo)
    keys_values(co, zord[2])
    attend(1, co)
    attend(0, co)
    down_from_z(2)
    gate_from_z(x, 1)
    output_send()
    attend(0, c)
    attend(2, co)
    attended_send(co)
    gate_from_z(x, 2)
    cot_from_x()
    attend(2, c)
    attend(1, c)
    attended_send(c)
    take(r.WO.at[co], k.woc)
    take(r.ATT.at[co, c], k.att)

    att_own = jnp.concatenate((r.ATT[0, c], r.ATT[1, c]), axis=1)
    tokens_f = tok[...].astype(F32)
    r.H[...] = tokens_f + jnp.concatenate(
        (dot(att_own, r.WO[0].reshape(DIM, HALF)), dot(att_own, r.WO[1].reshape(DIM, HALF))), axis=1
    )
    r.N2[x, c] = unit_rows(r.H[...])[0].astype(BF16)
    put(r.N2.at[x, c], r.N2.at[x, c], to_core, k.n2c + 0)
    put(r.N2.at[x, c], r.N2.at[x, c], to_x, k.n2x)

    for zz in [z] + zord:
        for xx in range(XS):
            take(r.WG.at[zz, xx, yo], k.gy + 4 * xx + zz)
        take(r.WD.at[zz, yo], k.dy + zz)
    take(r.COT.at[x, co], k.cotc + 0)
    take(r.COT.at[xo, co], k.cotc + 1)
    take(r.N2.at[x, co], k.n2c + 0)

    def feed_forward(xx):
        w_gu = r.WG[...].reshape(DIM, 2 * QUARTER)
        w_d = r.WD[...].reshape(QUARTER, DIM)
        n2 = r.N2[xx].reshape(2 * TOK, DIM)
        g = r.COT[xx].reshape(2 * TOK, DIM)
        gate = dot(n2, w_gu[:, :QUARTER])
        up = dot(n2, w_gu[:, QUARTER:])
        d_act = dot_tb(g, w_d)
        square = gate * gate
        inner = math.sqrt(2 / math.pi) * gate * (1.0 + 0.044715 * square)
        tanh = jnp.tanh(inner)
        half_open = 0.5 * (1.0 + tanh)
        gelu = gate * half_open
        slope = half_open + 0.5 * gate * (1.0 - tanh * tanh) * (
            math.sqrt(2 / math.pi) * (1.0 + 3 * 0.044715 * square)
        )
        act = (gelu * up).astype(BF16)
        r.ACT[xx] = act
        d_gu = jnp.concatenate(
            ((slope * (up * d_act)).astype(BF16), (gelu * d_act).astype(BF16)), axis=1
        )
        r.DGU[xx] = d_gu
        r.E2[xx] = dot_tb(d_gu, w_gu).astype(BF16).reshape(CS, TOK, DIM)
        put(r.E2.at[xx, co], r.E2C.at[xx], to_core, k.e2c + xx)
        r.MX[xx] = dot(act, w_d).astype(BF16).reshape(CS, TOK, DIM)
        put(r.MX.at[xx, co], r.MXC.at[xx], to_core, k.mxc + xx)

    feed_forward(x)
    take(r.N2.at[xo, c], k.n2x)
    put(r.N2.at[xo, c], r.N2.at[xo, c], to_core, k.n2c + 1)
    take(r.N2.at[xo, co], k.n2c + 1)
    feed_forward(xo)
    far_first = [zord[2], zord[1], zord[0], z]

    def down_grad(zz):
        return r.GD.at[zz, y]

    def gate_grad(zz):
        return r.GG.at[zz, :, y]

    def grad_from_y(part, got, slot, scatter, i):
        zz = far_first[i]
        take(got.at[zz], slot + zz)
        mine = part(zz)
        mine[...] = (mine[...].astype(F32) + got[zz].astype(F32)).astype(BF16)
        if i < 3:
            z_scatter(part, *scatter, 2 - i)

    down_scatter = (r.GDZ, r.GDC, k.rdz, k.rdc)
    gate_scatter = (r.GGZ, r.GGC, k.rgz, k.rgc)

    def down_from_y(i):
        grad_from_y(down_grad, r.GDY, k.rdy, down_scatter, i)

    def gate_from_y(i):
        grad_from_y(gate_grad, r.GGY, k.rgy, gate_scatter, i)

    def down_chain():
        z_chain(down_grad, *down_scatter)

    def gate_chain():
        z_chain(gate_grad, *gate_scatter)

    def chip_grad(ch, value):
        r.GA[ch] = value.astype(BF16).reshape(ZS, XS, YS, CHIP_ROWS, HALF)
        if HEAVY_X[ch]:
            put(r.GA.at[ch, :, xo], r.GA1.at[ch], to_x, k.ra1 + ch)
        else:
            put(r.GA.at[ch, :, :, yo], r.GA1.at[ch], to_y, k.ra1 + ch)

    def chip_step1(ch):
        take(r.GA1.at[ch], k.ra1 + ch)
        if HEAVY_X[ch]:
            r.GA[ch, :, x] = (r.GA[ch, :, x].astype(F32) + r.GA1[ch].astype(F32)).astype(BF16)
            put(r.GA.at[ch, :, x, yo], r.GA2.at[ch], to_y, k.ra2 + ch)
        else:
            r.GA[ch, :, :, y] = (r.GA[ch, :, :, y].astype(F32) + r.GA1[ch].astype(F32)).astype(BF16)
            put(r.GA.at[ch, :, xo, y], r.GA2.at[ch], to_x, k.ra2 + ch)

    def chip_scatter(ch):
        chain = None if FAR_DIRECT_CHIP[ch] else r.GAC.at[ch]
        return (lambda zz: r.GA.at[ch, zz, x, y]), r.GAZ.at[ch], chain, k.raz + 4 * ch, k.rac + ch

    def chip_step2(ch):
        take(r.GA2.at[ch], k.ra2 + ch)
        r.GA[ch, :, x, y] = (r.GA[ch, :, x, y].astype(F32) + r.GA2[ch].astype(F32)).astype(BF16)
        for i in (2, 1, 0):
            z_scatter(*chip_scatter(ch), i)

    def chip_chain(ch):
        if not FAR_DIRECT_CHIP[ch]:
            z_chain(*chip_scatter(ch))

    def chip_end(ch):
        total = z_sum(r.GA[ch, z, x, y], r.GAZ.at[ch], k.raz + 4 * ch, FAR_DIRECT_CHIP[ch])
        r.FA[ch] = total.reshape(CS, SHARD, HALF)
        put(r.FA.at[ch, co], r.F2.at[ch, c], to_core, k.f2 + ch)
        r.F2[ch, c] = r.FA[ch, c]

    reverse = (
        lax.broadcasted_iota(jnp.int32, (TOK, TOK), 0) + lax.broadcasted_iota(jnp.int32, (TOK, TOK), 1)
        == TOK - 1
    ).astype(BF16)
    reverse2 = jnp.concatenate((reverse, reverse), axis=1)

    def attend_back(p, q):
        d_out = stack_heads(r.DO[q, :, 128 * p : 128 * p + 128].astype(F32))
        kv = r.KV.at[p, q]
        probs = r.PS[p, q]
        weighted = probs.astype(F32) * dot_tb(d_out, kv[:, 128:])
        delta = jnp.sum(weighted, axis=1, keepdims=True)
        d_scores = (weighted - probs.astype(F32) * delta).astype(BF16)
        r.DQ[p, q] = unstack_heads(dot(d_scores, kv[:, :128])).astype(BF16)
        r.DKV[p, q, :128] = dot_ta(r.QS[p, q], d_scores).astype(BF16)
        r.DKV[p, q, 128:] = dot_ta(d_out, probs).astype(BF16)
        r.PS[p, q] = d_scores

    def grads_pair(p):
        kv_grad = dot(r.DKV[p, 0], r.N1[0].reshape(LENGTH, DIM)) + dot(
            r.DKV[p, 1], r.N1[1].reshape(LENGTH, DIM)
        )
        own_rows = r.N1O[...].reshape(CS * TOK, DIM)
        q_grad = dot_ta(r.DQ[p].reshape(CS * TOK, 128), own_rows)
        chip_grad(p, jnp.concatenate((q_grad, kv_grad), axis=0).astype(BF16).T)

    def grads_bias(p):
        for hh in range(2):
            both = r.PS[p, :, TOK * hh : TOK * hh + TOK, :].reshape(CS * TOK, LENGTH)
            padded = jnp.concatenate((dot(reverse2, both), jnp.zeros((TOK, TOK), F32)), axis=1)
            placed = pltpu.roll(padded, 0, 1, stride=1, stride_axis=0)
            r.DG[2 * p + hh : 2 * p + hh + 1, :] = jnp.sum(placed, axis=0, keepdims=True)

    w_kv = jnp.concatenate([r.WA[p].reshape(DIM, HALF)[:, 128:] for p in range(PAIRS)], axis=1)

    def token_grad(q, zz):
        lanes = pl.ds(pl.multiple_of(XS * TOK * zz, 128), XS * TOK)
        d_kv = r.DKV[:, q, :, lanes].reshape(PAIRS * 256, XS * TOK)
        out = dot(w_kv, d_kv)
        for xx in range(XS):
            r.DN[q, zz, xx] = out[:, TOK * xx : TOK * xx + TOK].astype(BF16)
        if zz is z:
            total = r.DN[q, z, x].astype(F32)
            for p in range(PAIRS):
                total = total + dot_tb(r.WA[p].reshape(DIM, HALF)[:, :128], r.DQ[p, q])
            r.DN[q, z, x] = total.astype(BF16)

    def token_exchange(zz):
        token_grad(co, zz)
        put(r.DN.at[co, zz], r.DNC.at[zz], to_core, k.dnc + zz)
        token_grad(c, zz)

    def token_to_x(zz):
        take(r.DNC.at[zz], k.dnc + zz)
        r.DN[c, zz] = (r.DN[c, zz].astype(F32) + r.DNC[zz].astype(F32)).astype(BF16)
        put(r.DN.at[c, zz, xo], r.DNX.at[zz], to_x, k.dnx + zz)

    def token_part(zz):
        return r.DN.at[c, zz, x]

    token_scatter = (r.DNZ, None if FAR_DIRECT_TOKEN else r.DNT, k.dnz, k.dnt)

    def token_chain():
        if not FAR_DIRECT_TOKEN:
            z_chain(token_part, *token_scatter)

    def token_to_z(i):
        zz = far_first[i]
        take(r.DNX.at[zz], k.dnx + zz)
        r.DN[c, zz, x] = (r.DN[c, zz, x].astype(F32) + r.DNX[zz].astype(F32)).astype(BF16)
        if i < 3:
            z_scatter(token_part, *token_scatter, 2 - i)

    def grads_down():
        cot_all = r.COT[...].reshape(4 * TOK, DIM)
        r.GD[...] = dot_ta(r.ACT[...].reshape(4 * TOK, QUARTER), cot_all).astype(BF16).reshape(
            ZS, YS, DOWN_ROWS, DIM
        )
        for zz in far_first:
            put(r.GD.at[zz, yo], r.GDY.at[zz], to_y, k.rdy + zz)

    def grads_gate():
        n2_all = r.N2[...].reshape(4 * TOK, DIM)
        d_gu_all = r.DGU[...].reshape(4 * TOK, 2 * QUARTER)
        r.GG[...] = dot_ta(n2_all, d_gu_all).astype(BF16).reshape(ZS, XS, YS, CHIP_ROWS, 2 * QUARTER)
        for zz in far_first:
            put(r.GG.at[zz, :, yo], r.GGY.at[zz], to_y, k.rgy + zz)

    def zeros():
        z_zero(r.GDZ)
        z_zero(r.GGZ)
        if not FAR_DIRECT_TOKEN:
            z_zero(r.DNZ)
        for ch in range(CHUNKS):
            if not FAR_DIRECT_CHIP[ch]:
                z_zero(r.GAZ.at[ch])

    def hidden_send():
        take(r.E2C.at[xo], k.e2c + xo)
        r.E2S[...] = (r.E2[xo, c].astype(F32) + r.E2C[xo].astype(F32)).astype(BF16)
        put(r.E2S, r.E2X, to_x, k.e2x)

    def hidden_back():
        take(r.E2C.at[x], k.e2c + x)
        take(r.E2X, k.e2x)
        e2 = r.E2[x, c].astype(F32) + r.E2C[x].astype(F32) + r.E2X[...].astype(F32)
        n2_own, r2 = unit_rows(r.H[...])
        r.DH[...] = r.cot[...].astype(F32) + r2 * (
            e2 - n2_own * jnp.mean(e2 * n2_own, axis=1, keepdims=True)
        )
        r.DB[c] = r.DH[...].astype(BF16)
        put(r.DB.at[c], r.DB.at[c], to_core, k.db)

    def mixed_send():
        take(r.MXC.at[xo], k.mxc + xo)
        r.MXS[...] = (r.MX[xo, c].astype(F32) + r.MXC[xo].astype(F32)).astype(BF16)
        put(r.MXS, r.MXX, to_x, k.mxx)

    def mixed_end():
        take(r.MXC.at[x], k.mxc + x)
        take(r.MXX, k.mxx)
        r.mixed[...] = (
            r.H[...] + r.MX[x, c].astype(F32) + r.MXC[x].astype(F32) + r.MXX[...].astype(F32)
        ).astype(BF16)

    def attended_back(q):
        if q is co:
            take(r.DB.at[co], k.db)
        rows = [r.WO[h, pl.ds(2 * c, 2)].reshape(HALF, HALF) for h in range(CS)]
        d_att = dot_tb(r.DB[q, :, :HALF], rows[0]) + dot_tb(r.DB[q, :, HALF:], rows[1])
        r.DO[q] = d_att.astype(BF16)

    def grads_output():
        take(r.ATT.at[co, co], k.att + 1)
        att_all = jnp.concatenate(
            [jnp.concatenate((r.ATT[0, q], r.ATT[1, q]), axis=1) for q in range(CS)], axis=0
        )
        db_cols = r.DB[:, :, pl.ds(pl.multiple_of(HALF * c, 128), HALF)].reshape(CS * TOK, HALF)
        chip_grad(PAIRS, dot_ta(att_all, db_cols))

    def table_start():
        r.DG[HEADS_HERE:, :] = jnp.zeros((8 - HEADS_HERE, SPAN), F32)
        onehot_back = (
            lax.broadcasted_iota(jnp.int32, (128, SPAN), 0)
            == r.BK[:, pl.ds(pl.multiple_of(LENGTH - TOK - TOK * s, 128), SPAN)]
        ).astype(F32)
        r.T1[...] = lax.dot_general(
            r.DG[...], onehot_back, (((1,), (1,)), ((), ())), precision=HIGHEST, preferred_element_type=F32
        )
        put(r.T1, r.TY, to_y, k.ty)

    def table_to_x():
        take(r.TY, k.ty)
        r.T2[...] = r.T1[...] + r.TY[...]
        put(r.T2, r.TX, to_x, k.tx)

    def table_to_z():
        take(r.TX, k.tx)
        r.T3[...] = r.T2[...] + r.TX[...]
        for who in to_z:
            put(r.T3, r.TZ.at[z], who, k.tz + z)
        r.TZ[z] = r.T3[...]

    def table_to_core():
        for zz in zord:
            take(r.TZ.at[zz], k.tz + zz)
        r.TO[c] = (r.TZ[0] + r.TZ[1]) + (r.TZ[2] + r.TZ[3])
        put(r.TO.at[c], r.TO.at[c], to_core, k.tc)

    def table_end():
        take(r.TO.at[co], k.tc)
        for q in range(CS):
            r.gtab[HEADS_HERE * q : HEADS_HERE * q + HEADS_HERE, :] = r.TO[q, :HEADS_HERE, :32]

    def down_end():
        r.gwd[...] = z_sum(r.GD[z, y], r.GDZ, k.rdz)

    def gate_to_x():
        total = z_sum(r.GG[z, :, y], r.GGZ, k.rgz)
        r.F4S[...] = total.astype(BF16)
        put(r.F4S.at[xo], r.F4X, to_x, k.f4x)

    def gate_to_core():
        take(r.F4X, k.f4x)
        r.F4S2[:, x] = r.F4S[x].astype(F32).reshape(CS, SHARD, 2 * QUARTER)
        r.F4S2[:, xo] = r.F4X[...].astype(F32).reshape(CS, SHARD, 2 * QUARTER)
        put(r.F4S2.at[co], r.F4.at[c], to_core, k.f4)
        r.F4[c] = r.F4S2[c]

    def gate_end():
        take(r.F4.at[co], k.f4)
        quarters = [r.F4[q % CS, q // CS] for q in range(BATCH_DEVICES)]
        gate_total = join_quarters([quarter[:, :QUARTER] for quarter in quarters])
        up_total = join_quarters([quarter[:, QUARTER:] for quarter in quarters])
        r.gwg[...] = gate_total * gain_f
        r.gwu[...] = up_total * gain_f
        r.ggf[...] = to_row(
            jnp.sum(
                gate_total * r.wg[...].astype(F32) + up_total * r.wu[...].astype(F32), axis=1, keepdims=True
            )
        )

    def token_end():
        e1 = z_sum(r.DN[c, z, x], r.DNZ, k.dnz, FAR_DIRECT_TOKEN).T
        n1_own, r1 = unit_rows(tok[...].astype(F32))
        r.tg[...] = (
            r.DH[...] + r1 * (e1 - n1_own * jnp.mean(e1 * n1_own, axis=1, keepdims=True))
        ).astype(BF16)

    def chip_out(ch):
        take(r.F2.at[ch, co], k.f2 + ch)
        if ch == PAIRS:
            for h in range(CS):
                r.gwo[:, HALF * h : HALF * h + HALF] = r.F2[ch, h]
            return
        gain_part = jnp.zeros((SHARD, 128), F32)
        for j, (w_ref, out_ref) in enumerate(((r.wq, r.gwq), (r.wk, r.gwk), (r.wv, r.gwv))):
            for h in range(CS):
                lanes = slice(HALF * h + 128 * ch, HALF * h + 128 * ch + 128)
                grad = r.F2[ch, h, :, 128 * j : 128 * j + 128]
                gain_part = gain_part + grad * w_ref[:, lanes].astype(F32)
                out_ref[:, lanes] = grad * gain_a
        r.GT[ch] = gain_part

    def gain_end():
        r.gga[...] = to_row(jnp.sum(r.GT[0] + r.GT[1] + r.GT[2], axis=1, keepdims=True))

    zeros()
    grads_down()
    hidden_send()
    down_from_y(0)
    grads_gate()
    mixed_send()
    hidden_back()
    down_from_y(2)
    attended_back(c)
    down_from_y(1)
    attend_back(2, c)
    attended_back(co)
    grads_output()
    attend_back(0, c)
    mixed_end()
    attend_back(2, co)
    down_from_y(3)
    down_chain()
    attend_back(1, co)
    grads_pair(2)
    gate_from_y(0)
    attend_back(0, co)
    grads_bias(2)
    attend_back(1, c)
    token_exchange(far_first[1])
    gate_from_y(1)
    chip_step1(PAIRS)
    down_end()
    token_exchange(far_first[0])
    grads_bias(1)
    grads_bias(0)
    table_start()
    token_to_x(far_first[1])
    gate_from_y(2)
    token_exchange(far_first[2])
    gate_chain()
    grads_pair(0)
    token_to_x(far_first[0])
    token_exchange(far_first[3])
    grads_pair(1)
    token_to_x(far_first[2])
    token_to_z(1)
    table_to_x()
    chip_step2(PAIRS)
    chip_step1(2)
    token_to_z(0)
    gate_from_y(3)
    chip_step1(0)
    chip_chain(PAIRS)
    table_to_z()
    token_to_x(far_first[3])
    token_to_z(2)
    chip_step2(0)
    token_chain()
    chip_end(PAIRS)
    chip_step1(1)
    chip_out(PAIRS)
    table_to_core()
    chip_step2(2)
    table_end()
    gate_to_x()
    token_to_z(3)
    chip_step2(1)
    chip_chain(0)
    token_end()
    chip_end(0)
    chip_chain(2)
    gate_to_core()
    chip_out(0)
    chip_chain(1)
    gate_end()
    chip_end(2)
    chip_end(1)
    chip_out(2)
    chip_out(1)
    gain_end()
    for i in range(len(sent) - SEND_RING, len(sent)):
        sent_wait(i)


def finish_kernel(*refs):
    count = len(refs) // 2
    for src, dst in zip(refs[:count], refs[count:]):
        dst[...] = src[...]


def fused_device(
    tokens, segments, buckets, gain_attn, w_query, w_key, w_value, w_output,
    gain_ffn, w_gate, w_up, w_down, bucket_bias_matrix, cotangent,
):
    operands = (
        tokens.reshape(TOK, DIM),
        cotangent.reshape(TOK, DIM),
        segments.reshape(1, LENGTH),
        buckets.reshape(1, 2 * LENGTH - 1),
        bucket_bias_matrix.T,
        gain_attn.reshape(1, SHARD),
        gain_ffn.reshape(1, SHARD),
        w_query, w_key, w_value, w_output, w_gate, w_up, w_down,
    )
    out_shape = [jax.ShapeDtypeStruct(shape, dtype) for shape, dtype in OUTPUTS.values()]
    in_vmem = pl.BlockSpec(memory_space=pltpu.VMEM)
    outs = pl.pallas_call(
        layer_kernel,
        out_shape=out_shape,
        in_specs=[in_vmem] * len(operands),
        out_specs=[in_vmem] * len(out_shape),
        scratch_shapes=[pltpu.VMEM(shape, dtype) for shape, dtype in SCRATCH.values()]
        + [pltpu.SemaphoreType.DMA((SEND_RING,)), pltpu.SemaphoreType.DMA((RECV_COUNT,))],
        compiler_params=pltpu.CompilerParams(
            collective_id=0, has_side_effects=True, vmem_limit_bytes=63 * 2**20
        ),
        name="layer",
    )(*operands)
    outs = pl.pallas_call(
        finish_kernel,
        out_shape=out_shape,
        in_specs=[in_vmem] * len(out_shape),
        out_specs=[in_vmem] * len(out_shape),
        name="finish",
    )(*outs)
    mixed, tokens_grad, gga, gwq, gwk, gwv, gwo, ggf, gwg, gwu, gwd, table_grad = outs
    return (
        mixed.reshape(tokens.shape), tokens_grad.reshape(tokens.shape), gga.reshape(SHARD),
        gwq, gwk, gwv, gwo, ggf.reshape(SHARD), gwg, gwu, gwd, table_grad.T,
    )


def fits_fused(mesh):
    return mesh.shape["seq"] == SEQ_DEVICES and mesh.shape["batch"] == BATCH_DEVICES


def solution(mesh):
    return jax.shard_map(
        fused_device if fits_fused(mesh) else on_device,
        mesh=mesh,
        in_specs=(
            P("seq", "batch", None),
            P(None, "batch"),
            P(),
            P(("seq", "batch")),
            P(("seq", "batch"), None),
            P(("seq", "batch"), None),
            P(("seq", "batch"), None),
            P(("seq", "batch"), None),
            P(("seq", "batch")),
            P(("seq", "batch"), None),
            P(("seq", "batch"), None),
            P(("seq", "batch"), None),
            P(),
            P("seq", "batch", None),
        ),
        out_specs=(
            P("seq", "batch", None),
            P("seq", "batch", None),
            P(("seq", "batch")),
            P(("seq", "batch"), None),
            P(("seq", "batch"), None),
            P(("seq", "batch"), None),
            P(("seq", "batch"), None),
            P(("seq", "batch")),
            P(("seq", "batch"), None),
            P(("seq", "batch"), None),
            P(("seq", "batch"), None),
            P(),
        ),
        check_vma=False,
    )
```

```python
from functools import partial
import math
from types import SimpleNamespace

import jax
import jax.numpy as jnp
from jax import lax
from jax.experimental import pallas as pl
from jax.experimental.pallas import tpu as pltpu
from jax.sharding import PartitionSpec as P

EPSILON = 1e-06
NEGATIVE = -1e30
HIGHEST = lax.Precision.HIGHEST


def normalize(hidden_state, scale_vec):
    return (
        hidden_state
        * lax.rsqrt(jnp.mean(hidden_state * hidden_state, axis=-1, keepdims=True) + EPSILON)
        * scale_vec
    )


def gelu_tanh(gate_vals):
    return jax.nn.gelu(gate_vals, approximate=True)


def project(left_side, weight):
    return jnp.einsum("tsk,kn->tsn", left_side, weight, preferred_element_type=jnp.float32)


def project_back(grad_rows, weight):
    return jnp.einsum("tsn,kn->tsk", grad_rows, weight, preferred_element_type=jnp.float32)


def weight_grad(left_side, grad_rows):
    return jnp.einsum("tsk,tsn->kn", left_side, grad_rows, preferred_element_type=jnp.float32)


def position_bias(
    buckets, bucket_bias_matrix, query_start, key_start, query_rows, key_rows, seq_length
):
    span = query_rows + key_rows - 1
    head_count = bucket_bias_matrix.shape[1]
    first = key_start - query_start + seq_length - query_rows
    chosen = lax.dynamic_slice_in_dim(buckets, first, span, 0)
    onehot = (
        chosen[:, None] == jnp.arange(bucket_bias_matrix.shape[0], dtype=jnp.int32)[None, :]
    ).astype(jnp.float32)
    per_offset = jnp.dot(onehot, bucket_bias_matrix.astype(jnp.float32), precision=HIGHEST)
    padded = jnp.concatenate((per_offset.T, jnp.zeros((head_count, 1), jnp.float32)), axis=1)
    tiled = jnp.broadcast_to(padded[:, None, :], (head_count, query_rows, span + 1)).reshape(
        head_count, query_rows * (span + 1)
    )
    skewed = tiled[:, : query_rows * span].reshape(head_count, query_rows, span)
    return (onehot, skewed[:, :, query_rows - 1 : query_rows - 1 + key_rows])


def table_term(onehot, score_gradient):
    summed = jnp.sum(score_gradient.astype(jnp.float32), axis=0)
    head_count, query_rows, key_rows = summed.shape
    span = query_rows + key_rows - 1
    placed = jnp.pad(summed, ((0, 0), (0, 0), (query_rows - 1, 0))).reshape(
        head_count, query_rows * span
    )
    placed = jnp.pad(placed, ((0, 0), (0, query_rows)))
    diagonal_sums = jnp.sum(placed.reshape(head_count, query_rows, span + 1), axis=1)[:, :span]
    return jnp.dot(onehot.T, diagonal_sums.T, precision=HIGHEST)


def pair_scores(table_set, query_block, query_segs, query_start, key_block, key_segs, key_start):
    buckets, bucket_bias_matrix, seq_length = table_set
    onehot, bias_contributions = position_bias(
        buckets,
        bucket_bias_matrix,
        query_start,
        key_start,
        query_block.shape[0],
        key_block.shape[0],
        seq_length,
    )
    scores = (
        jnp.einsum("qshd,kshd->shqk", query_block, key_block, preferred_element_type=jnp.float32)
        + bias_contributions[None]
    )
    allowed = (query_segs.T[:, :, None] == key_segs.T[:, None, :])[:, None]
    return (onehot, scores, allowed)


def pair_grads(
    table_set,
    query_block,
    query_segs,
    query_start,
    dout_block,
    log_sums,
    deltas,
    key_block,
    value_block,
    key_segs,
    key_start,
):
    onehot, scores, allowed = pair_scores(
        table_set, query_block, query_segs, query_start, key_block, key_segs, key_start
    )
    probabilities = jnp.where(allowed, jnp.exp(scores - log_sums[..., None]), 0.0)
    dprobs = jnp.einsum(
        "qshd,kshd->shqk", dout_block, value_block, preferred_element_type=jnp.float32
    )
    score_gradient = (probabilities * (dprobs - deltas[..., None])).astype(jnp.bfloat16)
    return (onehot, probabilities, score_gradient)


def attend_block(setting, carried, blocks, key_start):
    table_set, segments, query_heads, query_segs, query_start = setting
    running_max, running_sum, accum = carried
    key_block, value_block = blocks
    key_segs = lax.dynamic_slice_in_dim(segments, key_start, key_block.shape[0], 0)
    _, scores, allowed = pair_scores(
        table_set, query_heads, query_segs, query_start, key_block, key_segs, key_start
    )
    new_max = jnp.maximum(running_max, jnp.max(jnp.where(allowed, scores, NEGATIVE), axis=-1))
    weights_raw = jnp.where(allowed, jnp.exp(scores - new_max[..., None]), 0.0)
    factor = jnp.exp(running_max - new_max)
    running_sum = running_sum * factor + jnp.sum(weights_raw, axis=-1)
    accum = accum * jnp.transpose(factor, (2, 0, 1))[..., None] + jnp.einsum(
        "shqk,kshd->qshd",
        weights_raw.astype(jnp.bfloat16),
        value_block,
        preferred_element_type=jnp.float32,
    )
    return (new_max, running_sum, accum)


def merged_block(setting, extras, carried, scan_item):
    table_set, segments, query_heads, query_segs, query_start = setting
    dout_heads, log_sums, deltas = extras
    dquery, dtable = carried
    key_start, key_block, value_block = scan_item
    key_rows = key_block.shape[0]
    seq_count = key_block.shape[1]
    key_segs = lax.dynamic_slice_in_dim(segments, key_start, key_rows, 0)
    onehot, probabilities, score_gradient = pair_grads(
        table_set,
        query_heads,
        query_segs,
        query_start,
        dout_heads,
        log_sums,
        deltas,
        key_block,
        value_block,
        key_segs,
        key_start,
    )
    dquery = dquery + jnp.einsum(
        "shqk,kshd->qshd", score_gradient, key_block, preferred_element_type=jnp.float32
    )
    dtable = dtable + table_term(onehot, score_gradient)
    key_gradient = jnp.einsum(
        "shqk,qshd->kshd", score_gradient, query_heads, preferred_element_type=jnp.float32
    )
    dvalue = jnp.einsum(
        "shqk,qshd->kshd",
        probabilities.astype(jnp.bfloat16),
        dout_heads,
        preferred_element_type=jnp.float32,
    )
    joined = jnp.concatenate(
        (key_gradient.reshape(key_rows, seq_count, -1), dvalue.reshape(key_rows, seq_count, -1)),
        axis=2,
    )
    return ((dquery, dtable), joined)


def fold_blocks(step_fn, carried, pieces):
    piece_rows = pieces[0].shape[0]
    block_rows = math.gcd(piece_rows, 512)
    block_count = piece_rows // block_rows
    stacked = tuple(
        (piece.reshape((block_count, block_rows) + piece.shape[1:]) for piece in pieces)
    )

    def advance(state_now, scan_item):
        block_index, blocks = scan_item
        return (step_fn(state_now, blocks, block_index * block_rows), None)

    result, _ = lax.scan(advance, carried, (jnp.arange(block_count, dtype=jnp.int32), stacked))
    return result


def on_device(
    tokens,
    segments,
    buckets,
    gain_attn,
    w_query,
    w_key,
    w_value,
    w_output,
    gain_ffn,
    w_gate,
    w_up,
    w_down,
    bucket_bias_matrix,
    cotangent,
):
    tok_rows, seq_count, _ = tokens.shape
    head_count = bucket_bias_matrix.shape[1]
    inner_width = w_query.shape[1]
    head_width = inner_width // head_count
    head_shape = (tok_rows, seq_count, head_count, head_width)
    seq_length = (buckets.shape[0] + 1) // 2
    query_start = lax.axis_index("seq") * tok_rows
    (
        full_gain_attn,
        full_query,
        full_key,
        full_value,
        full_output,
        full_gain_ffn,
        full_gate,
        full_up,
        full_down,
    ) = (
        lax.all_gather(gain_attn, ("seq", "batch"), axis=0, tiled=True),
        lax.all_gather(w_query, ("seq", "batch"), axis=0, tiled=True),
        lax.all_gather(w_key, ("seq", "batch"), axis=0, tiled=True),
        lax.all_gather(w_value, ("seq", "batch"), axis=0, tiled=True),
        lax.all_gather(w_output, ("seq", "batch"), axis=0, tiled=True),
        lax.all_gather(gain_ffn, ("seq", "batch"), axis=0, tiled=True),
        lax.all_gather(w_gate, ("seq", "batch"), axis=0, tiled=True),
        lax.all_gather(w_up, ("seq", "batch"), axis=0, tiled=True),
        lax.all_gather(w_down, ("seq", "batch"), axis=0, tiled=True),
    )
    tokens_full = tokens.astype(jnp.float32)
    normed1 = normalize(tokens_full, full_gain_attn.astype(jnp.float32)).astype(jnp.bfloat16)
    query_heads = project(normed1, full_query).astype(jnp.bfloat16).reshape(head_shape)
    key_heads = project(normed1, full_key).astype(jnp.bfloat16).reshape(head_shape)
    value_heads = project(normed1, full_value).astype(jnp.bfloat16).reshape(head_shape)
    query_segs = lax.dynamic_slice_in_dim(segments, query_start, tok_rows, 0)
    table_set = (buckets, bucket_bias_matrix, seq_length)
    setting = (table_set, segments, query_heads, query_segs, query_start)
    start_state = (
        jnp.full((seq_count, head_count, tok_rows), NEGATIVE, jnp.float32),
        jnp.zeros((seq_count, head_count, tok_rows), jnp.float32),
        jnp.zeros(head_shape, jnp.float32),
    )
    step_forward = partial(attend_block, setting)
    running_max, running_sum, accum = fold_blocks(
        step_forward,
        start_state,
        (
            lax.all_gather(key_heads, "seq", axis=0, tiled=True),
            lax.all_gather(value_heads, "seq", axis=0, tiled=True),
        ),
    )
    attended_full = accum / jnp.transpose(running_sum, (2, 0, 1))[..., None]
    log_sums = running_max + jnp.log(running_sum)
    attended = attended_full.astype(jnp.bfloat16).reshape(tok_rows, seq_count, inner_width)
    hidden1 = tokens_full + project(attended, full_output)
    normed2 = normalize(hidden1, full_gain_ffn.astype(jnp.float32)).astype(jnp.bfloat16)
    gate = project(normed2, full_gate)
    up_val = project(normed2, full_up)
    gelu_out, gelu_pull = jax.vjp(gelu_tanh, gate)
    activated = (gelu_out * up_val).astype(jnp.bfloat16)
    mixed = (hidden1 + project(activated, full_down)).astype(jnp.bfloat16)
    (
        full_gain_attn,
        full_query,
        full_key,
        full_value,
        full_output,
        full_gain_ffn,
        full_gate,
        full_up,
        full_down,
    ) = (
        lax.all_gather(gain_attn, ("seq", "batch"), axis=0, tiled=True),
        lax.all_gather(w_query, ("seq", "batch"), axis=0, tiled=True),
        lax.all_gather(w_key, ("seq", "batch"), axis=0, tiled=True),
        lax.all_gather(w_value, ("seq", "batch"), axis=0, tiled=True),
        lax.all_gather(w_output, ("seq", "batch"), axis=0, tiled=True),
        lax.all_gather(gain_ffn, ("seq", "batch"), axis=0, tiled=True),
        lax.all_gather(w_gate, ("seq", "batch"), axis=0, tiled=True),
        lax.all_gather(w_up, ("seq", "batch"), axis=0, tiled=True),
        lax.all_gather(w_down, ("seq", "batch"), axis=0, tiled=True),
    )
    grad_down = weight_grad(activated, cotangent)
    d_activated = project_back(cotangent, full_down)
    d_gate = gelu_pull(d_activated * up_val)[0].astype(jnp.bfloat16)
    d_up = (gelu_out * d_activated).astype(jnp.bfloat16)
    grad_gate = weight_grad(normed2, d_gate)
    grad_up = weight_grad(normed2, d_up)
    d_normed2 = project_back(d_gate, full_gate) + project_back(d_up, full_up)
    _, norm_pull2 = jax.vjp(normalize, hidden1, full_gain_ffn.astype(jnp.float32))
    d_hidden_part, grad_gain_ffn = norm_pull2(d_normed2)
    d_hidden1 = cotangent.astype(jnp.float32) + d_hidden_part
    d_branch = d_hidden1.astype(jnp.bfloat16)
    grad_output = weight_grad(attended, d_branch)
    dout_heads = project_back(d_branch, full_output).astype(jnp.bfloat16).reshape(head_shape)
    deltas = jnp.transpose(
        jnp.sum(dout_heads.astype(jnp.float32) * attended_full, axis=-1), (1, 2, 0)
    )
    extras = (dout_heads, log_sums, deltas)
    keys_all, values_all = (
        lax.all_gather(key_heads, "seq", axis=0, tiled=True),
        lax.all_gather(value_heads, "seq", axis=0, tiled=True),
    )
    block_rows = math.gcd(seq_length, 512)
    block_count = seq_length // block_rows
    stacked_keys = keys_all.reshape((block_count, block_rows) + keys_all.shape[1:])
    stacked_values = values_all.reshape((block_count, block_rows) + values_all.shape[1:])
    block_starts = jnp.arange(block_count, dtype=jnp.int32) * block_rows
    query_init = (
        jnp.zeros(head_shape, jnp.float32),
        jnp.zeros(bucket_bias_matrix.shape, jnp.float32),
    )
    (dquery, dtable), joined_all = lax.scan(
        partial(merged_block, setting, extras),
        query_init,
        (block_starts, stacked_keys, stacked_values),
    )
    every_key_contribution = joined_all.reshape(seq_length, seq_count, 2 * inner_width)
    key_sums = lax.psum_scatter(every_key_contribution, "seq", scatter_dimension=0, tiled=True)
    dkey_rows = key_sums[:, :, :inner_width].astype(jnp.bfloat16)
    dvalue_rows = key_sums[:, :, inner_width:].astype(jnp.bfloat16)
    dquery_rows = dquery.reshape(tok_rows, seq_count, inner_width).astype(jnp.bfloat16)
    grad_query = weight_grad(normed1, dquery_rows)
    grad_key = weight_grad(normed1, dkey_rows)
    grad_value = weight_grad(normed1, dvalue_rows)
    d_normed1 = (
        project_back(dquery_rows, full_query)
        + project_back(dkey_rows, full_key)
        + project_back(dvalue_rows, full_value)
    )
    _, norm_pull1 = jax.vjp(normalize, tokens_full, full_gain_attn.astype(jnp.float32))
    d_input_part, grad_gain_attn = norm_pull1(d_normed1)
    tokens_grad = (d_hidden1 + d_input_part).astype(jnp.bfloat16)
    owned = (
        lax.psum_scatter(grad_gain_attn, ("seq", "batch"), scatter_dimension=0, tiled=True),
        lax.psum_scatter(grad_query, ("seq", "batch"), scatter_dimension=0, tiled=True),
        lax.psum_scatter(grad_key, ("seq", "batch"), scatter_dimension=0, tiled=True),
        lax.psum_scatter(grad_value, ("seq", "batch"), scatter_dimension=0, tiled=True),
        lax.psum_scatter(grad_output, ("seq", "batch"), scatter_dimension=0, tiled=True),
        lax.psum_scatter(grad_gain_ffn, ("seq", "batch"), scatter_dimension=0, tiled=True),
        lax.psum_scatter(grad_gate, ("seq", "batch"), scatter_dimension=0, tiled=True),
        lax.psum_scatter(grad_up, ("seq", "batch"), scatter_dimension=0, tiled=True),
        lax.psum_scatter(grad_down, ("seq", "batch"), scatter_dimension=0, tiled=True),
    )
    table_total = lax.psum(dtable, ("seq", "batch"))
    return (
        mixed,
        tokens_grad,
        owned[0],
        owned[1],
        owned[2],
        owned[3],
        owned[4],
        owned[5],
        owned[6],
        owned[7],
        owned[8],
        table_total,
    )


BF16 = jnp.bfloat16
F32 = jnp.float32
MESH_IDS = pl.DeviceIdType.MESH

ZS, XS, YS, CS = 4, 2, 2, 2
SEQ_DEVICES = ZS * XS
BATCH_DEVICES = YS * CS
TOK = 128
LENGTH = SEQ_DEVICES * TOK
DIM = 768
HALF = DIM // CS
PAIRS = HALF // 128
SHARD = DIM // (SEQ_DEVICES * BATCH_DEVICES)
CHIP_ROWS = SHARD * CS
GROUP_ROWS = SHARD * BATCH_DEVICES
FF_ALL = 2048
QUARTER = FF_ALL // BATCH_DEVICES
DOWN_ROWS = FF_ALL // (SEQ_DEVICES * BATCH_DEVICES)
CHUNKS = PAIRS + 1
SPAN = LENGTH + TOK
HEADS_HERE = 2 * PAIRS


def dot(a, b):
    return lax.dot_general(a, b, (((1,), (0,)), ((), ())), preferred_element_type=F32)


def dot_tb(a, b):
    return lax.dot_general(a, b, (((1,), (1,)), ((), ())), preferred_element_type=F32)


def dot_ta(a, b):
    return lax.dot_general(a, b, (((0,), (0,)), ((), ())), preferred_element_type=F32)


def to_column(row):
    n = row.shape[1]
    eye = lax.broadcasted_iota(jnp.int32, (n, n), 0) == lax.broadcasted_iota(jnp.int32, (n, n), 1)
    return jnp.sum(jnp.where(eye, jnp.broadcast_to(row, (n, n)), 0.0), axis=1, keepdims=True)


def to_row(col):
    n = col.shape[0]
    eye = lax.broadcasted_iota(jnp.int32, (n, n), 0) == lax.broadcasted_iota(jnp.int32, (n, n), 1)
    return jnp.sum(jnp.where(eye, jnp.broadcast_to(col, (n, n)), 0.0), axis=0, keepdims=True)


def unit_rows(x):
    r = lax.rsqrt(jnp.mean(x * x, axis=1, keepdims=True) + EPSILON)
    return x * r, r


def stack_heads(pair):
    low = lax.broadcasted_iota(jnp.int32, pair.shape, 1) < 64
    return jnp.concatenate((jnp.where(low, pair, 0.0), jnp.where(low, 0.0, pair)), axis=0).astype(BF16)


def unstack_heads(stacked):
    rows = stacked.shape[0] // 2
    low = lax.broadcasted_iota(jnp.int32, (rows, 128), 1) < 64
    return jnp.where(low, stacked[:rows], stacked[rows:])


def split_quarters(whole):
    low = lax.broadcasted_iota(jnp.int32, (whole.shape[0], 128), 1) < 64
    parts = []
    for q in range(BATCH_DEVICES):
        cols = []
        for m in range(ZS):
            first = 4 * m + 2 * (q // 2)
            a = whole[:, 128 * first : 128 * first + 128]
            b = whole[:, 128 * (first + 1) : 128 * (first + 1) + 128]
            if q % 2 == 0:
                cols.append(jnp.where(low, a, pltpu.roll(b, 64, 1)))
            else:
                cols.append(jnp.where(low, pltpu.roll(a, 64, 1), b))
        parts.append(jnp.concatenate(cols, axis=1))
    return parts


def join_quarters(parts):
    low = lax.broadcasted_iota(jnp.int32, (parts[0].shape[0], 128), 1) < 64
    cols = []
    for block in range(FF_ALL // 128):
        m, xx, yy = block // 4, block // 2 % 2, block % 2
        lanes = slice(128 * m, 128 * m + 128)
        a, b = parts[2 * xx][:, lanes], parts[2 * xx + 1][:, lanes]
        if yy == 0:
            cols.append(jnp.where(low, a, pltpu.roll(b, 64, 1)))
        else:
            cols.append(jnp.where(low, pltpu.roll(a, 64, 1), b))
    return jnp.concatenate(cols, axis=1)


SCRATCH = dict(
    W_MINE=((CS, SHARD, 4 * HALF + 4 * QUARTER), F32),
    W_CORE=((CS, SHARD, 4 * HALF + 4 * QUARTER), F32),
    UB=((XS, CHIP_ROWS, 2 * QUARTER), BF16),
    WA=((PAIRS, ZS, XS, YS, CHIP_ROWS, HALF), BF16),
    WO=((CS, ZS, XS, YS, CHIP_ROWS, HALF), BF16),
    WG=((ZS, XS, YS, CHIP_ROWS, 2 * QUARTER), BF16),
    WD=((ZS, YS, DOWN_ROWS, DIM), BF16),
    X=((CS, ZS, XS, TOK, DIM), BF16),
    N1=((CS, ZS, XS, TOK, DIM), BF16),
    N1O=((CS, TOK, DIM), BF16),
    COT=((XS, CS, TOK, DIM), BF16),
    SEG=((CS, 8, LENGTH), F32),
    BK=((1, 2 * LENGTH), jnp.int32),
    PH=((2 * CS * PAIRS, SPAN), F32),
    BIAS=((PAIRS, 2 * TOK, LENGTH), BF16),
    MASK=((CS, TOK, LENGTH), BF16),
    KV=((PAIRS, CS, LENGTH, 256), BF16),
    QS=((PAIRS, CS, 2 * TOK, 128), BF16),
    PS=((PAIRS, CS, 2 * TOK, LENGTH), BF16),
    ATT=((CS, CS, TOK, HALF), BF16),
    H=((TOK, DIM), F32),
    N2=((XS, CS, TOK, DIM), BF16),
    ACT=((XS, 2 * TOK, QUARTER), BF16),
    DGU=((XS, 2 * TOK, 2 * QUARTER), BF16),
    MX=((XS, CS, TOK, DIM), BF16),
    MXC=((XS, TOK, DIM), BF16),
    MXS=((TOK, DIM), BF16),
    MXX=((TOK, DIM), BF16),
    E2=((XS, CS, TOK, DIM), BF16),
    E2C=((XS, TOK, DIM), BF16),
    E2S=((TOK, DIM), BF16),
    E2X=((TOK, DIM), BF16),
    GG=((ZS, XS, YS, CHIP_ROWS, 2 * QUARTER), BF16),
    GGY=((ZS, XS, CHIP_ROWS, 2 * QUARTER), BF16),
    GGZ=((ZS, XS, CHIP_ROWS, 2 * QUARTER), BF16),
    GGC=((XS, CHIP_ROWS, 2 * QUARTER), BF16),
    GD=((ZS, YS, DOWN_ROWS, DIM), BF16),
    GDY=((ZS, DOWN_ROWS, DIM), BF16),
    GDZ=((ZS, DOWN_ROWS, DIM), BF16),
    GDC=((DOWN_ROWS, DIM), BF16),
    F4S=((XS, CHIP_ROWS, 2 * QUARTER), BF16),
    F4X=((CHIP_ROWS, 2 * QUARTER), BF16),
    F4S2=((CS, XS, SHARD, 2 * QUARTER), F32),
    F4=((CS, XS, SHARD, 2 * QUARTER), F32),
    DH=((TOK, DIM), F32),
    DB=((CS, TOK, DIM), BF16),
    DO=((CS, TOK, HALF), BF16),
    DQ=((PAIRS, CS, TOK, 128), BF16),
    DKV=((PAIRS, CS, 256, LENGTH), BF16),
    DG=((8, SPAN), F32),
    GA=((CHUNKS, ZS, XS, YS, CHIP_ROWS, HALF), BF16),
    GA1=((CHUNKS, ZS, 2, CHIP_ROWS, HALF), BF16),
    GA2=((CHUNKS, ZS, CHIP_ROWS, HALF), BF16),
    GAZ=((CHUNKS, ZS, CHIP_ROWS, HALF), BF16),
    GAC=((CHUNKS, CHIP_ROWS, HALF), BF16),
    FA=((CHUNKS, CS, SHARD, HALF), F32),
    F2=((CHUNKS, CS, SHARD, HALF), F32),
    GT=((PAIRS, SHARD, 128), F32),
    DN=((CS, ZS, XS, DIM, TOK), BF16),
    DNC=((ZS, XS, DIM, TOK), BF16),
    DNX=((ZS, DIM, TOK), BF16),
    DNZ=((ZS, DIM, TOK), BF16),
    DNT=((DIM, TOK), BF16),
    T1=((8, 128), F32),
    TY=((8, 128), F32),
    T2=((8, 128), F32),
    TX=((8, 128), F32),
    T3=((8, 128), F32),
    TZ=((ZS, 8, 128), F32),
    TO=((CS, 8, 128), F32),
)
SEND_RING = 72
SLOTS = dict(
    segc=1, wc=1, u=1, xz=4, xx=4, xc=8, wz=4 * CHUNKS, wx=4 * CHUNKS, wy=4 * CHUNKS, wr=CHUNKS, woc=1,
    gz=8, gy=8, dz=4, dy=4, cotx=1, cotc=2, att=2, n2x=1, n2c=2, mxc=2, mxx=1, e2c=2, e2x=1,
    rdy=4, rdz=4, rdc=1, rgy=4, rgz=4, rgc=1, f4x=1, f4=1, db=1,
    ra1=2 * CHUNKS, ra2=CHUNKS, raz=4 * CHUNKS, rac=CHUNKS, f2=CHUNKS,
    dnc=4, dnx=4, dnz=4, dnt=1, ty=1, tx=1, tz=4, tc=1,
)
RECV_COUNT = sum(SLOTS.values())


def slot_bases():
    bases, used = {}, 0
    for name, count in SLOTS.items():
        bases[name] = used
        used += count
    return SimpleNamespace(**bases)


INPUTS = dict(
    tok=0, cot=0, seg=0, buckets=0, table=0, ga=0, gf=0, wq=0, wk=0, wv=0, wo=0, wg=0, wu=0, wd=0
)
OUTPUTS = dict(
    mixed=((TOK, DIM), BF16), tg=((TOK, DIM), BF16), gga=((1, SHARD), F32),
    gwq=((SHARD, DIM), F32), gwk=((SHARD, DIM), F32), gwv=((SHARD, DIM), F32), gwo=((SHARD, DIM), F32),
    ggf=((1, SHARD), F32), gwg=((SHARD, FF_ALL), F32), gwu=((SHARD, FF_ALL), F32),
    gwd=((DOWN_ROWS, DIM), F32), gtab=((2 * CS * PAIRS, 32), F32),
)


RELAY_TO_Y = (True, True, False, False)
HEAVY_X = (False, False, True, True)
FAR_DIRECT_CHIP = (False, False, False, False)
FAR_DIRECT_TOKEN = False
SPREAD_TOKEN = False
SPREAD_CHIP = (False, False, False, False)
SPREAD_GATE = False
SPREAD_DOWN = False


def layer_kernel(*refs):
    names = (*INPUTS, *OUTPUTS, *SCRATCH)
    r = SimpleNamespace(**dict(zip(names, refs[:-2], strict=True)))
    ssem, rsem = refs[-2:]
    k = slot_bases()
    s, b = lax.axis_index("seq"), lax.axis_index("batch")
    z, x = s // XS, s % XS
    y, c = b // CS, b % CS
    xo, yo, co = 1 - x, 1 - y, 1 - c
    side = z // 2
    m = z + side * (3 - 2 * z)
    at_end, beside = m == 0, m == 1
    zord = [near + side * (3 - 2 * near) for near in (1 - m, 2, 3)]

    def at(zz, xx, yy, cc):
        return (XS * zz + xx, CS * yy + cc)

    to_core, to_x, to_y = at(z, x, y, co), at(z, xo, y, c), at(z, x, yo, c)
    to_z = [at(zz, x, y, c) for zz in zord]

    barrier = pltpu.get_barrier_semaphore()
    friends = [to_core, to_x, to_y] + to_z
    for who in friends:
        pl.semaphore_signal(barrier, inc=1, device_id=who, device_id_type=MESH_IDS)

    sent = []

    def sent_wait(i):
        copy, when = sent[i]
        if when is None:
            copy.wait_send()
        else:
            pl.when(when)(copy.wait_send)

    def put(src, dst, who, slot, when=None):
        if len(sent) >= SEND_RING:
            sent_wait(len(sent) - SEND_RING)
        copy = pltpu.make_async_remote_copy(
            src_ref=src, dst_ref=dst, send_sem=ssem.at[len(sent) % SEND_RING], recv_sem=rsem.at[slot],
            device_id=who, device_id_type=MESH_IDS,
        )
        if when is None:
            copy.start()
        else:
            pl.when(when)(copy.start)
        sent.append((copy, when))

    def take(dst, slot, when=None):
        wait = pltpu.make_async_remote_copy(
            src_ref=dst, dst_ref=dst, send_sem=ssem.at[0], recv_sem=rsem.at[slot],
            device_id=to_core, device_id_type=MESH_IDS,
        ).wait_recv
        if when is None:
            wait()
        else:
            pl.when(when)(wait)

    def z_send(src, dst, slot, direct):
        put(src, dst, to_z[0], slot + z)
        put(src, dst, to_z[1], slot + z)
        put(src, dst, to_z[2], slot + z, when=None if direct else beside)

    def z_take(block, slot, i, direct):
        zz = zord[i]
        take(block(zz), slot + zz)
        if i == 2 and not direct:
            put(block(zz), block(zz), to_z[0], slot + zz, when=beside)

    def z_scatter(part, land, chain, slot, chain_slot, i):
        if i == 2 and chain is None:
            put(part(zord[2]), land.at[z], to_z[2], slot + z)
        elif i == 2:
            put(part(zord[2]), chain, to_z[0], chain_slot, when=at_end)
        else:
            put(part(zord[i]), land.at[z], to_z[i], slot + z)

    def z_chain(part, land, chain, slot, chain_slot):
        @pl.when(beside)
        def _():
            take(chain, chain_slot)
            mine = part(zord[2])
            mine[...] = (mine[...].astype(F32) + chain[...].astype(F32)).astype(BF16)

        put(part(zord[2]), land.at[z], to_z[2], slot + z, when=beside)

    def z_zero(land):
        @pl.when(at_end)
        def _():
            land[zord[2]] = jnp.zeros(land.shape[1:], land.dtype)

    def z_sum(own, land, slot, direct=False):
        take(land.at[zord[0]], slot + zord[0])
        take(land.at[zord[1]], slot + zord[1])
        take(land.at[zord[2]], slot + zord[2], when=None if direct else beside)
        total = own.astype(F32)
        for zz in zord:
            total = total + land[zz].astype(F32)
        return total

    gain_a = to_column(r.ga[...].astype(F32))
    gain_f = to_column(r.gf[...].astype(F32))
    tok = r.tok
    r.SEG[c] = jnp.broadcast_to(r.seg[...].astype(F32), (8, LENGTH))
    for h in range(CS):
        for p in range(PAIRS):
            for j, w_ref in enumerate((r.wq, r.wk, r.wv)):
                lanes = slice(HALF * h + 128 * p, HALF * h + 128 * p + 128)
                r.W_MINE[h, :, HALF * p + 128 * j : HALF * p + 128 * j + 128] = (
                    w_ref[:, lanes].astype(F32) * gain_a
                )
        r.W_MINE[h, :, 3 * HALF : 4 * HALF] = r.wo[:, HALF * h : HALF * h + HALF].astype(F32)
    for j, w_ref in enumerate((r.wg, r.wu)):
        for q, part in enumerate(split_quarters(w_ref[...].astype(F32) * gain_f)):
            first = 4 * HALF + 2 * QUARTER * (q // CS) + QUARTER * j
            r.W_MINE[q % CS, :, first : first + QUARTER] = part

    pl.semaphore_wait(barrier, len(friends))

    put(r.W_MINE.at[co], r.W_CORE.at[c], to_core, k.wc)
    put(tok, r.X.at[c, z, x], to_x, k.xx + z)
    put(r.SEG.at[c], r.SEG.at[c], to_core, k.segc)
    put(tok, r.X.at[c, z, x], to_core, k.xc + s)
    r.X[c, z, x] = tok[...]
    r.WD[z, y] = r.wd[...]
    r.W_CORE[c] = r.W_MINE[c]

    def weight(ch):
        return r.WA.at[ch] if ch < PAIRS else r.WO.at[c]

    def weight_start(ch):
        own = weight(ch).at[z, x, y]
        z_send(own, own, k.wz + 4 * ch, SPREAD_CHIP[ch])
        put(own, own, to_y, k.wy + 4 * ch + z)
        put(own, own, to_x, k.wx + 4 * ch + z)

    def norm_block(q, zz, xx, own=False):
        value = unit_rows(r.X[q, zz, xx].astype(F32))[0].astype(BF16)
        r.N1[q, zz, xx] = value
        if own:
            r.N1O[q] = value

    def token_from_z(i):
        z_take(lambda zz: r.X.at[c, zz, x], k.xz, i, SPREAD_TOKEN)
        zz = zord[i]
        put(r.X.at[c, zz, x], r.X.at[c, zz, x], to_x, k.xx + zz)
        put(r.X.at[c, zz, x], r.X.at[c, zz, x], to_core, k.xc + XS * zz + x)
        norm_block(c, zz, x)

    def token_from_x(zz):
        take(r.X.at[c, zz, xo], k.xx + zz)
        put(r.X.at[c, zz, xo], r.X.at[c, zz, xo], to_core, k.xc + XS * zz + xo)
        norm_block(c, zz, xo)

    def token_from_core(zz, xx):
        take(r.X.at[co, zz, xx], k.xc + XS * zz + xx)
        norm_block(co, zz, xx, own=zz is z and xx is x)

    def bias_lines():
        r.BK[...] = jnp.zeros(r.BK.shape, jnp.int32)
        r.BK[:, : 2 * LENGTH - 1] = r.buckets[...]
        onehot = (
            lax.broadcasted_iota(jnp.int32, (32, SPAN), 0)
            == r.BK[:, pl.ds(pl.multiple_of(LENGTH - TOK - TOK * s, 128), SPAN)]
        )
        r.PH[...] = dot(r.table[...], onehot.astype(BF16))

    def bias_pair(p):
        for hh in range(2):
            line = r.PH[pl.ds(HEADS_HERE * c + 2 * p + hh, 1), :]
            skewed = pltpu.roll(
                jnp.broadcast_to(line, (TOK, SPAN)), SPAN - TOK + 1, 1, stride=1, stride_axis=0
            )
            r.BIAS[p, TOK * hh : TOK * hh + TOK, :] = skewed[:, :LENGTH].astype(BF16)

    def masks():
        take(r.SEG.at[co], k.segc)
        for q in range(CS):
            col = to_column(r.SEG[q, 0:1, pl.ds(pl.multiple_of(TOK * s, 128), TOK)])
            r.MASK[q] = jnp.where(col == r.SEG[q, 0:1, :], 0.0, NEGATIVE).astype(BF16)

    def weight_from_z(ch, i):
        w = weight(ch)
        z_take(lambda zz: w.at[zz, x, y], k.wz + 4 * ch, i, SPREAD_CHIP[ch])
        arrived = w.at[zord[i], x, y]
        put(arrived, arrived, to_y, k.wy + 4 * ch + zord[i])
        put(arrived, arrived, to_x, k.wx + 4 * ch + zord[i])

    def weight_relay(ch):
        w = weight(ch)
        for zz in [z] + zord:
            if RELAY_TO_Y[ch]:
                take(w.at[zz, xo, y], k.wx + 4 * ch + zz)
            else:
                take(w.at[zz, x, yo], k.wy + 4 * ch + zz)
        if RELAY_TO_Y[ch]:
            put(w.at[:, xo, y], w.at[:, xo, y], to_y, k.wr + ch)
        else:
            put(w.at[:, x, yo], w.at[:, x, yo], to_x, k.wr + ch)

    def weight_end(ch):
        w = weight(ch)
        for zz in [z] + zord:
            if RELAY_TO_Y[ch]:
                take(w.at[zz, x, yo], k.wy + 4 * ch + zz)
            else:
                take(w.at[zz, xo, y], k.wx + 4 * ch + zz)
        take(w.at[:, xo, yo], k.wr + ch)

    def gate_send(xx):
        own = r.WG.at[z, xx, y]
        z_send(own, own, k.gz + 4 * xx, SPREAD_GATE)
        put(own, own, to_y, k.gy + 4 * xx + z)

    def gate_from_z(xx, i):
        z_take(lambda zz: r.WG.at[zz, xx, y], k.gz + 4 * xx, i, SPREAD_GATE)
        arrived = r.WG.at[zord[i], xx, y]
        put(arrived, arrived, to_y, k.gy + 4 * xx + zord[i])

    def down_from_z(i):
        z_take(lambda zz: r.WD.at[zz, y], k.dz, i, SPREAD_DOWN)
        put(r.WD.at[zord[i], y], r.WD.at[zord[i], y], to_y, k.dy + zord[i])

    def tokens_send(i):
        far = beside if i == 2 and not SPREAD_TOKEN else None
        put(tok, r.X.at[c, z, x], to_z[i], k.xz + z, when=far)

    def down_send():
        put(r.wd, r.WD.at[z, y], to_y, k.dy + z)
        z_send(r.wd, r.WD.at[z, y], k.dz, SPREAD_DOWN)

    def shards():
        take(r.W_CORE.at[co], k.wc)
        shard = r.W_CORE[...].reshape(CHIP_ROWS, 4 * HALF + 4 * QUARTER).astype(BF16)
        for ch in range(PAIRS):
            r.WA[ch, z, x, y] = shard[:, HALF * ch : HALF * ch + HALF]
        r.WO[c, z, x, y] = shard[:, 3 * HALF : 4 * HALF]
        for xx in range(XS):
            first = 4 * HALF + 2 * QUARTER * xx
            r.UB[xx] = shard[:, first : first + 2 * QUARTER]
        r.WG[z, x, y] = r.UB[x]

    def gate_exchange():
        put(r.UB.at[xo], r.WG.at[z, x, y], to_x, k.u)

    def gate_other():
        take(r.WG.at[z, xo, y], k.u)
        gate_send(xo)

    def cot_send():
        put(r.cot, r.COT.at[x, c], to_core, k.cotc + 0)
        put(r.cot, r.COT.at[x, c], to_x, k.cotx)
        r.COT[x, c] = r.cot[...]

    def cot_from_x():
        take(r.COT.at[xo, c], k.cotx)
        put(r.COT.at[xo, c], r.COT.at[xo, c], to_core, k.cotc + 1)

    def output_send():
        put(r.WO.at[c], r.WO.at[c], to_core, k.woc)

    zall = [z] + zord

    def keys_values(q, zz):
        rows = r.N1[q, zz].reshape(XS * TOK, DIM)
        for p in range(PAIRS):
            kv = dot(rows, r.WA[p].reshape(DIM, HALF)[:, 128:])
            r.KV[p, q, pl.ds(pl.multiple_of(XS * TOK * zz, 128), XS * TOK), :] = kv.astype(BF16)

    def queries(q):
        for p in range(PAIRS):
            r.QS[p, q] = stack_heads(dot(r.N1O[q], r.WA[p].reshape(DIM, HALF)[:, :128]))

    def attend(p, q):
        kv = r.KV.at[p, q]
        stacked = r.QS[p, q]
        mask = r.MASK[q].astype(F32)
        scores = dot_tb(stacked, kv[:, :128]) + r.BIAS[p].astype(F32) + jnp.concatenate((mask, mask), axis=0)
        weights = jnp.exp(scores - jnp.max(scores, axis=1, keepdims=True))
        probs = (weights * (1.0 / jnp.sum(weights, axis=1, keepdims=True))).astype(BF16)
        r.PS[p, q] = probs
        r.ATT[c, q, :, 128 * p : 128 * p + 128] = unstack_heads(dot(probs, kv[:, 128:])).astype(BF16)

    def attended_send(q):
        put(r.ATT.at[c, q], r.ATT.at[c, q], to_core, k.att + (1 if q is c else 0))

    tokens_send(0)
    norm_block(c, z, x, own=True)
    bias_lines()
    bias_pair(2)
    shards()
    weight_start(PAIRS)
    masks()
    gate_exchange()
    bias_pair(0)
    weight_start(1)
    weight_start(2)
    weight_start(0)
    tokens_send(1)
    token_from_core(z, x)
    tokens_send(2)
    token_from_x(z)
    bias_pair(1)
    token_from_z(0)
    weight_from_z(PAIRS, 0)
    weight_from_z(1, 0)
    weight_from_z(1, 1)
    gate_other()
    down_send()
    weight_from_z(0, 0)
    weight_from_z(2, 1)
    token_from_core(zord[0], x)
    weight_from_z(2, 0)
    weight_from_z(1, 2)
    token_from_core(z, xo)
    gate_send(x)
    weight_from_z(PAIRS, 1)
    weight_from_z(0, 1)
    token_from_x(zord[0])
    token_from_core(zord[0], xo)
    weight_from_z(2, 2)
    weight_relay(1)
    weight_from_z(0, 2)
    weight_from_z(PAIRS, 2)
    token_from_z(1)
    weight_relay(0)
    down_from_z(0)
    weight_relay(2)
    gate_from_z(xo, 0)
    token_from_z(2)
    weight_relay(PAIRS)
    cot_send()
    gate_from_z(x, 0)
    token_from_core(zord[1], x)
    weight_end(1)
    gate_from_z(xo, 1)
    token_from_x(zord[1])
    weight_end(2)
    weight_end(0)
    keys_values(co, zord[0])
    keys_values(co, z)
    queries(0)
    keys_values(c, zord[1])
    keys_values(c, zord[0])
    token_from_core(zord[2], x)
    gate_from_z(xo, 2)
    keys_values(c, z)
    token_from_core(zord[1], xo)
    queries(1)
    down_from_z(1)
    token_from_x(zord[2])
    keys_values(c, zord[2])
    keys_values(co, zord[1])
    attend(2, c)
    gate_from_z(x, 1)
    token_from_core(zord[2], xo)
    keys_values(co, zord[2])
    weight_end(PAIRS)
    attend(0, co)
    down_from_z(2)
    output_send()
    attend(1, co)
    attend(2, co)
    attended_send(co)
    attend(0, c)
    attend(1, c)
    attended_send(c)
    gate_from_z(x, 2)
    cot_from_x()
    take(r.WO.at[co], k.woc)
    take(r.ATT.at[co, c], k.att)

    att_own = jnp.concatenate((r.ATT[0, c], r.ATT[1, c]), axis=1)
    tokens_f = tok[...].astype(F32)
    r.H[...] = tokens_f + jnp.concatenate(
        (dot(att_own, r.WO[0].reshape(DIM, HALF)), dot(att_own, r.WO[1].reshape(DIM, HALF))), axis=1
    )
    r.N2[x, c] = unit_rows(r.H[...])[0].astype(BF16)
    put(r.N2.at[x, c], r.N2.at[x, c], to_core, k.n2c + 0)
    put(r.N2.at[x, c], r.N2.at[x, c], to_x, k.n2x)

    for zz in [z] + zord:
        for xx in range(XS):
            take(r.WG.at[zz, xx, yo], k.gy + 4 * xx + zz)
        take(r.WD.at[zz, yo], k.dy + zz)
    take(r.COT.at[x, co], k.cotc + 0)
    take(r.COT.at[xo, co], k.cotc + 1)
    take(r.N2.at[x, co], k.n2c + 0)

    def feed_forward(xx):
        w_gu = r.WG[...].reshape(DIM, 2 * QUARTER)
        w_d = r.WD[...].reshape(QUARTER, DIM)
        n2 = r.N2[xx].reshape(2 * TOK, DIM)
        g = r.COT[xx].reshape(2 * TOK, DIM)
        gate = dot(n2, w_gu[:, :QUARTER])
        up = dot(n2, w_gu[:, QUARTER:])
        d_act = dot_tb(g, w_d)
        square = gate * gate
        inner = math.sqrt(2 / math.pi) * gate * (1.0 + 0.044715 * square)
        tanh = jnp.tanh(inner)
        half_open = 0.5 * (1.0 + tanh)
        gelu = gate * half_open
        slope = half_open + 0.5 * gate * (1.0 - tanh * tanh) * (
            math.sqrt(2 / math.pi) * (1.0 + 3 * 0.044715 * square)
        )
        act = (gelu * up).astype(BF16)
        r.ACT[xx] = act
        d_gu = jnp.concatenate(
            ((slope * (up * d_act)).astype(BF16), (gelu * d_act).astype(BF16)), axis=1
        )
        r.DGU[xx] = d_gu
        r.E2[xx] = dot_tb(d_gu, w_gu).astype(BF16).reshape(CS, TOK, DIM)
        put(r.E2.at[xx, co], r.E2C.at[xx], to_core, k.e2c + xx)
        r.MX[xx] = dot(act, w_d).astype(BF16).reshape(CS, TOK, DIM)
        put(r.MX.at[xx, co], r.MXC.at[xx], to_core, k.mxc + xx)

    feed_forward(x)
    take(r.N2.at[xo, c], k.n2x)
    put(r.N2.at[xo, c], r.N2.at[xo, c], to_core, k.n2c + 1)
    take(r.N2.at[xo, co], k.n2c + 1)
    feed_forward(xo)
    far_first = [zord[2], zord[1], zord[0], z]

    def down_grad(zz):
        return r.GD.at[zz, y]

    def gate_grad(zz):
        return r.GG.at[zz, :, y]

    def grad_from_y(part, got, slot, scatter, i):
        zz = far_first[i]
        take(got.at[zz], slot + zz)
        mine = part(zz)
        mine[...] = (mine[...].astype(F32) + got[zz].astype(F32)).astype(BF16)
        if i < 3:
            z_scatter(part, *scatter, 2 - i)

    down_scatter = (r.GDZ, r.GDC, k.rdz, k.rdc)
    gate_scatter = (r.GGZ, r.GGC, k.rgz, k.rgc)

    def down_from_y(i):
        grad_from_y(down_grad, r.GDY, k.rdy, down_scatter, i)

    def gate_from_y(i):
        grad_from_y(gate_grad, r.GGY, k.rgy, gate_scatter, i)

    def down_chain():
        z_chain(down_grad, *down_scatter)

    def gate_chain():
        z_chain(gate_grad, *gate_scatter)

    def chip_grad(ch, value):
        r.GA[ch] = value.astype(BF16).reshape(ZS, XS, YS, CHIP_ROWS, HALF)
        if HEAVY_X[ch]:
            put(r.GA.at[ch, :, xo, yo], r.GA1.at[ch, :, yo], to_x, k.ra1 + 2 * ch)
            put(r.GA.at[ch, :, xo, y], r.GA1.at[ch, :, y], to_x, k.ra1 + 2 * ch + 1)
        else:
            put(r.GA.at[ch, :, xo, yo], r.GA1.at[ch, :, xo], to_y, k.ra1 + 2 * ch)
            put(r.GA.at[ch, :, x, yo], r.GA1.at[ch, :, x], to_y, k.ra1 + 2 * ch + 1)

    def chip_step1(ch):
        if HEAVY_X[ch]:
            take(r.GA1.at[ch, :, yo], k.ra1 + 2 * ch)
            r.GA[ch, :, x, yo] = (r.GA[ch, :, x, yo].astype(F32) + r.GA1[ch, :, yo].astype(F32)).astype(BF16)
            put(r.GA.at[ch, :, x, yo], r.GA2.at[ch], to_y, k.ra2 + ch)
        else:
            take(r.GA1.at[ch, :, xo], k.ra1 + 2 * ch)
            r.GA[ch, :, xo, y] = (r.GA[ch, :, xo, y].astype(F32) + r.GA1[ch, :, xo].astype(F32)).astype(BF16)
            put(r.GA.at[ch, :, xo, y], r.GA2.at[ch], to_x, k.ra2 + ch)

    def chip_scatter(ch):
        chain = None if FAR_DIRECT_CHIP[ch] else r.GAC.at[ch]
        return (lambda zz: r.GA.at[ch, zz, x, y]), r.GAZ.at[ch], chain, k.raz + 4 * ch, k.rac + ch

    def chip_step2(ch):
        here = y if HEAVY_X[ch] else x
        take(r.GA1.at[ch, :, here], k.ra1 + 2 * ch + 1)
        take(r.GA2.at[ch], k.ra2 + ch)
        r.GA[ch, :, x, y] = (
            r.GA[ch, :, x, y].astype(F32) + r.GA1[ch, :, here].astype(F32) + r.GA2[ch].astype(F32)
        ).astype(BF16)
        for i in (2, 1, 0):
            z_scatter(*chip_scatter(ch), i)

    def chip_chain(ch):
        if not FAR_DIRECT_CHIP[ch]:
            z_chain(*chip_scatter(ch))

    def chip_end(ch):
        total = z_sum(r.GA[ch, z, x, y], r.GAZ.at[ch], k.raz + 4 * ch, FAR_DIRECT_CHIP[ch])
        r.FA[ch] = total.reshape(CS, SHARD, HALF)
        put(r.FA.at[ch, co], r.F2.at[ch, c], to_core, k.f2 + ch)
        r.F2[ch, c] = r.FA[ch, c]

    reverse = (
        lax.broadcasted_iota(jnp.int32, (TOK, TOK), 0) + lax.broadcasted_iota(jnp.int32, (TOK, TOK), 1)
        == TOK - 1
    ).astype(BF16)
    reverse2 = jnp.concatenate((reverse, reverse), axis=1)

    def attend_back(p, q):
        d_out = stack_heads(r.DO[q, :, 128 * p : 128 * p + 128].astype(F32))
        kv = r.KV.at[p, q]
        probs = r.PS[p, q]
        weighted = probs.astype(F32) * dot_tb(d_out, kv[:, 128:])
        delta = jnp.sum(weighted, axis=1, keepdims=True)
        d_scores = (weighted - probs.astype(F32) * delta).astype(BF16)
        r.DQ[p, q] = unstack_heads(dot(d_scores, kv[:, :128])).astype(BF16)
        r.DKV[p, q, :128] = dot_ta(r.QS[p, q], d_scores).astype(BF16)
        r.DKV[p, q, 128:] = dot_ta(d_out, probs).astype(BF16)
        r.PS[p, q] = d_scores

    def grads_pair(p):
        kv_grad = dot(r.DKV[p, 0], r.N1[0].reshape(LENGTH, DIM)) + dot(
            r.DKV[p, 1], r.N1[1].reshape(LENGTH, DIM)
        )
        own_rows = r.N1O[...].reshape(CS * TOK, DIM)
        q_grad = dot_ta(r.DQ[p].reshape(CS * TOK, 128), own_rows)
        chip_grad(p, jnp.concatenate((q_grad, kv_grad), axis=0).astype(BF16).T)

    def grads_bias(p):
        for hh in range(2):
            both = r.PS[p, :, TOK * hh : TOK * hh + TOK, :].reshape(CS * TOK, LENGTH)
            padded = jnp.concatenate((dot(reverse2, both), jnp.zeros((TOK, TOK), F32)), axis=1)
            placed = pltpu.roll(padded, 0, 1, stride=1, stride_axis=0)
            r.DG[2 * p + hh : 2 * p + hh + 1, :] = jnp.sum(placed, axis=0, keepdims=True)

    w_kv = jnp.concatenate([r.WA[p].reshape(DIM, HALF)[:, 128:] for p in range(PAIRS)], axis=1)

    def token_grad(q, zz):
        lanes = pl.ds(pl.multiple_of(XS * TOK * zz, 128), XS * TOK)
        d_kv = r.DKV[:, q, :, lanes].reshape(PAIRS * 256, XS * TOK)
        out = dot(w_kv, d_kv)
        for xx in range(XS):
            r.DN[q, zz, xx] = out[:, TOK * xx : TOK * xx + TOK].astype(BF16)
        if zz is z:
            total = r.DN[q, z, x].astype(F32)
            for p in range(PAIRS):
                total = total + dot_tb(r.WA[p].reshape(DIM, HALF)[:, :128], r.DQ[p, q])
            r.DN[q, z, x] = total.astype(BF16)

    def token_exchange(zz):
        token_grad(co, zz)
        put(r.DN.at[co, zz], r.DNC.at[zz], to_core, k.dnc + zz)
        token_grad(c, zz)

    def token_to_x(zz):
        take(r.DNC.at[zz], k.dnc + zz)
        r.DN[c, zz] = (r.DN[c, zz].astype(F32) + r.DNC[zz].astype(F32)).astype(BF16)
        put(r.DN.at[c, zz, xo], r.DNX.at[zz], to_x, k.dnx + zz)

    def token_part(zz):
        return r.DN.at[c, zz, x]

    token_scatter = (r.DNZ, None if FAR_DIRECT_TOKEN else r.DNT, k.dnz, k.dnt)

    def token_chain():
        if not FAR_DIRECT_TOKEN:
            z_chain(token_part, *token_scatter)

    def token_to_z(i):
        zz = far_first[i]
        take(r.DNX.at[zz], k.dnx + zz)
        r.DN[c, zz, x] = (r.DN[c, zz, x].astype(F32) + r.DNX[zz].astype(F32)).astype(BF16)
        if i < 3:
            z_scatter(token_part, *token_scatter, 2 - i)

    def grads_down():
        cot_all = r.COT[...].reshape(4 * TOK, DIM)
        r.GD[...] = dot_ta(r.ACT[...].reshape(4 * TOK, QUARTER), cot_all).astype(BF16).reshape(
            ZS, YS, DOWN_ROWS, DIM
        )
        for zz in far_first:
            put(r.GD.at[zz, yo], r.GDY.at[zz], to_y, k.rdy + zz)

    def grads_gate():
        n2_all = r.N2[...].reshape(4 * TOK, DIM)
        d_gu_all = r.DGU[...].reshape(4 * TOK, 2 * QUARTER)
        r.GG[...] = dot_ta(n2_all, d_gu_all).astype(BF16).reshape(ZS, XS, YS, CHIP_ROWS, 2 * QUARTER)
        for zz in far_first:
            put(r.GG.at[zz, :, yo], r.GGY.at[zz], to_y, k.rgy + zz)

    def zeros():
        z_zero(r.GDZ)
        z_zero(r.GGZ)
        if not FAR_DIRECT_TOKEN:
            z_zero(r.DNZ)
        for ch in range(CHUNKS):
            if not FAR_DIRECT_CHIP[ch]:
                z_zero(r.GAZ.at[ch])

    def hidden_send():
        take(r.E2C.at[xo], k.e2c + xo)
        r.E2S[...] = (r.E2[xo, c].astype(F32) + r.E2C[xo].astype(F32)).astype(BF16)
        put(r.E2S, r.E2X, to_x, k.e2x)

    def hidden_back():
        take(r.E2C.at[x], k.e2c + x)
        take(r.E2X, k.e2x)
        e2 = r.E2[x, c].astype(F32) + r.E2C[x].astype(F32) + r.E2X[...].astype(F32)
        n2_own, r2 = unit_rows(r.H[...])
        r.DH[...] = r.cot[...].astype(F32) + r2 * (
            e2 - n2_own * jnp.mean(e2 * n2_own, axis=1, keepdims=True)
        )
        r.DB[c] = r.DH[...].astype(BF16)
        put(r.DB.at[c], r.DB.at[c], to_core, k.db)

    def mixed_send():
        take(r.MXC.at[xo], k.mxc + xo)
        r.MXS[...] = (r.MX[xo, c].astype(F32) + r.MXC[xo].astype(F32)).astype(BF16)
        put(r.MXS, r.MXX, to_x, k.mxx)

    def mixed_end():
        take(r.MXC.at[x], k.mxc + x)
        take(r.MXX, k.mxx)
        r.mixed[...] = (
            r.H[...] + r.MX[x, c].astype(F32) + r.MXC[x].astype(F32) + r.MXX[...].astype(F32)
        ).astype(BF16)

    def attended_back(q):
        if q is co:
            take(r.DB.at[co], k.db)
        rows = [r.WO[h, pl.ds(2 * c, 2)].reshape(HALF, HALF) for h in range(CS)]
        d_att = dot_tb(r.DB[q, :, :HALF], rows[0]) + dot_tb(r.DB[q, :, HALF:], rows[1])
        r.DO[q] = d_att.astype(BF16)

    def grads_output():
        take(r.ATT.at[co, co], k.att + 1)
        att_all = jnp.concatenate(
            [jnp.concatenate((r.ATT[0, q], r.ATT[1, q]), axis=1) for q in range(CS)], axis=0
        )
        db_cols = r.DB[:, :, pl.ds(pl.multiple_of(HALF * c, 128), HALF)].reshape(CS * TOK, HALF)
        chip_grad(PAIRS, dot_ta(att_all, db_cols))

    def table_start():
        r.DG[HEADS_HERE:, :] = jnp.zeros((8 - HEADS_HERE, SPAN), F32)
        onehot_back = (
            lax.broadcasted_iota(jnp.int32, (128, SPAN), 0)
            == r.BK[:, pl.ds(pl.multiple_of(LENGTH - TOK - TOK * s, 128), SPAN)]
        ).astype(F32)
        r.T1[...] = lax.dot_general(
            r.DG[...], onehot_back, (((1,), (1,)), ((), ())), precision=HIGHEST, preferred_element_type=F32
        )
        put(r.T1, r.TY, to_y, k.ty)

    def table_to_x():
        take(r.TY, k.ty)
        r.T2[...] = r.T1[...] + r.TY[...]
        put(r.T2, r.TX, to_x, k.tx)

    def table_to_z():
        take(r.TX, k.tx)
        r.T3[...] = r.T2[...] + r.TX[...]
        for who in to_z:
            put(r.T3, r.TZ.at[z], who, k.tz + z)
        r.TZ[z] = r.T3[...]

    def table_to_core():
        for zz in zord:
            take(r.TZ.at[zz], k.tz + zz)
        r.TO[c] = (r.TZ[0] + r.TZ[1]) + (r.TZ[2] + r.TZ[3])
        put(r.TO.at[c], r.TO.at[c], to_core, k.tc)

    def table_end():
        take(r.TO.at[co], k.tc)
        for q in range(CS):
            r.gtab[HEADS_HERE * q : HEADS_HERE * q + HEADS_HERE, :] = r.TO[q, :HEADS_HERE, :32]

    def down_end():
        r.gwd[...] = z_sum(r.GD[z, y], r.GDZ, k.rdz)

    def gate_to_x():
        total = z_sum(r.GG[z, :, y], r.GGZ, k.rgz)
        r.F4S[...] = total.astype(BF16)
        put(r.F4S.at[xo], r.F4X, to_x, k.f4x)

    def gate_to_core():
        take(r.F4X, k.f4x)
        r.F4S2[:, x] = r.F4S[x].astype(F32).reshape(CS, SHARD, 2 * QUARTER)
        r.F4S2[:, xo] = r.F4X[...].astype(F32).reshape(CS, SHARD, 2 * QUARTER)
        put(r.F4S2.at[co], r.F4.at[c], to_core, k.f4)
        r.F4[c] = r.F4S2[c]

    def gate_end():
        take(r.F4.at[co], k.f4)
        quarters = [r.F4[q % CS, q // CS] for q in range(BATCH_DEVICES)]
        gate_total = join_quarters([quarter[:, :QUARTER] for quarter in quarters])
        up_total = join_quarters([quarter[:, QUARTER:] for quarter in quarters])
        r.gwg[...] = gate_total * gain_f
        r.gwu[...] = up_total * gain_f
        r.ggf[...] = to_row(
            jnp.sum(
                gate_total * r.wg[...].astype(F32) + up_total * r.wu[...].astype(F32), axis=1, keepdims=True
            )
        )

    def token_end():
        e1 = z_sum(r.DN[c, z, x], r.DNZ, k.dnz, FAR_DIRECT_TOKEN).T
        n1_own, r1 = unit_rows(tok[...].astype(F32))
        r.tg[...] = (
            r.DH[...] + r1 * (e1 - n1_own * jnp.mean(e1 * n1_own, axis=1, keepdims=True))
        ).astype(BF16)

    def chip_out(ch):
        take(r.F2.at[ch, co], k.f2 + ch)
        if ch == PAIRS:
            for h in range(CS):
                r.gwo[:, HALF * h : HALF * h + HALF] = r.F2[ch, h]
            return
        gain_part = jnp.zeros((SHARD, 128), F32)
        for j, (w_ref, out_ref) in enumerate(((r.wq, r.gwq), (r.wk, r.gwk), (r.wv, r.gwv))):
            for h in range(CS):
                lanes = slice(HALF * h + 128 * ch, HALF * h + 128 * ch + 128)
                grad = r.F2[ch, h, :, 128 * j : 128 * j + 128]
                gain_part = gain_part + grad * w_ref[:, lanes].astype(F32)
                out_ref[:, lanes] = grad * gain_a
        r.GT[ch] = gain_part

    def gain_end():
        r.gga[...] = to_row(jnp.sum(r.GT[0] + r.GT[1] + r.GT[2], axis=1, keepdims=True))

    zeros()
    grads_down()
    hidden_send()
    down_from_y(0)
    mixed_send()
    grads_gate()
    hidden_back()
    down_from_y(1)
    attended_back(c)
    attend_back(2, c)
    down_from_y(2)
    attended_back(co)
    down_chain()
    grads_output()
    attend_back(0, c)
    attend_back(1, co)
    attend_back(2, co)
    down_from_y(3)
    grads_bias(2)
    grads_pair(2)
    gate_from_y(0)
    attend_back(0, co)
    down_end()
    chip_step1(PAIRS)
    attend_back(1, c)
    token_exchange(far_first[1])
    mixed_end()
    grads_bias(1)
    gate_from_y(1)
    grads_bias(0)
    token_exchange(far_first[2])
    gate_chain()
    token_to_x(far_first[1])
    table_start()
    token_exchange(far_first[0])
    chip_step1(2)
    gate_from_y(2)
    grads_pair(0)
    grads_pair(1)
    token_to_x(far_first[0])
    token_to_x(far_first[2])
    token_exchange(far_first[3])
    token_to_z(1)
    gate_from_y(3)
    table_to_x()
    chip_step2(PAIRS)
    token_to_x(far_first[3])
    chip_chain(PAIRS)
    token_to_z(0)
    table_to_z()
    token_to_z(2)
    chip_step1(0)
    chip_step1(1)
    gate_to_x()
    token_to_z(3)
    chip_step2(2)
    token_chain()
    chip_end(PAIRS)
    chip_step2(0)
    chip_chain(2)
    table_to_core()
    chip_out(PAIRS)
    chip_step2(1)
    chip_end(2)
    gate_to_core()
    chip_chain(0)
    chip_out(2)
    table_end()
    chip_chain(1)
    token_end()
    gate_end()
    chip_end(0)
    chip_end(1)
    chip_out(0)
    chip_out(1)
    gain_end()
    for i in range(len(sent) - SEND_RING, len(sent)):
        sent_wait(i)


def finish_kernel(*refs):
    count = len(refs) // 2
    for src, dst in zip(refs[:count], refs[count:]):
        dst[...] = src[...]


def fused_device(
    tokens, segments, buckets, gain_attn, w_query, w_key, w_value, w_output,
    gain_ffn, w_gate, w_up, w_down, bucket_bias_matrix, cotangent,
):
    operands = (
        tokens.reshape(TOK, DIM),
        cotangent.reshape(TOK, DIM),
        segments.reshape(1, LENGTH),
        buckets.reshape(1, 2 * LENGTH - 1),
        bucket_bias_matrix.T,
        gain_attn.reshape(1, SHARD),
        gain_ffn.reshape(1, SHARD),
        w_query, w_key, w_value, w_output, w_gate, w_up, w_down,
    )
    out_shape = [jax.ShapeDtypeStruct(shape, dtype) for shape, dtype in OUTPUTS.values()]
    in_vmem = pl.BlockSpec(memory_space=pltpu.VMEM)
    outs = pl.pallas_call(
        layer_kernel,
        out_shape=out_shape,
        in_specs=[in_vmem] * len(operands),
        out_specs=[in_vmem] * len(out_shape),
        scratch_shapes=[pltpu.VMEM(shape, dtype) for shape, dtype in SCRATCH.values()]
        + [pltpu.SemaphoreType.DMA((SEND_RING,)), pltpu.SemaphoreType.DMA((RECV_COUNT,))],
        compiler_params=pltpu.CompilerParams(
            collective_id=0, has_side_effects=True, vmem_limit_bytes=63 * 2**20
        ),
        name="layer",
    )(*operands)
    outs = pl.pallas_call(
        finish_kernel,
        out_shape=out_shape,
        in_specs=[in_vmem] * len(out_shape),
        out_specs=[in_vmem] * len(out_shape),
        name="finish",
    )(*outs)
    mixed, tokens_grad, gga, gwq, gwk, gwv, gwo, ggf, gwg, gwu, gwd, table_grad = outs
    return (
        mixed.reshape(tokens.shape), tokens_grad.reshape(tokens.shape), gga.reshape(SHARD),
        gwq, gwk, gwv, gwo, ggf.reshape(SHARD), gwg, gwu, gwd, table_grad.T,
    )


def fits_fused(mesh):
    return mesh.shape["seq"] == SEQ_DEVICES and mesh.shape["batch"] == BATCH_DEVICES


def solution(mesh):
    return jax.shard_map(
        fused_device if fits_fused(mesh) else on_device,
        mesh=mesh,
        in_specs=(
            P("seq", "batch", None),
            P(None, "batch"),
            P(),
            P(("seq", "batch")),
            P(("seq", "batch"), None),
            P(("seq", "batch"), None),
            P(("seq", "batch"), None),
            P(("seq", "batch"), None),
            P(("seq", "batch")),
            P(("seq", "batch"), None),
            P(("seq", "batch"), None),
            P(("seq", "batch"), None),
            P(),
            P("seq", "batch", None),
        ),
        out_specs=(
            P("seq", "batch", None),
            P("seq", "batch", None),
            P(("seq", "batch")),
            P(("seq", "batch"), None),
            P(("seq", "batch"), None),
            P(("seq", "batch"), None),
            P(("seq", "batch"), None),
            P(("seq", "batch")),
            P(("seq", "batch"), None),
            P(("seq", "batch"), None),
            P(("seq", "batch"), None),
            P(),
        ),
        check_vma=False,
    )
```

```python
from functools import partial
import math
from types import SimpleNamespace

import jax
import jax.numpy as jnp
from jax import lax
from jax.experimental import pallas as pl
from jax.experimental.pallas import tpu as pltpu
from jax.sharding import PartitionSpec as P

EPSILON = 1e-06
NEGATIVE = -1e30
HIGHEST = lax.Precision.HIGHEST


def normalize(hidden_state, scale_vec):
    return (
        hidden_state
        * lax.rsqrt(jnp.mean(hidden_state * hidden_state, axis=-1, keepdims=True) + EPSILON)
        * scale_vec
    )


def gelu_tanh(gate_vals):
    return jax.nn.gelu(gate_vals, approximate=True)


def project(left_side, weight):
    return jnp.einsum("tsk,kn->tsn", left_side, weight, preferred_element_type=jnp.float32)


def project_back(grad_rows, weight):
    return jnp.einsum("tsn,kn->tsk", grad_rows, weight, preferred_element_type=jnp.float32)


def weight_grad(left_side, grad_rows):
    return jnp.einsum("tsk,tsn->kn", left_side, grad_rows, preferred_element_type=jnp.float32)


def position_bias(
    buckets, bucket_bias_matrix, query_start, key_start, query_rows, key_rows, seq_length
):
    span = query_rows + key_rows - 1
    head_count = bucket_bias_matrix.shape[1]
    first = key_start - query_start + seq_length - query_rows
    chosen = lax.dynamic_slice_in_dim(buckets, first, span, 0)
    onehot = (
        chosen[:, None] == jnp.arange(bucket_bias_matrix.shape[0], dtype=jnp.int32)[None, :]
    ).astype(jnp.float32)
    per_offset = jnp.dot(onehot, bucket_bias_matrix.astype(jnp.float32), precision=HIGHEST)
    padded = jnp.concatenate((per_offset.T, jnp.zeros((head_count, 1), jnp.float32)), axis=1)
    tiled = jnp.broadcast_to(padded[:, None, :], (head_count, query_rows, span + 1)).reshape(
        head_count, query_rows * (span + 1)
    )
    skewed = tiled[:, : query_rows * span].reshape(head_count, query_rows, span)
    return (onehot, skewed[:, :, query_rows - 1 : query_rows - 1 + key_rows])


def table_term(onehot, score_gradient):
    summed = jnp.sum(score_gradient.astype(jnp.float32), axis=0)
    head_count, query_rows, key_rows = summed.shape
    span = query_rows + key_rows - 1
    placed = jnp.pad(summed, ((0, 0), (0, 0), (query_rows - 1, 0))).reshape(
        head_count, query_rows * span
    )
    placed = jnp.pad(placed, ((0, 0), (0, query_rows)))
    diagonal_sums = jnp.sum(placed.reshape(head_count, query_rows, span + 1), axis=1)[:, :span]
    return jnp.dot(onehot.T, diagonal_sums.T, precision=HIGHEST)


def pair_scores(table_set, query_block, query_segs, query_start, key_block, key_segs, key_start):
    buckets, bucket_bias_matrix, seq_length = table_set
    onehot, bias_contributions = position_bias(
        buckets,
        bucket_bias_matrix,
        query_start,
        key_start,
        query_block.shape[0],
        key_block.shape[0],
        seq_length,
    )
    scores = (
        jnp.einsum("qshd,kshd->shqk", query_block, key_block, preferred_element_type=jnp.float32)
        + bias_contributions[None]
    )
    allowed = (query_segs.T[:, :, None] == key_segs.T[:, None, :])[:, None]
    return (onehot, scores, allowed)


def pair_grads(
    table_set,
    query_block,
    query_segs,
    query_start,
    dout_block,
    log_sums,
    deltas,
    key_block,
    value_block,
    key_segs,
    key_start,
):
    onehot, scores, allowed = pair_scores(
        table_set, query_block, query_segs, query_start, key_block, key_segs, key_start
    )
    probabilities = jnp.where(allowed, jnp.exp(scores - log_sums[..., None]), 0.0)
    dprobs = jnp.einsum(
        "qshd,kshd->shqk", dout_block, value_block, preferred_element_type=jnp.float32
    )
    score_gradient = (probabilities * (dprobs - deltas[..., None])).astype(jnp.bfloat16)
    return (onehot, probabilities, score_gradient)


def attend_block(setting, carried, blocks, key_start):
    table_set, segments, query_heads, query_segs, query_start = setting
    running_max, running_sum, accum = carried
    key_block, value_block = blocks
    key_segs = lax.dynamic_slice_in_dim(segments, key_start, key_block.shape[0], 0)
    _, scores, allowed = pair_scores(
        table_set, query_heads, query_segs, query_start, key_block, key_segs, key_start
    )
    new_max = jnp.maximum(running_max, jnp.max(jnp.where(allowed, scores, NEGATIVE), axis=-1))
    weights_raw = jnp.where(allowed, jnp.exp(scores - new_max[..., None]), 0.0)
    factor = jnp.exp(running_max - new_max)
    running_sum = running_sum * factor + jnp.sum(weights_raw, axis=-1)
    accum = accum * jnp.transpose(factor, (2, 0, 1))[..., None] + jnp.einsum(
        "shqk,kshd->qshd",
        weights_raw.astype(jnp.bfloat16),
        value_block,
        preferred_element_type=jnp.float32,
    )
    return (new_max, running_sum, accum)


def merged_block(setting, extras, carried, scan_item):
    table_set, segments, query_heads, query_segs, query_start = setting
    dout_heads, log_sums, deltas = extras
    dquery, dtable = carried
    key_start, key_block, value_block = scan_item
    key_rows = key_block.shape[0]
    seq_count = key_block.shape[1]
    key_segs = lax.dynamic_slice_in_dim(segments, key_start, key_rows, 0)
    onehot, probabilities, score_gradient = pair_grads(
        table_set,
        query_heads,
        query_segs,
        query_start,
        dout_heads,
        log_sums,
        deltas,
        key_block,
        value_block,
        key_segs,
        key_start,
    )
    dquery = dquery + jnp.einsum(
        "shqk,kshd->qshd", score_gradient, key_block, preferred_element_type=jnp.float32
    )
    dtable = dtable + table_term(onehot, score_gradient)
    key_gradient = jnp.einsum(
        "shqk,qshd->kshd", score_gradient, query_heads, preferred_element_type=jnp.float32
    )
    dvalue = jnp.einsum(
        "shqk,qshd->kshd",
        probabilities.astype(jnp.bfloat16),
        dout_heads,
        preferred_element_type=jnp.float32,
    )
    joined = jnp.concatenate(
        (key_gradient.reshape(key_rows, seq_count, -1), dvalue.reshape(key_rows, seq_count, -1)),
        axis=2,
    )
    return ((dquery, dtable), joined)


def fold_blocks(step_fn, carried, pieces):
    piece_rows = pieces[0].shape[0]
    block_rows = math.gcd(piece_rows, 512)
    block_count = piece_rows // block_rows
    stacked = tuple(
        (piece.reshape((block_count, block_rows) + piece.shape[1:]) for piece in pieces)
    )

    def advance(state_now, scan_item):
        block_index, blocks = scan_item
        return (step_fn(state_now, blocks, block_index * block_rows), None)

    result, _ = lax.scan(advance, carried, (jnp.arange(block_count, dtype=jnp.int32), stacked))
    return result


def on_device(
    tokens,
    segments,
    buckets,
    gain_attn,
    w_query,
    w_key,
    w_value,
    w_output,
    gain_ffn,
    w_gate,
    w_up,
    w_down,
    bucket_bias_matrix,
    cotangent,
):
    tok_rows, seq_count, _ = tokens.shape
    head_count = bucket_bias_matrix.shape[1]
    inner_width = w_query.shape[1]
    head_width = inner_width // head_count
    head_shape = (tok_rows, seq_count, head_count, head_width)
    seq_length = (buckets.shape[0] + 1) // 2
    query_start = lax.axis_index("seq") * tok_rows
    (
        full_gain_attn,
        full_query,
        full_key,
        full_value,
        full_output,
        full_gain_ffn,
        full_gate,
        full_up,
        full_down,
    ) = (
        lax.all_gather(gain_attn, ("seq", "batch"), axis=0, tiled=True),
        lax.all_gather(w_query, ("seq", "batch"), axis=0, tiled=True),
        lax.all_gather(w_key, ("seq", "batch"), axis=0, tiled=True),
        lax.all_gather(w_value, ("seq", "batch"), axis=0, tiled=True),
        lax.all_gather(w_output, ("seq", "batch"), axis=0, tiled=True),
        lax.all_gather(gain_ffn, ("seq", "batch"), axis=0, tiled=True),
        lax.all_gather(w_gate, ("seq", "batch"), axis=0, tiled=True),
        lax.all_gather(w_up, ("seq", "batch"), axis=0, tiled=True),
        lax.all_gather(w_down, ("seq", "batch"), axis=0, tiled=True),
    )
    tokens_full = tokens.astype(jnp.float32)
    normed1 = normalize(tokens_full, full_gain_attn.astype(jnp.float32)).astype(jnp.bfloat16)
    query_heads = project(normed1, full_query).astype(jnp.bfloat16).reshape(head_shape)
    key_heads = project(normed1, full_key).astype(jnp.bfloat16).reshape(head_shape)
    value_heads = project(normed1, full_value).astype(jnp.bfloat16).reshape(head_shape)
    query_segs = lax.dynamic_slice_in_dim(segments, query_start, tok_rows, 0)
    table_set = (buckets, bucket_bias_matrix, seq_length)
    setting = (table_set, segments, query_heads, query_segs, query_start)
    start_state = (
        jnp.full((seq_count, head_count, tok_rows), NEGATIVE, jnp.float32),
        jnp.zeros((seq_count, head_count, tok_rows), jnp.float32),
        jnp.zeros(head_shape, jnp.float32),
    )
    step_forward = partial(attend_block, setting)
    running_max, running_sum, accum = fold_blocks(
        step_forward,
        start_state,
        (
            lax.all_gather(key_heads, "seq", axis=0, tiled=True),
            lax.all_gather(value_heads, "seq", axis=0, tiled=True),
        ),
    )
    attended_full = accum / jnp.transpose(running_sum, (2, 0, 1))[..., None]
    log_sums = running_max + jnp.log(running_sum)
    attended = attended_full.astype(jnp.bfloat16).reshape(tok_rows, seq_count, inner_width)
    hidden1 = tokens_full + project(attended, full_output)
    normed2 = normalize(hidden1, full_gain_ffn.astype(jnp.float32)).astype(jnp.bfloat16)
    gate = project(normed2, full_gate)
    up_val = project(normed2, full_up)
    gelu_out, gelu_pull = jax.vjp(gelu_tanh, gate)
    activated = (gelu_out * up_val).astype(jnp.bfloat16)
    mixed = (hidden1 + project(activated, full_down)).astype(jnp.bfloat16)
    (
        full_gain_attn,
        full_query,
        full_key,
        full_value,
        full_output,
        full_gain_ffn,
        full_gate,
        full_up,
        full_down,
    ) = (
        lax.all_gather(gain_attn, ("seq", "batch"), axis=0, tiled=True),
        lax.all_gather(w_query, ("seq", "batch"), axis=0, tiled=True),
        lax.all_gather(w_key, ("seq", "batch"), axis=0, tiled=True),
        lax.all_gather(w_value, ("seq", "batch"), axis=0, tiled=True),
        lax.all_gather(w_output, ("seq", "batch"), axis=0, tiled=True),
        lax.all_gather(gain_ffn, ("seq", "batch"), axis=0, tiled=True),
        lax.all_gather(w_gate, ("seq", "batch"), axis=0, tiled=True),
        lax.all_gather(w_up, ("seq", "batch"), axis=0, tiled=True),
        lax.all_gather(w_down, ("seq", "batch"), axis=0, tiled=True),
    )
    grad_down = weight_grad(activated, cotangent)
    d_activated = project_back(cotangent, full_down)
    d_gate = gelu_pull(d_activated * up_val)[0].astype(jnp.bfloat16)
    d_up = (gelu_out * d_activated).astype(jnp.bfloat16)
    grad_gate = weight_grad(normed2, d_gate)
    grad_up = weight_grad(normed2, d_up)
    d_normed2 = project_back(d_gate, full_gate) + project_back(d_up, full_up)
    _, norm_pull2 = jax.vjp(normalize, hidden1, full_gain_ffn.astype(jnp.float32))
    d_hidden_part, grad_gain_ffn = norm_pull2(d_normed2)
    d_hidden1 = cotangent.astype(jnp.float32) + d_hidden_part
    d_branch = d_hidden1.astype(jnp.bfloat16)
    grad_output = weight_grad(attended, d_branch)
    dout_heads = project_back(d_branch, full_output).astype(jnp.bfloat16).reshape(head_shape)
    deltas = jnp.transpose(
        jnp.sum(dout_heads.astype(jnp.float32) * attended_full, axis=-1), (1, 2, 0)
    )
    extras = (dout_heads, log_sums, deltas)
    keys_all, values_all = (
        lax.all_gather(key_heads, "seq", axis=0, tiled=True),
        lax.all_gather(value_heads, "seq", axis=0, tiled=True),
    )
    block_rows = math.gcd(seq_length, 512)
    block_count = seq_length // block_rows
    stacked_keys = keys_all.reshape((block_count, block_rows) + keys_all.shape[1:])
    stacked_values = values_all.reshape((block_count, block_rows) + values_all.shape[1:])
    block_starts = jnp.arange(block_count, dtype=jnp.int32) * block_rows
    query_init = (
        jnp.zeros(head_shape, jnp.float32),
        jnp.zeros(bucket_bias_matrix.shape, jnp.float32),
    )
    (dquery, dtable), joined_all = lax.scan(
        partial(merged_block, setting, extras),
        query_init,
        (block_starts, stacked_keys, stacked_values),
    )
    every_key_contribution = joined_all.reshape(seq_length, seq_count, 2 * inner_width)
    key_sums = lax.psum_scatter(every_key_contribution, "seq", scatter_dimension=0, tiled=True)
    dkey_rows = key_sums[:, :, :inner_width].astype(jnp.bfloat16)
    dvalue_rows = key_sums[:, :, inner_width:].astype(jnp.bfloat16)
    dquery_rows = dquery.reshape(tok_rows, seq_count, inner_width).astype(jnp.bfloat16)
    grad_query = weight_grad(normed1, dquery_rows)
    grad_key = weight_grad(normed1, dkey_rows)
    grad_value = weight_grad(normed1, dvalue_rows)
    d_normed1 = (
        project_back(dquery_rows, full_query)
        + project_back(dkey_rows, full_key)
        + project_back(dvalue_rows, full_value)
    )
    _, norm_pull1 = jax.vjp(normalize, tokens_full, full_gain_attn.astype(jnp.float32))
    d_input_part, grad_gain_attn = norm_pull1(d_normed1)
    tokens_grad = (d_hidden1 + d_input_part).astype(jnp.bfloat16)
    owned = (
        lax.psum_scatter(grad_gain_attn, ("seq", "batch"), scatter_dimension=0, tiled=True),
        lax.psum_scatter(grad_query, ("seq", "batch"), scatter_dimension=0, tiled=True),
        lax.psum_scatter(grad_key, ("seq", "batch"), scatter_dimension=0, tiled=True),
        lax.psum_scatter(grad_value, ("seq", "batch"), scatter_dimension=0, tiled=True),
        lax.psum_scatter(grad_output, ("seq", "batch"), scatter_dimension=0, tiled=True),
        lax.psum_scatter(grad_gain_ffn, ("seq", "batch"), scatter_dimension=0, tiled=True),
        lax.psum_scatter(grad_gate, ("seq", "batch"), scatter_dimension=0, tiled=True),
        lax.psum_scatter(grad_up, ("seq", "batch"), scatter_dimension=0, tiled=True),
        lax.psum_scatter(grad_down, ("seq", "batch"), scatter_dimension=0, tiled=True),
    )
    table_total = lax.psum(dtable, ("seq", "batch"))
    return (
        mixed,
        tokens_grad,
        owned[0],
        owned[1],
        owned[2],
        owned[3],
        owned[4],
        owned[5],
        owned[6],
        owned[7],
        owned[8],
        table_total,
    )


BF16 = jnp.bfloat16
F32 = jnp.float32
MESH_IDS = pl.DeviceIdType.MESH

ZS, XS, YS, CS = 4, 2, 2, 2
SEQ_DEVICES = ZS * XS
BATCH_DEVICES = YS * CS
TOK = 128
LENGTH = SEQ_DEVICES * TOK
DIM = 768
HALF = DIM // CS
PAIRS = HALF // 128
SHARD = DIM // (SEQ_DEVICES * BATCH_DEVICES)
CHIP_ROWS = SHARD * CS
GROUP_ROWS = SHARD * BATCH_DEVICES
FF_ALL = 2048
QUARTER = FF_ALL // BATCH_DEVICES
DOWN_ROWS = FF_ALL // (SEQ_DEVICES * BATCH_DEVICES)
CHUNKS = PAIRS + 1
SPAN = LENGTH + TOK
HEADS_HERE = 2 * PAIRS


def dot(a, b):
    return lax.dot_general(a, b, (((1,), (0,)), ((), ())), preferred_element_type=F32)


def dot_tb(a, b):
    return lax.dot_general(a, b, (((1,), (1,)), ((), ())), preferred_element_type=F32)


def dot_ta(a, b):
    return lax.dot_general(a, b, (((0,), (0,)), ((), ())), preferred_element_type=F32)


def to_column(row):
    n = row.shape[1]
    eye = lax.broadcasted_iota(jnp.int32, (n, n), 0) == lax.broadcasted_iota(jnp.int32, (n, n), 1)
    return jnp.sum(jnp.where(eye, jnp.broadcast_to(row, (n, n)), 0.0), axis=1, keepdims=True)


def to_row(col):
    n = col.shape[0]
    eye = lax.broadcasted_iota(jnp.int32, (n, n), 0) == lax.broadcasted_iota(jnp.int32, (n, n), 1)
    return jnp.sum(jnp.where(eye, jnp.broadcast_to(col, (n, n)), 0.0), axis=0, keepdims=True)


def unit_rows(x):
    r = lax.rsqrt(jnp.mean(x * x, axis=1, keepdims=True) + EPSILON)
    return x * r, r


def stack_heads(pair):
    low = lax.broadcasted_iota(jnp.int32, pair.shape, 1) < 64
    return jnp.concatenate((jnp.where(low, pair, 0.0), jnp.where(low, 0.0, pair)), axis=0).astype(BF16)


def unstack_heads(stacked):
    rows = stacked.shape[0] // 2
    low = lax.broadcasted_iota(jnp.int32, (rows, 128), 1) < 64
    return jnp.where(low, stacked[:rows], stacked[rows:])


def split_quarters(whole):
    low = lax.broadcasted_iota(jnp.int32, (whole.shape[0], 128), 1) < 64
    parts = []
    for q in range(BATCH_DEVICES):
        cols = []
        for m in range(ZS):
            first = 4 * m + 2 * (q // 2)
            a = whole[:, 128 * first : 128 * first + 128]
            b = whole[:, 128 * (first + 1) : 128 * (first + 1) + 128]
            if q % 2 == 0:
                cols.append(jnp.where(low, a, pltpu.roll(b, 64, 1)))
            else:
                cols.append(jnp.where(low, pltpu.roll(a, 64, 1), b))
        parts.append(jnp.concatenate(cols, axis=1))
    return parts


def join_quarters(parts):
    low = lax.broadcasted_iota(jnp.int32, (parts[0].shape[0], 128), 1) < 64
    cols = []
    for block in range(FF_ALL // 128):
        m, xx, yy = block // 4, block // 2 % 2, block % 2
        lanes = slice(128 * m, 128 * m + 128)
        a, b = parts[2 * xx][:, lanes], parts[2 * xx + 1][:, lanes]
        if yy == 0:
            cols.append(jnp.where(low, a, pltpu.roll(b, 64, 1)))
        else:
            cols.append(jnp.where(low, pltpu.roll(a, 64, 1), b))
    return jnp.concatenate(cols, axis=1)


SCRATCH = dict(
    W_MINE=((CS, SHARD, 4 * HALF + 4 * QUARTER), F32),
    W_CORE=((CS, SHARD, 4 * HALF + 4 * QUARTER), F32),
    UB=((XS, CHIP_ROWS, 2 * QUARTER), BF16),
    WA=((PAIRS, ZS, XS, YS, CHIP_ROWS, HALF), BF16),
    WO=((CS, ZS, XS, YS, CHIP_ROWS, HALF), BF16),
    WG=((ZS, XS, YS, CHIP_ROWS, 2 * QUARTER), BF16),
    WD=((ZS, YS, DOWN_ROWS, DIM), BF16),
    X=((CS, ZS, XS, TOK, DIM), BF16),
    N1=((CS, ZS, XS, TOK, DIM), BF16),
    N1O=((CS, TOK, DIM), BF16),
    COT=((XS, CS, TOK, DIM), BF16),
    SEG=((CS, 8, LENGTH), F32),
    BK=((1, 2 * LENGTH), jnp.int32),
    PH=((2 * CS * PAIRS, SPAN), F32),
    BIAS=((PAIRS, 2 * TOK, LENGTH), BF16),
    MASK=((CS, TOK, LENGTH), BF16),
    KV=((PAIRS, CS, LENGTH, 256), BF16),
    QS=((PAIRS, CS, 2 * TOK, 128), BF16),
    PS=((PAIRS, CS, 2 * TOK, LENGTH), BF16),
    ATT=((CS, CS, TOK, HALF), BF16),
    H=((TOK, DIM), F32),
    N2=((XS, CS, TOK, DIM), BF16),
    ACT=((XS, 2 * TOK, QUARTER), BF16),
    DGU=((XS, 2 * TOK, 2 * QUARTER), BF16),
    MX=((XS, CS, TOK, DIM), BF16),
    MXC=((XS, TOK, DIM), BF16),
    MXS=((TOK, DIM), BF16),
    MXX=((TOK, DIM), BF16),
    E2=((XS, CS, TOK, DIM), BF16),
    E2C=((XS, TOK, DIM), BF16),
    E2S=((TOK, DIM), BF16),
    E2X=((TOK, DIM), BF16),
    GG=((ZS, XS, YS, CHIP_ROWS, 2 * QUARTER), BF16),
    GGY=((ZS, XS, CHIP_ROWS, 2 * QUARTER), BF16),
    GGZ=((ZS, XS, CHIP_ROWS, 2 * QUARTER), BF16),
    GGC=((XS, CHIP_ROWS, 2 * QUARTER), BF16),
    GD=((ZS, YS, DOWN_ROWS, DIM), BF16),
    GDY=((ZS, DOWN_ROWS, DIM), BF16),
    GDZ=((ZS, DOWN_ROWS, DIM), BF16),
    GDC=((DOWN_ROWS, DIM), BF16),
    F4S=((XS, CHIP_ROWS, 2 * QUARTER), BF16),
    F4X=((CHIP_ROWS, 2 * QUARTER), BF16),
    F4S2=((CS, XS, SHARD, 2 * QUARTER), F32),
    F4=((CS, XS, SHARD, 2 * QUARTER), F32),
    DH=((TOK, DIM), F32),
    DB=((CS, TOK, DIM), BF16),
    DO=((CS, TOK, HALF), BF16),
    DQ=((PAIRS, CS, TOK, 128), BF16),
    DKV=((PAIRS, CS, 256, LENGTH), BF16),
    DG=((8, SPAN), F32),
    GA=((CHUNKS, ZS, XS, YS, CHIP_ROWS, HALF), BF16),
    GA1=((CHUNKS, ZS, 2, CHIP_ROWS, HALF), BF16),
    GA2=((CHUNKS, ZS, CHIP_ROWS, HALF), BF16),
    GAZ=((CHUNKS, ZS, CHIP_ROWS, HALF), BF16),
    GAC=((CHUNKS, CHIP_ROWS, HALF), BF16),
    FA=((CHUNKS, CS, SHARD, HALF), F32),
    F2=((CHUNKS, CS, SHARD, HALF), F32),
    GT=((PAIRS, SHARD, 128), F32),
    DN=((CS, ZS, XS, DIM, TOK), BF16),
    DNC=((ZS, XS, DIM, TOK), BF16),
    DNX=((ZS, DIM, TOK), BF16),
    DNZ=((ZS, DIM, TOK), BF16),
    DNT=((DIM, TOK), BF16),
    T1=((8, 128), F32),
    TY=((8, 128), F32),
    T2=((8, 128), F32),
    TX=((8, 128), F32),
    T3=((8, 128), F32),
    TZ=((ZS, 8, 128), F32),
    TO=((CS, 8, 128), F32),
)
SEND_RING = 64
SLOTS = dict(
    segc=1, wc=1, u=1, xz=4, xx=4, xc=8, wz=4 * CHUNKS, wx=CHUNKS, wy=CHUNKS, wr=CHUNKS, woc=1,
    gz=8, gy=1, dz=4, dy=1, cotx=1, cotc=2, att=2, n2x=1, n2c=2, mxc=2, mxx=1, e2c=2, e2x=1,
    rdy=4, rdz=4, rdc=1, rgy=4, rgz=4, rgc=1, f4x=1, f4=1, db=1,
    ra1=2 * CHUNKS, ra2=CHUNKS, raz=4 * CHUNKS, rac=CHUNKS, f2=CHUNKS,
    dnc=4, dnx=4, dnz=4, dnt=1, ty=1, tx=1, tz=4, tc=1,
)
RECV_COUNT = sum(SLOTS.values())


def slot_bases():
    bases, used = {}, 0
    for name, count in SLOTS.items():
        bases[name] = used
        used += count
    return SimpleNamespace(**bases)


INPUTS = dict(
    tok=0, cot=0, seg=0, buckets=0, table=0, ga=0, gf=0, wq=0, wk=0, wv=0, wo=0, wg=0, wu=0, wd=0
)
OUTPUTS = dict(
    mixed=((TOK, DIM), BF16), tg=((TOK, DIM), BF16), gga=((1, SHARD), F32),
    gwq=((SHARD, DIM), F32), gwk=((SHARD, DIM), F32), gwv=((SHARD, DIM), F32), gwo=((SHARD, DIM), F32),
    ggf=((1, SHARD), F32), gwg=((SHARD, FF_ALL), F32), gwu=((SHARD, FF_ALL), F32),
    gwd=((DOWN_ROWS, DIM), F32), gtab=((2 * CS * PAIRS, 32), F32),
)


RELAY_TO_Y = (True, True, False, False)
HEAVY_X = (False, False, True, True)
FAR_DIRECT_CHIP = (False, False, False, False)
FAR_DIRECT_TOKEN = False
SPREAD_TOKEN = False
SPREAD_CHIP = (False, False, False, False)
SPREAD_GATE = False
SPREAD_DOWN = False


def layer_kernel(*refs):
    names = (*INPUTS, *OUTPUTS, *SCRATCH)
    r = SimpleNamespace(**dict(zip(names, refs[:-2], strict=True)))
    ssem, rsem = refs[-2:]
    k = slot_bases()
    s, b = lax.axis_index("seq"), lax.axis_index("batch")
    z, x = s // XS, s % XS
    y, c = b // CS, b % CS
    xo, yo, co = 1 - x, 1 - y, 1 - c
    side = z // 2
    m = z + side * (3 - 2 * z)
    at_end, beside = m == 0, m == 1
    zord = [near + side * (3 - 2 * near) for near in (1 - m, 2, 3)]

    def at(zz, xx, yy, cc):
        return (XS * zz + xx, CS * yy + cc)

    to_core, to_x, to_y = at(z, x, y, co), at(z, xo, y, c), at(z, x, yo, c)
    to_z = [at(zz, x, y, c) for zz in zord]

    barrier = pltpu.get_barrier_semaphore()
    friends = [to_core, to_x, to_y] + to_z
    for who in friends:
        pl.semaphore_signal(barrier, inc=1, device_id=who, device_id_type=MESH_IDS)

    sent = []

    def sent_wait(i):
        copy, when = sent[i]
        if when is None:
            copy.wait_send()
        else:
            pl.when(when)(copy.wait_send)

    def put(src, dst, who, slot, when=None):
        if len(sent) >= SEND_RING:
            sent_wait(len(sent) - SEND_RING)
        copy = pltpu.make_async_remote_copy(
            src_ref=src, dst_ref=dst, send_sem=ssem.at[len(sent) % SEND_RING], recv_sem=rsem.at[slot],
            device_id=who, device_id_type=MESH_IDS,
        )
        if when is None:
            copy.start()
        else:
            pl.when(when)(copy.start)
        sent.append((copy, when))

    def take(dst, slot, when=None):
        wait = pltpu.make_async_remote_copy(
            src_ref=dst, dst_ref=dst, send_sem=ssem.at[0], recv_sem=rsem.at[slot],
            device_id=to_core, device_id_type=MESH_IDS,
        ).wait_recv
        if when is None:
            wait()
        else:
            pl.when(when)(wait)

    def z_send(src, dst, slot, direct):
        put(src, dst, to_z[0], slot + z)
        put(src, dst, to_z[1], slot + z)
        put(src, dst, to_z[2], slot + z, when=None if direct else beside)

    def z_take(block, slot, i, direct):
        zz = zord[i]
        take(block(zz), slot + zz)
        if i == 2 and not direct:
            put(block(zz), block(zz), to_z[0], slot + zz, when=beside)

    def z_scatter(part, land, chain, slot, chain_slot, i):
        if i == 2 and chain is None:
            put(part(zord[2]), land.at[z], to_z[2], slot + z)
        elif i == 2:
            put(part(zord[2]), chain, to_z[0], chain_slot, when=at_end)
        else:
            put(part(zord[i]), land.at[z], to_z[i], slot + z)

    def z_chain(part, land, chain, slot, chain_slot):
        @pl.when(beside)
        def _():
            take(chain, chain_slot)
            mine = part(zord[2])
            mine[...] = (mine[...].astype(F32) + chain[...].astype(F32)).astype(BF16)

        put(part(zord[2]), land.at[z], to_z[2], slot + z, when=beside)

    def z_zero(land):
        @pl.when(at_end)
        def _():
            land[zord[2]] = jnp.zeros(land.shape[1:], land.dtype)

    def z_sum(own, land, slot, direct=False):
        take(land.at[zord[0]], slot + zord[0])
        take(land.at[zord[1]], slot + zord[1])
        take(land.at[zord[2]], slot + zord[2], when=None if direct else beside)
        total = own.astype(F32)
        for zz in zord:
            total = total + land[zz].astype(F32)
        return total

    gain_a = to_column(r.ga[...].astype(F32))
    gain_f = to_column(r.gf[...].astype(F32))
    tok = r.tok
    r.SEG[c] = jnp.broadcast_to(r.seg[...].astype(F32), (8, LENGTH))
    for h in range(CS):
        for p in range(PAIRS):
            for j, w_ref in enumerate((r.wq, r.wk, r.wv)):
                lanes = slice(HALF * h + 128 * p, HALF * h + 128 * p + 128)
                r.W_MINE[h, :, HALF * p + 128 * j : HALF * p + 128 * j + 128] = (
                    w_ref[:, lanes].astype(F32) * gain_a
                )
        r.W_MINE[h, :, 3 * HALF : 4 * HALF] = r.wo[:, HALF * h : HALF * h + HALF].astype(F32)
    for j, w_ref in enumerate((r.wg, r.wu)):
        for q, part in enumerate(split_quarters(w_ref[...].astype(F32) * gain_f)):
            first = 4 * HALF + 2 * QUARTER * (q // CS) + QUARTER * j
            r.W_MINE[q % CS, :, first : first + QUARTER] = part

    pl.semaphore_wait(barrier, len(friends))

    put(r.W_MINE.at[co], r.W_CORE.at[c], to_core, k.wc)
    put(tok, r.X.at[c, z, x], to_x, k.xx + z)
    put(r.SEG.at[c], r.SEG.at[c], to_core, k.segc)
    put(tok, r.X.at[c, z, x], to_core, k.xc + s)
    r.X[c, z, x] = tok[...]
    r.WD[z, y] = r.wd[...]
    r.W_CORE[c] = r.W_MINE[c]

    def weight(ch):
        return r.WA.at[ch] if ch < PAIRS else r.WO.at[c]

    def weight_start(ch):
        own = weight(ch).at[z, x, y]
        z_send(own, own, k.wz + 4 * ch, SPREAD_CHIP[ch])
        put(own, own, to_y, k.wy + ch)
        put(own, own, to_x, k.wx + ch)

    def norm_block(q, zz, xx, own=False):
        value = unit_rows(r.X[q, zz, xx].astype(F32))[0].astype(BF16)
        r.N1[q, zz, xx] = value
        if own:
            r.N1O[q] = value

    def token_from_z(i):
        z_take(lambda zz: r.X.at[c, zz, x], k.xz, i, SPREAD_TOKEN)
        zz = zord[i]
        put(r.X.at[c, zz, x], r.X.at[c, zz, x], to_x, k.xx + zz)
        put(r.X.at[c, zz, x], r.X.at[c, zz, x], to_core, k.xc + XS * zz + x)
        norm_block(c, zz, x)

    def token_from_x(zz):
        take(r.X.at[c, zz, xo], k.xx + zz)
        put(r.X.at[c, zz, xo], r.X.at[c, zz, xo], to_core, k.xc + XS * zz + xo)
        norm_block(c, zz, xo)

    def token_from_core(zz, xx):
        take(r.X.at[co, zz, xx], k.xc + XS * zz + xx)
        norm_block(co, zz, xx, own=zz is z and xx is x)

    def bias_lines():
        r.BK[...] = jnp.zeros(r.BK.shape, jnp.int32)
        r.BK[:, : 2 * LENGTH - 1] = r.buckets[...]
        onehot = (
            lax.broadcasted_iota(jnp.int32, (32, SPAN), 0)
            == r.BK[:, pl.ds(pl.multiple_of(LENGTH - TOK - TOK * s, 128), SPAN)]
        )
        r.PH[...] = dot(r.table[...], onehot.astype(BF16))

    def bias_pair(p):
        for hh in range(2):
            line = r.PH[pl.ds(HEADS_HERE * c + 2 * p + hh, 1), :]
            skewed = pltpu.roll(
                jnp.broadcast_to(line, (TOK, SPAN)), SPAN - TOK + 1, 1, stride=1, stride_axis=0
            )
            r.BIAS[p, TOK * hh : TOK * hh + TOK, :] = skewed[:, :LENGTH].astype(BF16)

    def masks():
        take(r.SEG.at[co], k.segc)
        for q in range(CS):
            col = to_column(r.SEG[q, 0:1, pl.ds(pl.multiple_of(TOK * s, 128), TOK)])
            r.MASK[q] = jnp.where(col == r.SEG[q, 0:1, :], 0.0, NEGATIVE).astype(BF16)

    def weight_from_z(ch, i):
        w = weight(ch)
        z_take(lambda zz: w.at[zz, x, y], k.wz + 4 * ch, i, SPREAD_CHIP[ch])
        arrived = w.at[zord[i], x, y]
        put(arrived, arrived, to_y, k.wy + ch)
        put(arrived, arrived, to_x, k.wx + ch)

    def weight_relay(ch):
        w = weight(ch)
        if RELAY_TO_Y[ch]:
            take(w.at[:, xo, y], k.wx + ch)
        else:
            take(w.at[:, x, yo], k.wy + ch)
        if RELAY_TO_Y[ch]:
            put(w.at[:, xo, y], w.at[:, xo, y], to_y, k.wr + ch)
        else:
            put(w.at[:, x, yo], w.at[:, x, yo], to_x, k.wr + ch)

    def weight_end(ch):
        w = weight(ch)
        if RELAY_TO_Y[ch]:
            take(w.at[:, x, yo], k.wy + ch)
        else:
            take(w.at[:, xo, y], k.wx + ch)
        take(w.at[:, xo, yo], k.wr + ch)

    def gate_send(xx):
        own = r.WG.at[z, xx, y]
        z_send(own, own, k.gz + 4 * xx, SPREAD_GATE)
        put(own, own, to_y, k.gy)

    def gate_from_z(xx, i):
        z_take(lambda zz: r.WG.at[zz, xx, y], k.gz + 4 * xx, i, SPREAD_GATE)
        arrived = r.WG.at[zord[i], xx, y]
        put(arrived, arrived, to_y, k.gy)

    def down_from_z(i):
        z_take(lambda zz: r.WD.at[zz, y], k.dz, i, SPREAD_DOWN)
        put(r.WD.at[zord[i], y], r.WD.at[zord[i], y], to_y, k.dy)

    def tokens_send(i):
        far = beside if i == 2 and not SPREAD_TOKEN else None
        put(tok, r.X.at[c, z, x], to_z[i], k.xz + z, when=far)

    def down_send():
        put(r.wd, r.WD.at[z, y], to_y, k.dy)
        z_send(r.wd, r.WD.at[z, y], k.dz, SPREAD_DOWN)

    def shards():
        take(r.W_CORE.at[co], k.wc)
        shard = r.W_CORE[...].reshape(CHIP_ROWS, 4 * HALF + 4 * QUARTER).astype(BF16)
        for ch in range(PAIRS):
            r.WA[ch, z, x, y] = shard[:, HALF * ch : HALF * ch + HALF]
        r.WO[c, z, x, y] = shard[:, 3 * HALF : 4 * HALF]
        for xx in range(XS):
            first = 4 * HALF + 2 * QUARTER * xx
            r.UB[xx] = shard[:, first : first + 2 * QUARTER]
        r.WG[z, x, y] = r.UB[x]

    def gate_exchange():
        put(r.UB.at[xo], r.WG.at[z, x, y], to_x, k.u)

    def gate_other():
        take(r.WG.at[z, xo, y], k.u)
        gate_send(xo)

    def cot_send():
        put(r.cot, r.COT.at[x, c], to_core, k.cotc + 0)
        put(r.cot, r.COT.at[x, c], to_x, k.cotx)
        r.COT[x, c] = r.cot[...]

    def cot_from_x():
        take(r.COT.at[xo, c], k.cotx)
        put(r.COT.at[xo, c], r.COT.at[xo, c], to_core, k.cotc + 1)

    def output_send():
        put(r.WO.at[c], r.WO.at[c], to_core, k.woc)

    zall = [z] + zord

    def keys_values(q, zz):
        rows = r.N1[q, zz].reshape(XS * TOK, DIM)
        for p in range(PAIRS):
            kv = dot(rows, r.WA[p].reshape(DIM, HALF)[:, 128:])
            r.KV[p, q, pl.ds(pl.multiple_of(XS * TOK * zz, 128), XS * TOK), :] = kv.astype(BF16)

    def queries(q):
        for p in range(PAIRS):
            r.QS[p, q] = stack_heads(dot(r.N1O[q], r.WA[p].reshape(DIM, HALF)[:, :128]))

    def attend(p, q):
        kv = r.KV.at[p, q]
        stacked = r.QS[p, q]
        mask = r.MASK[q].astype(F32)
        scores = dot_tb(stacked, kv[:, :128]) + r.BIAS[p].astype(F32) + jnp.concatenate((mask, mask), axis=0)
        weights = jnp.exp(scores - jnp.max(scores, axis=1, keepdims=True))
        probs = (weights * (1.0 / jnp.sum(weights, axis=1, keepdims=True))).astype(BF16)
        r.PS[p, q] = probs
        r.ATT[c, q, :, 128 * p : 128 * p + 128] = unstack_heads(dot(probs, kv[:, 128:])).astype(BF16)

    def attended_send(q):
        put(r.ATT.at[c, q], r.ATT.at[c, q], to_core, k.att + (1 if q is c else 0))

    tokens_send(0)
    norm_block(c, z, x, own=True)
    bias_lines()
    bias_pair(2)
    shards()
    weight_start(PAIRS)
    masks()
    gate_exchange()
    bias_pair(0)
    weight_start(1)
    weight_start(2)
    weight_start(0)
    tokens_send(1)
    token_from_core(z, x)
    tokens_send(2)
    token_from_x(z)
    bias_pair(1)
    token_from_z(0)
    weight_from_z(PAIRS, 0)
    weight_from_z(1, 0)
    weight_from_z(1, 1)
    gate_other()
    down_send()
    weight_from_z(0, 0)
    weight_from_z(2, 1)
    token_from_core(zord[0], x)
    weight_from_z(2, 0)
    weight_from_z(1, 2)
    token_from_core(z, xo)
    gate_send(x)
    weight_from_z(PAIRS, 1)
    weight_from_z(0, 1)
    token_from_x(zord[0])
    token_from_core(zord[0], xo)
    weight_from_z(2, 2)
    weight_relay(1)
    weight_from_z(0, 2)
    weight_from_z(PAIRS, 2)
    token_from_z(1)
    weight_relay(0)
    down_from_z(0)
    weight_relay(2)
    gate_from_z(xo, 0)
    token_from_z(2)
    weight_relay(PAIRS)
    cot_send()
    gate_from_z(x, 0)
    token_from_core(zord[1], x)
    weight_end(1)
    gate_from_z(xo, 1)
    token_from_x(zord[1])
    weight_end(2)
    weight_end(0)
    keys_values(co, zord[0])
    keys_values(co, z)
    queries(0)
    keys_values(c, zord[1])
    keys_values(c, zord[0])
    token_from_core(zord[2], x)
    gate_from_z(xo, 2)
    keys_values(c, z)
    token_from_core(zord[1], xo)
    queries(1)
    down_from_z(1)
    token_from_x(zord[2])
    keys_values(c, zord[2])
    keys_values(co, zord[1])
    attend(2, c)
    gate_from_z(x, 1)
    token_from_core(zord[2], xo)
    keys_values(co, zord[2])
    weight_end(PAIRS)
    attend(0, co)
    down_from_z(2)
    output_send()
    attend(1, co)
    attend(2, co)
    attended_send(co)
    attend(0, c)
    attend(1, c)
    attended_send(c)
    gate_from_z(x, 2)
    cot_from_x()
    take(r.WO.at[co], k.woc)
    take(r.ATT.at[co, c], k.att)

    att_own = jnp.concatenate((r.ATT[0, c], r.ATT[1, c]), axis=1)
    tokens_f = tok[...].astype(F32)
    r.H[...] = tokens_f + jnp.concatenate(
        (dot(att_own, r.WO[0].reshape(DIM, HALF)), dot(att_own, r.WO[1].reshape(DIM, HALF))), axis=1
    )
    r.N2[x, c] = unit_rows(r.H[...])[0].astype(BF16)
    put(r.N2.at[x, c], r.N2.at[x, c], to_core, k.n2c + 0)
    put(r.N2.at[x, c], r.N2.at[x, c], to_x, k.n2x)

    take(r.WG.at[:, :, yo], k.gy)
    take(r.WD.at[:, yo], k.dy)
    take(r.COT.at[x, co], k.cotc + 0)
    take(r.COT.at[xo, co], k.cotc + 1)
    take(r.N2.at[x, co], k.n2c + 0)

    def feed_forward(xx):
        w_gu = r.WG[...].reshape(DIM, 2 * QUARTER)
        w_d = r.WD[...].reshape(QUARTER, DIM)
        n2 = r.N2[xx].reshape(2 * TOK, DIM)
        g = r.COT[xx].reshape(2 * TOK, DIM)
        gate = dot(n2, w_gu[:, :QUARTER])
        up = dot(n2, w_gu[:, QUARTER:])
        d_act = dot_tb(g, w_d)
        square = gate * gate
        inner = math.sqrt(2 / math.pi) * gate * (1.0 + 0.044715 * square)
        tanh = jnp.tanh(inner)
        half_open = 0.5 * (1.0 + tanh)
        gelu = gate * half_open
        slope = half_open + 0.5 * gate * (1.0 - tanh * tanh) * (
            math.sqrt(2 / math.pi) * (1.0 + 3 * 0.044715 * square)
        )
        act = (gelu * up).astype(BF16)
        r.ACT[xx] = act
        d_gu = jnp.concatenate(
            ((slope * (up * d_act)).astype(BF16), (gelu * d_act).astype(BF16)), axis=1
        )
        r.DGU[xx] = d_gu
        r.E2[xx] = dot_tb(d_gu, w_gu).astype(BF16).reshape(CS, TOK, DIM)
        put(r.E2.at[xx, co], r.E2C.at[xx], to_core, k.e2c + xx)
        r.MX[xx] = dot(act, w_d).astype(BF16).reshape(CS, TOK, DIM)
        put(r.MX.at[xx, co], r.MXC.at[xx], to_core, k.mxc + xx)

    feed_forward(x)
    take(r.N2.at[xo, c], k.n2x)
    put(r.N2.at[xo, c], r.N2.at[xo, c], to_core, k.n2c + 1)
    take(r.N2.at[xo, co], k.n2c + 1)
    feed_forward(xo)
    far_first = [zord[2], zord[1], zord[0], z]

    def down_grad(zz):
        return r.GD.at[zz, y]

    def gate_grad(zz):
        return r.GG.at[zz, :, y]

    def grad_from_y(part, got, slot, scatter, i):
        zz = far_first[i]
        take(got.at[zz], slot + zz)
        mine = part(zz)
        mine[...] = (mine[...].astype(F32) + got[zz].astype(F32)).astype(BF16)
        if i < 3:
            z_scatter(part, *scatter, 2 - i)

    down_scatter = (r.GDZ, r.GDC, k.rdz, k.rdc)
    gate_scatter = (r.GGZ, r.GGC, k.rgz, k.rgc)

    def down_from_y(i):
        grad_from_y(down_grad, r.GDY, k.rdy, down_scatter, i)

    def gate_from_y(i):
        grad_from_y(gate_grad, r.GGY, k.rgy, gate_scatter, i)

    def down_chain():
        z_chain(down_grad, *down_scatter)

    def gate_chain():
        z_chain(gate_grad, *gate_scatter)

    def chip_grad(ch, value):
        r.GA[ch] = value.astype(BF16).reshape(ZS, XS, YS, CHIP_ROWS, HALF)
        if HEAVY_X[ch]:
            put(r.GA.at[ch, :, xo, yo], r.GA1.at[ch, :, yo], to_x, k.ra1 + 2 * ch)
            put(r.GA.at[ch, :, xo, y], r.GA1.at[ch, :, y], to_x, k.ra1 + 2 * ch + 1)
        else:
            put(r.GA.at[ch, :, xo, yo], r.GA1.at[ch, :, xo], to_y, k.ra1 + 2 * ch)
            put(r.GA.at[ch, :, x, yo], r.GA1.at[ch, :, x], to_y, k.ra1 + 2 * ch + 1)

    def chip_step1(ch):
        if HEAVY_X[ch]:
            take(r.GA1.at[ch, :, yo], k.ra1 + 2 * ch)
            r.GA[ch, :, x, yo] = (r.GA[ch, :, x, yo].astype(F32) + r.GA1[ch, :, yo].astype(F32)).astype(BF16)
            put(r.GA.at[ch, :, x, yo], r.GA2.at[ch], to_y, k.ra2 + ch)
        else:
            take(r.GA1.at[ch, :, xo], k.ra1 + 2 * ch)
            r.GA[ch, :, xo, y] = (r.GA[ch, :, xo, y].astype(F32) + r.GA1[ch, :, xo].astype(F32)).astype(BF16)
            put(r.GA.at[ch, :, xo, y], r.GA2.at[ch], to_x, k.ra2 + ch)

    def chip_scatter(ch):
        chain = None if FAR_DIRECT_CHIP[ch] else r.GAC.at[ch]
        return (lambda zz: r.GA.at[ch, zz, x, y]), r.GAZ.at[ch], chain, k.raz + 4 * ch, k.rac + ch

    def chip_step2(ch):
        here = y if HEAVY_X[ch] else x
        take(r.GA1.at[ch, :, here], k.ra1 + 2 * ch + 1)
        take(r.GA2.at[ch], k.ra2 + ch)
        r.GA[ch, :, x, y] = (
            r.GA[ch, :, x, y].astype(F32) + r.GA1[ch, :, here].astype(F32) + r.GA2[ch].astype(F32)
        ).astype(BF16)
        for i in (2, 1, 0):
            z_scatter(*chip_scatter(ch), i)

    def chip_chain(ch):
        if not FAR_DIRECT_CHIP[ch]:
            z_chain(*chip_scatter(ch))

    def chip_end(ch):
        total = z_sum(r.GA[ch, z, x, y], r.GAZ.at[ch], k.raz + 4 * ch, FAR_DIRECT_CHIP[ch])
        r.FA[ch] = total.reshape(CS, SHARD, HALF)
        put(r.FA.at[ch, co], r.F2.at[ch, c], to_core, k.f2 + ch)
        r.F2[ch, c] = r.FA[ch, c]

    reverse = (
        lax.broadcasted_iota(jnp.int32, (TOK, TOK), 0) + lax.broadcasted_iota(jnp.int32, (TOK, TOK), 1)
        == TOK - 1
    ).astype(BF16)
    reverse2 = jnp.concatenate((reverse, reverse), axis=1)

    def attend_back(p, q):
        d_out = stack_heads(r.DO[q, :, 128 * p : 128 * p + 128].astype(F32))
        kv = r.KV.at[p, q]
        probs = r.PS[p, q]
        weighted = probs.astype(F32) * dot_tb(d_out, kv[:, 128:])
        delta = jnp.sum(weighted, axis=1, keepdims=True)
        d_scores = (weighted - probs.astype(F32) * delta).astype(BF16)
        r.DQ[p, q] = unstack_heads(dot(d_scores, kv[:, :128])).astype(BF16)
        r.DKV[p, q, :128] = dot_ta(r.QS[p, q], d_scores).astype(BF16)
        r.DKV[p, q, 128:] = dot_ta(d_out, probs).astype(BF16)
        r.PS[p, q] = d_scores

    def grads_pair(p):
        kv_grad = dot(r.DKV[p, 0], r.N1[0].reshape(LENGTH, DIM)) + dot(
            r.DKV[p, 1], r.N1[1].reshape(LENGTH, DIM)
        )
        own_rows = r.N1O[...].reshape(CS * TOK, DIM)
        q_grad = dot_ta(r.DQ[p].reshape(CS * TOK, 128), own_rows)
        chip_grad(p, jnp.concatenate((q_grad, kv_grad), axis=0).astype(BF16).T)

    def grads_bias(p):
        for hh in range(2):
            both = r.PS[p, :, TOK * hh : TOK * hh + TOK, :].reshape(CS * TOK, LENGTH)
            padded = jnp.concatenate((dot(reverse2, both), jnp.zeros((TOK, TOK), F32)), axis=1)
            placed = pltpu.roll(padded, 0, 1, stride=1, stride_axis=0)
            r.DG[2 * p + hh : 2 * p + hh + 1, :] = jnp.sum(placed, axis=0, keepdims=True)

    w_kv = jnp.concatenate([r.WA[p].reshape(DIM, HALF)[:, 128:] for p in range(PAIRS)], axis=1)

    def token_grad(q, zz):
        lanes = pl.ds(pl.multiple_of(XS * TOK * zz, 128), XS * TOK)
        d_kv = r.DKV[:, q, :, lanes].reshape(PAIRS * 256, XS * TOK)
        out = dot(w_kv, d_kv)
        for xx in range(XS):
            r.DN[q, zz, xx] = out[:, TOK * xx : TOK * xx + TOK].astype(BF16)
        if zz is z:
            total = r.DN[q, z, x].astype(F32)
            for p in range(PAIRS):
                total = total + dot_tb(r.WA[p].reshape(DIM, HALF)[:, :128], r.DQ[p, q])
            r.DN[q, z, x] = total.astype(BF16)

    def token_exchange(zz):
        token_grad(co, zz)
        put(r.DN.at[co, zz], r.DNC.at[zz], to_core, k.dnc + zz)
        token_grad(c, zz)

    def token_to_x(zz):
        take(r.DNC.at[zz], k.dnc + zz)
        r.DN[c, zz] = (r.DN[c, zz].astype(F32) + r.DNC[zz].astype(F32)).astype(BF16)
        put(r.DN.at[c, zz, xo], r.DNX.at[zz], to_x, k.dnx + zz)

    def token_part(zz):
        return r.DN.at[c, zz, x]

    token_scatter = (r.DNZ, None if FAR_DIRECT_TOKEN else r.DNT, k.dnz, k.dnt)

    def token_chain():
        if not FAR_DIRECT_TOKEN:
            z_chain(token_part, *token_scatter)

    def token_to_z(i):
        zz = far_first[i]
        take(r.DNX.at[zz], k.dnx + zz)
        r.DN[c, zz, x] = (r.DN[c, zz, x].astype(F32) + r.DNX[zz].astype(F32)).astype(BF16)
        if i < 3:
            z_scatter(token_part, *token_scatter, 2 - i)

    def grads_down():
        cot_all = r.COT[...].reshape(4 * TOK, DIM)
        r.GD[...] = dot_ta(r.ACT[...].reshape(4 * TOK, QUARTER), cot_all).astype(BF16).reshape(
            ZS, YS, DOWN_ROWS, DIM
        )
        for zz in far_first:
            put(r.GD.at[zz, yo], r.GDY.at[zz], to_y, k.rdy + zz)

    def grads_gate():
        n2_all = r.N2[...].reshape(4 * TOK, DIM)
        d_gu_all = r.DGU[...].reshape(4 * TOK, 2 * QUARTER)
        r.GG[...] = dot_ta(n2_all, d_gu_all).astype(BF16).reshape(ZS, XS, YS, CHIP_ROWS, 2 * QUARTER)
        for zz in far_first:
            put(r.GG.at[zz, :, yo], r.GGY.at[zz], to_y, k.rgy + zz)

    def zeros():
        z_zero(r.GDZ)
        z_zero(r.GGZ)
        if not FAR_DIRECT_TOKEN:
            z_zero(r.DNZ)
        for ch in range(CHUNKS):
            if not FAR_DIRECT_CHIP[ch]:
                z_zero(r.GAZ.at[ch])

    def hidden_send():
        take(r.E2C.at[xo], k.e2c + xo)
        r.E2S[...] = (r.E2[xo, c].astype(F32) + r.E2C[xo].astype(F32)).astype(BF16)
        put(r.E2S, r.E2X, to_x, k.e2x)

    def hidden_back():
        take(r.E2C.at[x], k.e2c + x)
        take(r.E2X, k.e2x)
        e2 = r.E2[x, c].astype(F32) + r.E2C[x].astype(F32) + r.E2X[...].astype(F32)
        n2_own, r2 = unit_rows(r.H[...])
        r.DH[...] = r.cot[...].astype(F32) + r2 * (
            e2 - n2_own * jnp.mean(e2 * n2_own, axis=1, keepdims=True)
        )
        r.DB[c] = r.DH[...].astype(BF16)
        put(r.DB.at[c], r.DB.at[c], to_core, k.db)

    def mixed_send():
        take(r.MXC.at[xo], k.mxc + xo)
        r.MXS[...] = (r.MX[xo, c].astype(F32) + r.MXC[xo].astype(F32)).astype(BF16)
        put(r.MXS, r.MXX, to_x, k.mxx)

    def mixed_end():
        take(r.MXC.at[x], k.mxc + x)
        take(r.MXX, k.mxx)
        r.mixed[...] = (
            r.H[...] + r.MX[x, c].astype(F32) + r.MXC[x].astype(F32) + r.MXX[...].astype(F32)
        ).astype(BF16)

    def attended_back(q):
        if q is co:
            take(r.DB.at[co], k.db)
        rows = [r.WO[h, pl.ds(2 * c, 2)].reshape(HALF, HALF) for h in range(CS)]
        d_att = dot_tb(r.DB[q, :, :HALF], rows[0]) + dot_tb(r.DB[q, :, HALF:], rows[1])
        r.DO[q] = d_att.astype(BF16)

    def grads_output():
        take(r.ATT.at[co, co], k.att + 1)
        att_all = jnp.concatenate(
            [jnp.concatenate((r.ATT[0, q], r.ATT[1, q]), axis=1) for q in range(CS)], axis=0
        )
        db_cols = r.DB[:, :, pl.ds(pl.multiple_of(HALF * c, 128), HALF)].reshape(CS * TOK, HALF)
        chip_grad(PAIRS, dot_ta(att_all, db_cols))

    def table_start():
        r.DG[HEADS_HERE:, :] = jnp.zeros((8 - HEADS_HERE, SPAN), F32)
        onehot_back = (
            lax.broadcasted_iota(jnp.int32, (128, SPAN), 0)
            == r.BK[:, pl.ds(pl.multiple_of(LENGTH - TOK - TOK * s, 128), SPAN)]
        ).astype(F32)
        r.T1[...] = lax.dot_general(
            r.DG[...], onehot_back, (((1,), (1,)), ((), ())), precision=HIGHEST, preferred_element_type=F32
        )
        put(r.T1, r.TY, to_y, k.ty)

    def table_to_x():
        take(r.TY, k.ty)
        r.T2[...] = r.T1[...] + r.TY[...]
        put(r.T2, r.TX, to_x, k.tx)

    def table_to_z():
        take(r.TX, k.tx)
        r.T3[...] = r.T2[...] + r.TX[...]
        for who in to_z:
            put(r.T3, r.TZ.at[z], who, k.tz + z)
        r.TZ[z] = r.T3[...]

    def table_to_core():
        for zz in zord:
            take(r.TZ.at[zz], k.tz + zz)
        r.TO[c] = (r.TZ[0] + r.TZ[1]) + (r.TZ[2] + r.TZ[3])
        put(r.TO.at[c], r.TO.at[c], to_core, k.tc)

    def table_end():
        take(r.TO.at[co], k.tc)
        for q in range(CS):
            r.gtab[HEADS_HERE * q : HEADS_HERE * q + HEADS_HERE, :] = r.TO[q, :HEADS_HERE, :32]

    def down_end():
        r.gwd[...] = z_sum(r.GD[z, y], r.GDZ, k.rdz)

    def gate_to_x():
        total = z_sum(r.GG[z, :, y], r.GGZ, k.rgz)
        r.F4S[...] = total.astype(BF16)
        put(r.F4S.at[xo], r.F4X, to_x, k.f4x)

    def gate_to_core():
        take(r.F4X, k.f4x)
        r.F4S2[:, x] = r.F4S[x].astype(F32).reshape(CS, SHARD, 2 * QUARTER)
        r.F4S2[:, xo] = r.F4X[...].astype(F32).reshape(CS, SHARD, 2 * QUARTER)
        put(r.F4S2.at[co], r.F4.at[c], to_core, k.f4)
        r.F4[c] = r.F4S2[c]

    def gate_end():
        take(r.F4.at[co], k.f4)
        quarters = [r.F4[q % CS, q // CS] for q in range(BATCH_DEVICES)]
        gate_total = join_quarters([quarter[:, :QUARTER] for quarter in quarters])
        up_total = join_quarters([quarter[:, QUARTER:] for quarter in quarters])
        r.gwg[...] = gate_total * gain_f
        r.gwu[...] = up_total * gain_f
        r.ggf[...] = to_row(
            jnp.sum(
                gate_total * r.wg[...].astype(F32) + up_total * r.wu[...].astype(F32), axis=1, keepdims=True
            )
        )

    def token_end():
        e1 = z_sum(r.DN[c, z, x], r.DNZ, k.dnz, FAR_DIRECT_TOKEN).T
        n1_own, r1 = unit_rows(tok[...].astype(F32))
        r.tg[...] = (
            r.DH[...] + r1 * (e1 - n1_own * jnp.mean(e1 * n1_own, axis=1, keepdims=True))
        ).astype(BF16)

    def chip_out(ch):
        take(r.F2.at[ch, co], k.f2 + ch)
        if ch == PAIRS:
            for h in range(CS):
                r.gwo[:, HALF * h : HALF * h + HALF] = r.F2[ch, h]
            return
        gain_part = jnp.zeros((SHARD, 128), F32)
        for j, (w_ref, out_ref) in enumerate(((r.wq, r.gwq), (r.wk, r.gwk), (r.wv, r.gwv))):
            for h in range(CS):
                lanes = slice(HALF * h + 128 * ch, HALF * h + 128 * ch + 128)
                grad = r.F2[ch, h, :, 128 * j : 128 * j + 128]
                gain_part = gain_part + grad * w_ref[:, lanes].astype(F32)
                out_ref[:, lanes] = grad * gain_a
        r.GT[ch] = gain_part

    def gain_end():
        r.gga[...] = to_row(jnp.sum(r.GT[0] + r.GT[1] + r.GT[2], axis=1, keepdims=True))

    zeros()
    grads_down()
    hidden_send()
    down_from_y(0)
    mixed_send()
    grads_gate()
    hidden_back()
    down_from_y(1)
    attended_back(c)
    attend_back(2, c)
    down_from_y(2)
    attended_back(co)
    down_chain()
    grads_output()
    attend_back(0, c)
    attend_back(1, co)
    attend_back(2, co)
    down_from_y(3)
    grads_bias(2)
    grads_pair(2)
    gate_from_y(0)
    attend_back(0, co)
    down_end()
    chip_step1(PAIRS)
    attend_back(1, c)
    token_exchange(far_first[1])
    mixed_end()
    grads_bias(1)
    gate_from_y(1)
    grads_bias(0)
    token_exchange(far_first[2])
    gate_chain()
    token_to_x(far_first[1])
    table_start()
    token_exchange(far_first[0])
    chip_step1(2)
    gate_from_y(2)
    grads_pair(0)
    grads_pair(1)
    token_to_x(far_first[0])
    token_to_x(far_first[2])
    token_exchange(far_first[3])
    token_to_z(1)
    gate_from_y(3)
    table_to_x()
    chip_step2(PAIRS)
    token_to_x(far_first[3])
    chip_chain(PAIRS)
    token_to_z(0)
    table_to_z()
    token_to_z(2)
    chip_step1(0)
    chip_step1(1)
    gate_to_x()
    token_to_z(3)
    chip_step2(2)
    token_chain()
    chip_end(PAIRS)
    chip_step2(0)
    chip_chain(2)
    table_to_core()
    chip_out(PAIRS)
    chip_step2(1)
    chip_end(2)
    gate_to_core()
    chip_chain(0)
    chip_out(2)
    table_end()
    chip_chain(1)
    token_end()
    gate_end()
    chip_end(0)
    chip_end(1)
    chip_out(0)
    chip_out(1)
    gain_end()
    for i in range(len(sent) - SEND_RING, len(sent)):
        sent_wait(i)


def finish_kernel(*refs):
    count = len(refs) // 2
    for src, dst in zip(refs[:count], refs[count:]):
        dst[...] = src[...]


def fused_device(
    tokens, segments, buckets, gain_attn, w_query, w_key, w_value, w_output,
    gain_ffn, w_gate, w_up, w_down, bucket_bias_matrix, cotangent,
):
    operands = (
        tokens.reshape(TOK, DIM),
        cotangent.reshape(TOK, DIM),
        segments.reshape(1, LENGTH),
        buckets.reshape(1, 2 * LENGTH - 1),
        bucket_bias_matrix.T,
        gain_attn.reshape(1, SHARD),
        gain_ffn.reshape(1, SHARD),
        w_query, w_key, w_value, w_output, w_gate, w_up, w_down,
    )
    out_shape = [jax.ShapeDtypeStruct(shape, dtype) for shape, dtype in OUTPUTS.values()]
    in_vmem = pl.BlockSpec(memory_space=pltpu.VMEM)
    outs = pl.pallas_call(
        layer_kernel,
        out_shape=out_shape,
        in_specs=[in_vmem] * len(operands),
        out_specs=[in_vmem] * len(out_shape),
        scratch_shapes=[pltpu.VMEM(shape, dtype) for shape, dtype in SCRATCH.values()]
        + [pltpu.SemaphoreType.DMA((SEND_RING,)), pltpu.SemaphoreType.DMA((RECV_COUNT,))],
        compiler_params=pltpu.CompilerParams(
            collective_id=0, has_side_effects=True, vmem_limit_bytes=63 * 2**20
        ),
        name="layer",
    )(*operands)
    outs = pl.pallas_call(
        finish_kernel,
        out_shape=out_shape,
        in_specs=[in_vmem] * len(out_shape),
        out_specs=[in_vmem] * len(out_shape),
        name="finish",
    )(*outs)
    mixed, tokens_grad, gga, gwq, gwk, gwv, gwo, ggf, gwg, gwu, gwd, table_grad = outs
    return (
        mixed.reshape(tokens.shape), tokens_grad.reshape(tokens.shape), gga.reshape(SHARD),
        gwq, gwk, gwv, gwo, ggf.reshape(SHARD), gwg, gwu, gwd, table_grad.T,
    )


def fits_fused(mesh):
    return mesh.shape["seq"] == SEQ_DEVICES and mesh.shape["batch"] == BATCH_DEVICES


def solution(mesh):
    return jax.shard_map(
        fused_device if fits_fused(mesh) else on_device,
        mesh=mesh,
        in_specs=(
            P("seq", "batch", None),
            P(None, "batch"),
            P(),
            P(("seq", "batch")),
            P(("seq", "batch"), None),
            P(("seq", "batch"), None),
            P(("seq", "batch"), None),
            P(("seq", "batch"), None),
            P(("seq", "batch")),
            P(("seq", "batch"), None),
            P(("seq", "batch"), None),
            P(("seq", "batch"), None),
            P(),
            P("seq", "batch", None),
        ),
        out_specs=(
            P("seq", "batch", None),
            P("seq", "batch", None),
            P(("seq", "batch")),
            P(("seq", "batch"), None),
            P(("seq", "batch"), None),
            P(("seq", "batch"), None),
            P(("seq", "batch"), None),
            P(("seq", "batch")),
            P(("seq", "batch"), None),
            P(("seq", "batch"), None),
            P(("seq", "batch"), None),
            P(),
        ),
        check_vma=False,
    )
```
